512 devices in a mesh: cp: 8 (over y_hi, core), blk: 8 (over x, y_lo), head: 8 (over z).
Axes of the slice: x: 4, y: 8 (y_hi: 4, y_lo: 2; y = y_hi * 2 + y_lo), z: 8, core: 2. Of those that a mesh axis runs over, the one named last changes fastest.
Arguments:
- queries: bfloat16 [8192, 8, 1024], P(('cp', 'blk'), 'head'), may hold values from -4 to 4
- new_kv: bfloat16 [8192, 8, 2, 128], P(('cp', 'blk'), 'head'), may hold values from -105 to 105
- cached_key_value: bfloat16 [4096, 8, 2, 128], P(('cp', 'blk'), 'head'), may hold values from -4 to 4
- new_doc: int32 [8192], replicated, may hold values from 0 to 15, never falling along the last dimension, each value on 1 to 1024 neighbouring positions
- cache_doc: int32 [4096], replicated, may hold values from 0 to 15, never falling along the last dimension, each value on 1 to 512 neighbouring positions
- cache_len: int32 [64], replicated, may hold values from 16 to 64, as said below
Outputs:
- attended: bfloat16 [8192, 8, 1024], P(('cp', 'blk', 'head'))
The draws below stay inside these ranges and needn't reach their ends.
Inputs may be any that keep to these rules, and one draw needn't show every extreme that they name: `new_doc`: request numbers never fall along the new positions, and each of the 16 requests has at least one new position. `cache_doc`: request numbers never fall along the cached positions, and each of the 16 requests has at least one cached position. `cache_len`: shard s holds cached positions s * 64 to (s + 1) * 64 - 1, the valid ones first; some shard is full.
All inputs are finite; a program needn't handle non-finite values.
Results may differ from the reference program's by a relative error of at most 0.0065.
Values may be sent and summed in bfloat16 or wider, within the bound.
No kernel may reach another device: no remote copies, remote signals or barrier semaphores. Data moves between devices by JAX's collectives and lax.ppermute only.
A program may use at most 64 MiB of HBM per device.

```python
import math
import jax
import jax.numpy as jnp
import numpy as np
from jax import lax

HEAD_SIZE = 128
QUERY_HEAD_GROUP = 8
CACHE_DEV = 64
NDOC = 16
KEY_VALUE_HEADS = 8
SHARDS = 64
FRESH_TOKEN_ROWS = 8192
CACHED_TOKENS = 4096


def shared_queries(key):
    return jnp.clip(jax.random.normal(key, (FRESH_TOKEN_ROWS, KEY_VALUE_HEADS, QUERY_HEAD_GROUP * HEAD_SIZE), jnp.float32), -4.0, 4.0)


def draw_queries(key, part):
    shared = shared_queries(key)
    return shared.astype(jnp.bfloat16)


def draw_new_kv(key, part):
    key = jax.random.fold_in(key, 12)
    sampled_key_value = jnp.clip(jax.random.normal(key, (FRESH_TOKEN_ROWS, KEY_VALUE_HEADS, 2, HEAD_SIZE), jnp.float32), -4.0, 4.0)
    return sampled_key_value.astype(jnp.bfloat16)


def draw_cache_len(key, part):
    key = jax.random.fold_in(key, 13)
    lengths = jax.random.randint(key, (SHARDS,), CACHE_DEV // 4, CACHE_DEV + 1)
    fullest = jax.random.randint(jax.random.fold_in(key, 1), (), 0, SHARDS)
    return jnp.where(jnp.arange(SHARDS) == fullest, CACHE_DEV, lengths).astype(jnp.int32)


def steps_of(stream_key, extent, pieces, low, high):
    gain = 1.0
    for axis_at, parts in pieces:
        draws = jax.random.uniform(jax.random.fold_in(jax.random.fold_in(stream_key, 6), axis_at), (parts,), jnp.float32, low / len(pieces), high / len(pieces))
        gain = gain * jnp.repeat(jnp.exp(draws), extent[axis_at] // parts).reshape((-1,) + (1,) * (len(extent) - 1 - axis_at))
    return gain


def length_profile(number_of, total, bound, slope):
    portions = [(1 << 20) // math.isqrt(standing ** slope) + 1 for standing in range(2, number_of + 1)]
    surplus, counts = total - bound - (number_of - 1), [1] * (number_of - 1)
    while surplus > 0:
        candidates = [i for i in range(number_of - 1) if counts[i] < bound]
        whole, budget = sum([portions[i] for i in candidates]), surplus
        for i in candidates:
            addition = min(bound - counts[i], max(1, budget * portions[i] // whole), surplus)
            counts[i] = counts[i] + addition
            surplus = surplus - addition
    return np.array([bound] + counts)


def uneven(stream_key, count, total, limit, lean):
    if count == 2:
        one = jax.random.randint(stream_key, (), max(1, total - limit), min(limit, total - 1) + 1)
        return jnp.stack([one, total - one])
    sizes = jnp.asarray(length_profile(count, total, limit, lean), jnp.int32)
    pairs = (count - 1) // 2
    giver, sink = sizes[1:1 + 2 * pairs:2], sizes[2:2 + 2 * pairs:2]
    room = jnp.minimum(giver - 1, limit - sink)
    passed = jax.random.randint(jax.random.fold_in(stream_key, 1), (pairs,), 0, 1 << 20) % (room + 1)
    sizes = sizes.at[1:1 + 2 * pairs:2].set(giver - passed).at[2:2 + 2 * pairs:2].set(sink + passed)
    return sizes[jax.random.permutation(jax.random.fold_in(stream_key, 2), count)]


def gaussian(rng, dims, scale, most, shards=(), kind=jnp.bfloat16):
    gain = steps_of(rng, dims, shards, -0.22, 0.18) if shards else 1.0
    entries = jax.random.normal(rng, dims, jnp.float32) * scale * gain
    return jnp.minimum(jnp.maximum(entries, -most), most).astype(kind)


def setup_inputs(seed: int = 0) -> dict:
    keys = jax.random.split(jax.random.key(seed), 7)
    queries = draw_queries(jax.random.fold_in(keys[6], 71), 0)
    new_kv = draw_new_kv(jax.random.fold_in(keys[6], 71), 0)
    cached_key_value = gaussian(keys[2], (CACHED_TOKENS, KEY_VALUE_HEADS, 2, HEAD_SIZE), 1.0, 4.0, ((0, 64), (1, 8)))
    new_doc = jnp.searchsorted(jnp.cumsum(uneven(keys[3], NDOC, FRESH_TOKEN_ROWS, 2 * FRESH_TOKEN_ROWS // NDOC, 1)), jnp.arange(FRESH_TOKEN_ROWS), side="right").astype(jnp.int32)
    cache_doc = jnp.searchsorted(jnp.cumsum(uneven(keys[4], NDOC, CACHED_TOKENS, 2 * CACHED_TOKENS // NDOC, 1)), jnp.arange(CACHED_TOKENS), side="right").astype(jnp.int32)
    cache_len = draw_cache_len(jax.random.fold_in(keys[6], 71), 0)
    return {"queries": queries, "new_kv": new_kv, "cached_key_value": cached_key_value, "new_doc": new_doc, "cache_doc": cache_doc, "cache_len": cache_len}


def reference(queries, new_kv, cached_key_value, new_doc, cache_doc, cache_len):
    new_count = new_doc.shape[0]
    cache_count = cache_doc.shape[0]
    head_width = new_kv.shape[-1]
    kv_heads = new_kv.shape[1]
    query_heads = queries.shape[-1] // head_width
    cache_slot = jnp.arange(cache_count, dtype=jnp.int32)
    usable = cache_slot % CACHE_DEV < cache_len[cache_slot // CACHE_DEV]
    key_doc = jnp.concatenate([jnp.where(usable, cache_doc, -1).astype(jnp.int32), new_doc.astype(jnp.int32)])
    key_place = jnp.concatenate([jnp.full((cache_count,), -1, jnp.int32), jnp.arange(new_count, dtype=jnp.int32)])
    all_kv = jnp.concatenate([cached_key_value, new_kv], axis=0)
    block_rows = math.gcd(new_count, 512)
    score_scale = head_width ** -0.5

    def per_head(head_number):
        head_kv = lax.dynamic_index_in_dim(all_kv, head_number, 1, keepdims=False).astype(jnp.float32)
        head_queries = lax.dynamic_index_in_dim(queries, head_number, 1, keepdims=False)

        def per_block(first_row):
            block_queries = lax.dynamic_slice_in_dim(head_queries, first_row, block_rows, 0)
            block_queries = block_queries.astype(jnp.float32).reshape(block_rows, query_heads, head_width)
            block_doc = lax.dynamic_slice_in_dim(new_doc, first_row, block_rows, 0)
            block_place = first_row + jnp.arange(block_rows, dtype=jnp.int32)
            allowed = (block_doc[:, None] == key_doc[None, :]) & (key_place[None, :] <= block_place[:, None])
            scores = jnp.einsum("thd,nd->thn", block_queries, head_kv[:, 0, :]) * score_scale
            scores = jnp.where(allowed[:, None, :], scores, -1.0e30)
            row_max = jnp.max(scores, axis=2, keepdims=True)
            weights = jnp.where(allowed[:, None, :], jnp.exp(scores - row_max), 0.0)
            row_total = jnp.sum(weights, axis=2)
            rounded = lax.optimization_barrier(weights.astype(jnp.bfloat16)).astype(jnp.float32)
            summed = jnp.einsum("thn,nd->thd", rounded, head_kv[:, 1, :])
            result = (summed / row_total[:, :, None]).astype(jnp.bfloat16)
            return result.reshape(block_rows, query_heads * head_width)

        first_rows = jnp.arange(0, new_count, block_rows, dtype=jnp.int32)
        return lax.map(per_block, first_rows).reshape(new_count, query_heads * head_width)

    outputs = lax.map(per_head, jnp.arange(kv_heads, dtype=jnp.int32))
    return jnp.transpose(outputs, (1, 0, 2))
```

```python
import functools
import math

import jax
import jax.numpy as jnp
from jax import lax
from jax.experimental import pallas as pl
from jax.experimental.pallas import tpu as pltpu
from jax.sharding import PartitionSpec as P

negative = -1e30
cache_tile = 256
documents = 16


def attention_kernel(
    place_ref,
    new_starts_ref,
    cache_starts_ref,
    cache_len_ref,
    queries_ref,
    window_ref,
    cache_ref,
    out_ref,
    new_scores,
    cache_scores,
    lane_max,
    lane_sum,
    total,
    *,
    blk_count,
    shard_rows,
):
    tok, width = queries_ref.shape
    head = 128
    heads = width // head
    exponent_scale = math.log2(math.e) * head**-0.5
    cp_index = place_ref[0]
    blk_index = place_ref[1]
    block = cp_index * blk_count + blk_index
    first = block * tok

    row_place = first + lax.broadcasted_iota(jnp.int32, (tok, 1), 0)
    row_start = jnp.zeros((tok, 1), jnp.int32)
    row_low = jnp.zeros((tok, 1), jnp.int32)
    row_high = jnp.full((tok, 1), cache_starts_ref[1], jnp.int32)
    new_low = jnp.int32(0)
    cache_low = jnp.int32(0)
    cache_high = cache_starts_ref[1]
    for doc in range(1, documents):
        start = new_starts_ref[doc]
        low = cache_starts_ref[doc]
        high = cache_starts_ref[doc + 1]
        reached = row_place >= start
        row_start = jnp.where(reached, start, row_start)
        row_low = jnp.where(reached, low, row_low)
        row_high = jnp.where(reached, high, row_high)
        new_low = jnp.where(first >= start, start, new_low)
        cache_low = jnp.where(first >= start, low, cache_low)
        cache_high = jnp.where(first + tok - 1 >= start, high, cache_high)

    lane_max[...] = jnp.full(lane_max.shape, negative, jnp.float32)
    lane_sum[...] = jnp.zeros(lane_sum.shape, jnp.float32)
    total[...] = jnp.zeros(total.shape, jnp.float32)

    def window_place(number):
        group = number // blk_count
        return number % blk_count, (group - cp_index + 1) * tok

    def score(keys, allowed, store):
        for h in range(heads):
            scores = lax.dot_general(
                queries_ref[:, h * head : (h + 1) * head],
                keys,
                (((1,), (1,)), ((), ())),
                preferred_element_type=jnp.float32,
            )
            scores = jnp.where(allowed, scores, negative)
            store(h, scores)
            best = scores[:, :head]
            for part in range(1, scores.shape[1] // head):
                best = jnp.maximum(best, scores[:, part * head : (part + 1) * head])
            lane_max[h] = jnp.maximum(lane_max[h], best)

    first_block = new_low // tok

    @pl.loop(first_block, block + 1)
    def _(number):
        slot, offset = window_place(number)
        keys = window_ref[slot, pl.ds(pl.multiple_of(offset, tok), tok), :head]
        key_place = number * tok + lax.broadcasted_iota(jnp.int32, (1, tok), 1)
        allowed = (key_place >= row_start) & (key_place <= row_place)

        def store(h, scores):
            new_scores[number - first_block, h] = scores

        score(keys, allowed, store)

    first_tile = cache_low // cache_tile
    end_tile = (cache_high + cache_tile - 1) // cache_tile

    @pl.loop(first_tile, end_tile)
    def _(number):
        offset = pl.multiple_of(number * cache_tile, cache_tile)
        keys = cache_ref[pl.ds(offset, cache_tile), :head]
        lane = lax.broadcasted_iota(jnp.int32, (1, cache_tile), 1)
        filled = jnp.zeros((1, cache_tile), jnp.int32)
        for part in range(cache_tile // shard_rows):
            shard = number * (cache_tile // shard_rows) + part
            filled = jnp.where(
                lane >= part * shard_rows, part * shard_rows + cache_len_ref[shard], filled
            )
        key_place = offset + lane
        usable = lane < filled
        allowed = (key_place >= row_low) & (key_place < row_high) & usable

        def store(h, scores):
            cache_scores[number, h] = scores

        score(keys, allowed, store)

    for h in range(heads):
        best = jnp.max(lane_max[h], axis=1, keepdims=True)
        lane_max[h] = jnp.broadcast_to(best, (tok, head))

    def gather(values, load):
        for h in range(heads):
            scores = load(h)
            best = lane_max[h]
            parts = []
            added = lane_sum[h]
            for part in range(scores.shape[1] // head):
                piece = scores[:, part * head : (part + 1) * head]
                weight = jnp.exp2((piece - best) * exponent_scale)
                added = added + weight
                parts.append(weight.astype(jnp.bfloat16))
            lane_sum[h] = added
            rounded = parts[0] if len(parts) == 1 else jnp.concatenate(parts, axis=1)
            total[h] += jnp.dot(rounded, values, preferred_element_type=jnp.float32)

    @pl.loop(first_block, block + 1)
    def _(number):
        slot, offset = window_place(number)
        values = window_ref[slot, pl.ds(pl.multiple_of(offset, tok), tok), head:]
        gather(values, lambda h: new_scores[number - first_block, h])

    @pl.loop(first_tile, end_tile)
    def _(number):
        offset = pl.multiple_of(number * cache_tile, cache_tile)
        values = cache_ref[pl.ds(offset, cache_tile), head:]
        gather(values, lambda h: cache_scores[number, h])

    for h in range(heads):
        row_total = jnp.sum(lane_sum[h], axis=1, keepdims=True)
        out_ref[:, h * head : (h + 1) * head] = (total[h] / row_total).astype(jnp.bfloat16)


def local(queries, new_kv, cached_key_value, new_doc, cache_doc, cache_len):
    tok = queries.shape[0]
    width = queries.shape[-1]
    head = new_kv.shape[-1]
    heads = width // head
    shard_rows = cached_key_value.shape[0]
    blk_count = lax.axis_size("blk")
    cp_count = lax.axis_size("cp")
    head_count = lax.axis_size("head")
    place = jnp.stack([lax.axis_index("cp"), lax.axis_index("blk")]).astype(jnp.int32)
    own_new = new_kv.reshape(tok, 2 * head)
    own_cache = cached_key_value.reshape(shard_rows, 2 * head)
    cache = lax.all_gather(own_cache, ("cp", "blk"), axis=0, tiled=True)
    behind = lax.ppermute(own_new, "cp", [(i, (i + 1) % cp_count) for i in range(cp_count)])
    window = lax.all_gather(jnp.concatenate([behind, own_new], axis=0), "blk", axis=0)
    marks = jnp.arange(documents + 1, dtype=jnp.int32)
    new_starts = jnp.sum((new_doc[None, :] < marks[:, None]).astype(jnp.int32), axis=1)
    cache_starts = jnp.sum((cache_doc[None, :] < marks[:, None]).astype(jnp.int32), axis=1)
    smem = pl.BlockSpec(memory_space=pltpu.SMEM)
    vmem = pl.BlockSpec(memory_space=pltpu.VMEM)
    reach = 1024 // tok + 1
    tiles = cache.shape[0] // cache_tile
    attended = pl.pallas_call(
        functools.partial(attention_kernel, blk_count=blk_count, shard_rows=shard_rows),
        out_shape=jax.ShapeDtypeStruct((tok, width), jnp.bfloat16),
        in_specs=[smem, smem, smem, smem, vmem, vmem, vmem],
        out_specs=vmem,
        scratch_shapes=[
            pltpu.VMEM((reach, heads, tok, tok), jnp.float32),
            pltpu.VMEM((tiles, heads, tok, cache_tile), jnp.float32),
            pltpu.VMEM((heads, tok, head), jnp.float32),
            pltpu.VMEM((heads, tok, head), jnp.float32),
            pltpu.VMEM((heads, tok, head), jnp.float32),
        ],
        compiler_params=pltpu.CompilerParams(vmem_limit_bytes=44 * 1024 * 1024),
    )(place, new_starts, cache_starts, cache_len, queries[:, 0], window, cache)
    share = tok // head_count
    moved = lax.all_to_all(
        attended.reshape(head_count, share, width), "head", split_axis=0, concat_axis=0
    )
    return jnp.transpose(moved, (1, 0, 2))


def solution(mesh):
    placed = (
        P(("cp", "blk"), "head", None),
        P(("cp", "blk"), "head", None, None),
        P(("cp", "blk"), "head", None, None),
        P(),
        P(),
        P(),
    )
    return jax.shard_map(
        local,
        mesh=mesh,
        in_specs=placed,
        out_specs=P(("cp", "blk", "head"), None, None),
        check_vma=False,
    )
```

```python
import functools
import math

import jax
import jax.numpy as jnp
from jax import lax
from jax.experimental import pallas as pl
from jax.experimental.pallas import tpu as pltpu
from jax.sharding import PartitionSpec as P

negative = -1e30
documents = 16
longest = 1024
head = 128
pieces = 4
smem = pl.BlockSpec(memory_space=pltpu.SMEM)
vmem = pl.BlockSpec(memory_space=pltpu.VMEM)
limits = pltpu.CompilerParams(vmem_limit_bytes=44 * 1024 * 1024)


def split_pairs(raw, wide, rows):
    wide[: 2 * rows, :] = raw.astype(jnp.float32)
    keys = wide[pl.ds(0, rows, 2), :]
    values = wide[pl.ds(1, rows, 2), :]
    return jnp.concatenate([keys, values], axis=1).astype(jnp.bfloat16)


def prepare_kernel(
    new_ref, cache_ref, new_doc_ref, cache_doc_ref, own_ref, spread_ref, starts_ref, wide
):
    own_ref[...] = split_pairs(new_ref[...], wide, own_ref.shape[0])
    shard = split_pairs(cache_ref[...], wide, spread_ref.shape[1])
    for target in range(spread_ref.shape[0]):
        spread_ref[target] = shard
    new_doc = new_doc_ref[...]
    cache_doc = cache_doc_ref[...]
    first_doc = new_doc[:, :1]
    last_doc = new_doc[:, -1:]
    low = jnp.zeros(first_doc.shape, jnp.float32)
    high = jnp.full(first_doc.shape, float(cache_doc.size), jnp.float32)
    starts_ref[0] = 0
    starts_ref[documents + 1] = 0
    for doc in range(1, documents):
        before = jnp.sum((new_doc < doc).astype(jnp.float32))
        starts_ref[doc] = before.astype(jnp.int32)
        before = jnp.sum((cache_doc < doc).astype(jnp.float32))
        starts_ref[documents + 1 + doc] = before.astype(jnp.int32)
        low = jnp.where(first_doc == doc, before, low)
        high = jnp.where(last_doc == doc - 1, before, high)
    starts_ref[documents] = new_doc.size
    starts_ref[2 * documents + 1] = cache_doc.size
    starts_ref[2 * documents + 2] = jnp.max(high - low).astype(jnp.int32)


def pack_kernel(place_ref, starts_ref, shards_ref, own_ref, behind_ref, out_ref, *, rounds):
    groups, shard_rows, _ = shards_ref.shape
    count = out_ref.shape[0]
    tok = own_ref.shape[0]
    period = count * shard_rows
    cp_index = place_ref[0]
    blk_index = place_ref[1]
    row = lax.broadcasted_iota(jnp.int32, (shard_rows, 1), 0)
    for target in range(count):
        first = (cp_index * count + target) * tok
        low = jnp.int32(0)
        for doc in range(1, documents):
            low = jnp.where(first >= starts_ref[doc], starts_ref[documents + 1 + doc], low)
        reached = low - blk_index * shard_rows
        group = (reached - (shard_rows - 1) + period - 1) // period
        cut = reached - group * period
        for turn in range(rounds):
            here = jnp.minimum(group + turn, groups - 1)
            after = jnp.minimum(group + turn + 1, groups - 1)
            chosen = jnp.where(
                row >= cut,
                shards_ref[here].astype(jnp.float32),
                shards_ref[after].astype(jnp.float32),
            )
            out_ref[target, turn * shard_rows : (turn + 1) * shard_rows] = chosen.astype(
                jnp.bfloat16
            )

        @pl.when(blk_index <= target)
        def _():
            out_ref[target, rounds * shard_rows :] = own_ref[...]

        @pl.when(blk_index > target)
        def _():
            out_ref[target, rounds * shard_rows :] = behind_ref[...]


def attention_kernel(
    place_ref,
    starts_ref,
    cache_len_ref,
    queries_ref,
    arrived_ref,
    behind_ref,
    out_ref,
    new_scores,
    cache_scores,
    lane_max,
    lane_sum,
    total,
    *,
    shard_rows,
    rounds,
):
    tok, width = queries_ref.shape
    heads = width // head
    count = arrived_ref.shape[0]
    shards = cache_len_ref.shape[0]
    period = count * shard_rows
    span = pieces * shard_rows
    new_offset = rounds * shard_rows
    exponent_scale = math.log2(math.e) * head**-0.5
    block = place_ref[0] * count + place_ref[1]
    first = block * tok

    row_place = first + lax.broadcasted_iota(jnp.int32, (tok, 1), 0)
    row_start = jnp.zeros((tok, 1), jnp.int32)
    row_low = jnp.zeros((tok, 1), jnp.int32)
    row_high = jnp.full((tok, 1), starts_ref[documents + 2], jnp.int32)
    new_low = jnp.int32(0)
    cache_low = jnp.int32(0)
    cache_high = starts_ref[documents + 2]
    for doc in range(1, documents):
        start = starts_ref[doc]
        low = starts_ref[documents + 1 + doc]
        high = starts_ref[documents + 2 + doc]
        reached = row_place >= start
        row_start = jnp.where(reached, start, row_start)
        row_low = jnp.where(reached, low, row_low)
        row_high = jnp.where(reached, high, row_high)
        new_low = jnp.where(first >= start, start, new_low)
        cache_low = jnp.where(first >= start, low, cache_low)
        cache_high = jnp.where(first + tok - 1 >= start, high, cache_high)

    lane_max[...] = jnp.full(lane_max.shape, negative, jnp.float32)
    lane_sum[...] = jnp.zeros(lane_sum.shape, jnp.float32)
    total[...] = jnp.zeros(total.shape, jnp.float32)

    def score(keys, allowed, scores_ref, at):
        for h in range(heads):
            scores = lax.dot_general(
                queries_ref[:, h * head : (h + 1) * head],
                keys,
                (((1,), (1,)), ((), ())),
                preferred_element_type=jnp.float32,
            )
            scores = jnp.where(allowed, scores, negative)
            scores_ref[at, h] = scores
            best = scores[:, :head]
            for part in range(1, scores.shape[1] // head):
                best = jnp.maximum(best, scores[:, part * head : (part + 1) * head])
            lane_max[h] = jnp.maximum(lane_max[h], best)

    def weigh(values, scores_ref, at):
        for h in range(heads):
            scores = scores_ref[at, h]
            best = lane_max[h]
            added = lane_sum[h]
            parts = []
            for part in range(scores.shape[1] // head):
                piece = scores[:, part * head : (part + 1) * head]
                weight = jnp.exp2((piece - best) * exponent_scale)
                added = added + weight
                parts.append(weight.astype(jnp.bfloat16))
            lane_sum[h] = added
            rounded = parts[0] if len(parts) == 1 else jnp.concatenate(parts, axis=1)
            total[h] += jnp.dot(rounded, values, preferred_element_type=jnp.float32)

    first_block = new_low // tok
    farthest = block - count
    nearest = jnp.maximum(first_block, farthest + 1)

    def new_allowed(number):
        key_place = number * tok + lax.broadcasted_iota(jnp.int32, (1, tok), 1)
        return (key_place >= row_start) & (key_place <= row_place)

    @pl.loop(nearest, block + 1)
    def _(number):
        slot = number % count
        keys = arrived_ref[slot, new_offset:, :head]
        score(keys, new_allowed(number), new_scores, slot)

    @pl.when(first_block <= farthest)
    def _():
        score(behind_ref[:, :head], new_allowed(farthest), new_scores, count)

    def cache_tile(number):
        turn = number // (count // pieces)
        source = number % (count // pieces) * pieces
        base = cache_low + turn * period
        begin = base + jnp.bitwise_and(source * shard_rows - base, period - 1)
        holds = jnp.bitwise_and(base - source * shard_rows, period - 1) < span
        return turn, source, base, (begin < cache_high) | (holds & (base < cache_high))

    def cache_part(turn, source, first_lane):
        offset = pl.multiple_of(turn * shard_rows, shard_rows)
        return jnp.concatenate(
            [
                arrived_ref[source + part, pl.ds(offset, shard_rows), first_lane : first_lane + head]
                for part in range(pieces)
            ],
            axis=0,
        )

    tiles = rounds * count // pieces

    @pl.loop(0, tiles)
    def _(number):
        turn, source, base, needed = cache_tile(number)

        @pl.when(needed)
        def _():
            lane = lax.broadcasted_iota(jnp.int32, (1, span), 1)
            place = base + jnp.bitwise_and(source * shard_rows + lane - base, period - 1)
            shard = place // shard_rows
            filled = jnp.zeros((1, span), jnp.int32)
            for part in range(pieces):
                edge = (source + part) * shard_rows
                for at in (0, shard_rows - 1):
                    where = base + jnp.bitwise_and(edge + at - base, period - 1)
                    where = where // shard_rows
                    length = cache_len_ref[jnp.minimum(where, shards - 1)]
                    filled = jnp.where(shard == where, length, filled)
            usable = jnp.bitwise_and(place, shard_rows - 1) < filled
            allowed = (place >= row_low) & (place < row_high) & usable
            score(cache_part(turn, source, 0), allowed, cache_scores, number)

    for h in range(heads):
        best = jnp.max(lane_max[h], axis=1, keepdims=True)
        lane_max[h] = jnp.broadcast_to(best, (tok, head))

    @pl.loop(nearest, block + 1)
    def _(number):
        slot = number % count
        weigh(arrived_ref[slot, new_offset:, head:], new_scores, slot)

    @pl.when(first_block <= farthest)
    def _():
        weigh(behind_ref[:, head:], new_scores, count)

    @pl.loop(0, tiles)
    def _(number):
        turn, source, base, needed = cache_tile(number)

        @pl.when(needed)
        def _():
            weigh(cache_part(turn, source, head), cache_scores, number)

    for h in range(heads):
        row_total = jnp.sum(lane_sum[h], axis=1, keepdims=True)
        out_ref[:, h * head : (h + 1) * head] = (total[h] / row_total).astype(jnp.bfloat16)


def local(queries, new_kv, cached_key_value, new_doc, cache_doc, cache_len):
    tok = queries.shape[0]
    width = queries.shape[-1]
    heads = width // head
    shard_rows = cached_key_value.shape[0]
    blk_count = lax.axis_size("blk")
    cp_count = lax.axis_size("cp")
    head_count = lax.axis_size("head")
    assert tok * blk_count >= longest
    place = jnp.stack([lax.axis_index("cp"), lax.axis_index("blk")]).astype(jnp.int32)
    own, spread, starts = pl.pallas_call(
        prepare_kernel,
        out_shape=[
            jax.ShapeDtypeStruct((tok, 2 * head), jnp.bfloat16),
            jax.ShapeDtypeStruct((cp_count, shard_rows, 2 * head), jnp.bfloat16),
            jax.ShapeDtypeStruct((2 * documents + 3,), jnp.int32),
        ],
        in_specs=[vmem] * 4,
        out_specs=[vmem, vmem, smem],
        scratch_shapes=[pltpu.VMEM((2 * tok, head), jnp.float32)],
        compiler_params=limits,
    )(
        new_kv.reshape(2 * tok, head),
        cached_key_value.reshape(2 * shard_rows, head),
        new_doc.reshape(-1, tok),
        cache_doc.reshape(-1, 128),
    )
    behind = lax.ppermute(own, "cp", [(i, (i + 1) % cp_count) for i in range(cp_count)])
    shards = lax.all_to_all(spread, "cp", split_axis=0, concat_axis=0)

    def exchange(rounds):
        def run(shards, own, behind, starts, cache_len, queries):
            rows = rounds * shard_rows + tok
            packed = pl.pallas_call(
                functools.partial(pack_kernel, rounds=rounds),
                out_shape=jax.ShapeDtypeStruct((blk_count, rows, 2 * head), jnp.bfloat16),
                in_specs=[smem, smem, vmem, vmem, vmem],
                out_specs=vmem,
                compiler_params=limits,
            )(place, starts, shards, own, behind)
            arrived = lax.all_to_all(packed, "blk", split_axis=0, concat_axis=0)
            span = pieces * shard_rows
            tiles = rounds * blk_count // pieces
            return pl.pallas_call(
                functools.partial(attention_kernel, shard_rows=shard_rows, rounds=rounds),
                out_shape=jax.ShapeDtypeStruct((tok, width), jnp.bfloat16),
                in_specs=[smem, smem, smem, vmem, vmem, vmem],
                out_specs=vmem,
                scratch_shapes=[
                    pltpu.VMEM((blk_count + 1, heads, tok, tok), jnp.float32),
                    pltpu.VMEM((tiles, heads, tok, span), jnp.float32),
                    pltpu.VMEM((heads, tok, head), jnp.float32),
                    pltpu.VMEM((heads, tok, head), jnp.float32),
                    pltpu.VMEM((heads, tok, head), jnp.float32),
                ],
                compiler_params=limits,
            )(place, starts, cache_len, queries, arrived, behind)

        return run

    widest = starts[2 * documents + 2]
    period = blk_count * shard_rows
    turns = [2, 3, cp_count]
    pick = sum((widest > turn * period).astype(jnp.int32) for turn in turns[:-1])
    attended = lax.switch(
        pick,
        [exchange(turn) for turn in turns],
        shards,
        own,
        behind,
        starts,
        cache_len,
        queries[:, 0],
    )
    share = tok // head_count
    moved = lax.all_to_all(
        attended.reshape(head_count, share, width), "head", split_axis=0, concat_axis=0
    )
    return jnp.transpose(moved, (1, 0, 2))


def solution(mesh):
    placed = (
        P(("cp", "blk"), "head", None),
        P(("cp", "blk"), "head", None, None),
        P(("cp", "blk"), "head", None, None),
        P(),
        P(),
        P(),
    )
    return jax.shard_map(
        local,
        mesh=mesh,
        in_specs=placed,
        out_specs=P(("cp", "blk", "head"), None, None),
        check_vma=False,
    )
```

```python
import functools
import math

import jax
import jax.numpy as jnp
from jax import lax
from jax.experimental import pallas as pl
from jax.experimental.pallas import tpu as pltpu
from jax.sharding import PartitionSpec as P

negative = -1e30
documents = 16
longest = 1024
head = 128
pieces = 4
smem = pl.BlockSpec(memory_space=pltpu.SMEM)
vmem = pl.BlockSpec(memory_space=pltpu.VMEM)
limits = pltpu.CompilerParams(vmem_limit_bytes=44 * 1024 * 1024)


def split_pairs(raw, wide, rows):
    wide[: 2 * rows, :] = raw.astype(jnp.float32)
    keys = wide[pl.ds(0, rows, 2), :]
    values = wide[pl.ds(1, rows, 2), :]
    return jnp.concatenate([keys, values], axis=1).astype(jnp.bfloat16)


def prepare_kernel(
    new_ref,
    cache_ref,
    new_doc_ref,
    cache_doc_ref,
    own_ref,
    spread_ref,
    starts_ref,
    pick_ref,
    wide,
    *,
    turns,
    period,
):
    own_ref[...] = split_pairs(new_ref[...], wide, own_ref.shape[0])
    shard = split_pairs(cache_ref[...], wide, spread_ref.shape[1])
    for target in range(spread_ref.shape[0]):
        spread_ref[target] = shard
    new_doc = new_doc_ref[...]
    cache_doc = cache_doc_ref[...]
    first_doc = new_doc[:, :1]
    last_doc = new_doc[:, -1:]
    low = jnp.zeros(first_doc.shape, jnp.float32)
    high = jnp.full(first_doc.shape, float(cache_doc.size), jnp.float32)
    starts_ref[0] = 0
    starts_ref[documents + 1] = 0
    for doc in range(1, documents):
        before = jnp.sum((new_doc < doc).astype(jnp.float32))
        starts_ref[doc] = before.astype(jnp.int32)
        before = jnp.sum((cache_doc < doc).astype(jnp.float32))
        starts_ref[documents + 1 + doc] = before.astype(jnp.int32)
        low = jnp.where(first_doc == doc, before, low)
        high = jnp.where(last_doc == doc - 1, before, high)
    starts_ref[documents] = new_doc.size
    starts_ref[2 * documents + 1] = cache_doc.size
    widest = jnp.max(high - low).astype(jnp.int32)
    pick = jnp.int32(0)
    for turn in turns[:-1]:
        pick += (widest > turn * period).astype(jnp.int32)
    pick_ref[0] = pick


def pack_new_kernel(place_ref, own_ref, raw_ref, out_ref, behind_ref, wide):
    tok = own_ref.shape[0]
    own = own_ref[...]
    behind = split_pairs(raw_ref[...], wide, tok)
    behind_ref[...] = behind
    for target in range(out_ref.shape[0]):

        @pl.when(place_ref[1] <= target)
        def _():
            out_ref[target] = own

        @pl.when(place_ref[1] > target)
        def _():
            out_ref[target] = behind


def pack_cache_kernel(place_ref, starts_ref, shards_ref, out_ref, *, rounds, tok):
    groups, shard_rows, _ = shards_ref.shape
    count = out_ref.shape[0]
    period = count * shard_rows
    cp_index = place_ref[0]
    blk_index = place_ref[1]
    row = lax.broadcasted_iota(jnp.int32, (shard_rows, 1), 0)
    for target in range(count):
        first = (cp_index * count + target) * tok
        low = jnp.int32(0)
        for doc in range(1, documents):
            low = jnp.where(first >= starts_ref[doc], starts_ref[documents + 1 + doc], low)
        reached = low - blk_index * shard_rows
        group = (reached - (shard_rows - 1) + period - 1) // period
        cut = reached - group * period
        for turn in range(rounds):
            here = jnp.minimum(group + turn, groups - 1)
            after = jnp.minimum(group + turn + 1, groups - 1)
            chosen = jnp.where(
                row >= cut,
                shards_ref[here].astype(jnp.float32),
                shards_ref[after].astype(jnp.float32),
            )
            out_ref[target, turn * shard_rows : (turn + 1) * shard_rows] = chosen.astype(
                jnp.bfloat16
            )


def attention_kernel(
    place_ref,
    starts_ref,
    cache_len_ref,
    queries_ref,
    fresh_ref,
    behind_ref,
    arrived_ref,
    out_ref,
    new_scores,
    cache_scores,
    lane_max,
    lane_sum,
    total,
    *,
    shard_rows,
    rounds,
):
    tok, width = queries_ref.shape
    heads = width // head
    count = arrived_ref.shape[0]
    shards = cache_len_ref.shape[0]
    period = count * shard_rows
    span = pieces * shard_rows
    exponent_scale = math.log2(math.e) * head**-0.5
    block = place_ref[0] * count + place_ref[1]
    first = block * tok

    row_place = first + lax.broadcasted_iota(jnp.int32, (tok, 1), 0)
    row_start = jnp.zeros((tok, 1), jnp.int32)
    row_low = jnp.zeros((tok, 1), jnp.int32)
    row_high = jnp.full((tok, 1), starts_ref[documents + 2], jnp.int32)
    new_low = jnp.int32(0)
    cache_low = jnp.int32(0)
    cache_high = starts_ref[documents + 2]
    for doc in range(1, documents):
        start = starts_ref[doc]
        low = starts_ref[documents + 1 + doc]
        high = starts_ref[documents + 2 + doc]
        reached = row_place >= start
        row_start = jnp.where(reached, start, row_start)
        row_low = jnp.where(reached, low, row_low)
        row_high = jnp.where(reached, high, row_high)
        new_low = jnp.where(first >= start, start, new_low)
        cache_low = jnp.where(first >= start, low, cache_low)
        cache_high = jnp.where(first + tok - 1 >= start, high, cache_high)

    lane_max[...] = jnp.full(lane_max.shape, negative, jnp.float32)
    lane_sum[...] = jnp.zeros(lane_sum.shape, jnp.float32)
    total[...] = jnp.zeros(total.shape, jnp.float32)

    def score(keys, allowed, scores_ref, at):
        for h in range(heads):
            scores = lax.dot_general(
                queries_ref[:, h * head : (h + 1) * head],
                keys,
                (((1,), (1,)), ((), ())),
                preferred_element_type=jnp.float32,
            )
            scores = jnp.where(allowed, scores, negative)
            scores_ref[at, h] = scores
            best = scores[:, :head]
            for part in range(1, scores.shape[1] // head):
                best = jnp.maximum(best, scores[:, part * head : (part + 1) * head])
            lane_max[h] = jnp.maximum(lane_max[h], best)

    def weigh(values, scores_ref, at):
        for h in range(heads):
            scores = scores_ref[at, h]
            best = lane_max[h]
            added = lane_sum[h]
            parts = []
            for part in range(scores.shape[1] // head):
                piece = scores[:, part * head : (part + 1) * head]
                weight = jnp.exp2((piece - best) * exponent_scale)
                added = added + weight
                parts.append(weight.astype(jnp.bfloat16))
            lane_sum[h] = added
            rounded = parts[0] if len(parts) == 1 else jnp.concatenate(parts, axis=1)
            total[h] += jnp.dot(rounded, values, preferred_element_type=jnp.float32)

    first_block = new_low // tok
    farthest = block - count
    nearest = jnp.maximum(first_block, farthest + 1)

    def new_allowed(number):
        key_place = number * tok + lax.broadcasted_iota(jnp.int32, (1, tok), 1)
        return (key_place >= row_start) & (key_place <= row_place)

    @pl.loop(nearest, block + 1)
    def _(number):
        slot = number % count
        keys = fresh_ref[slot, :, :head]
        score(keys, new_allowed(number), new_scores, slot)

    @pl.when(first_block <= farthest)
    def _():
        score(behind_ref[:, :head], new_allowed(farthest), new_scores, count)

    def cache_tile(number):
        turn = number // (count // pieces)
        source = number % (count // pieces) * pieces
        base = cache_low + turn * period
        begin = base + jnp.bitwise_and(source * shard_rows - base, period - 1)
        holds = jnp.bitwise_and(base - source * shard_rows, period - 1) < span
        return turn, source, base, (begin < cache_high) | (holds & (base < cache_high))

    def cache_part(turn, source, first_lane):
        offset = pl.multiple_of(turn * shard_rows, shard_rows)
        return jnp.concatenate(
            [
                arrived_ref[source + part, pl.ds(offset, shard_rows), first_lane : first_lane + head]
                for part in range(pieces)
            ],
            axis=0,
        )

    tiles = rounds * count // pieces

    @pl.loop(0, tiles)
    def _(number):
        turn, source, base, needed = cache_tile(number)

        @pl.when(needed)
        def _():
            lane = lax.broadcasted_iota(jnp.int32, (1, span), 1)
            place = base + jnp.bitwise_and(source * shard_rows + lane - base, period - 1)
            shard = place // shard_rows
            filled = jnp.zeros((1, span), jnp.int32)
            for part in range(pieces):
                edge = (source + part) * shard_rows
                for at in (0, shard_rows - 1):
                    where = base + jnp.bitwise_and(edge + at - base, period - 1)
                    where = where // shard_rows
                    length = cache_len_ref[jnp.minimum(where, shards - 1)]
                    filled = jnp.where(shard == where, length, filled)
            usable = jnp.bitwise_and(place, shard_rows - 1) < filled
            allowed = (place >= row_low) & (place < row_high) & usable
            score(cache_part(turn, source, 0), allowed, cache_scores, number)

    for h in range(heads):
        best = jnp.max(lane_max[h], axis=1, keepdims=True)
        lane_max[h] = jnp.broadcast_to(best, (tok, head))

    @pl.loop(nearest, block + 1)
    def _(number):
        slot = number % count
        weigh(fresh_ref[slot, :, head:], new_scores, slot)

    @pl.when(first_block <= farthest)
    def _():
        weigh(behind_ref[:, head:], new_scores, count)

    @pl.loop(0, tiles)
    def _(number):
        turn, source, base, needed = cache_tile(number)

        @pl.when(needed)
        def _():
            weigh(cache_part(turn, source, head), cache_scores, number)

    for h in range(heads):
        row_total = jnp.sum(lane_sum[h], axis=1, keepdims=True)
        out_ref[:, h * head : (h + 1) * head] = (total[h] / row_total).astype(jnp.bfloat16)


def local(queries, new_kv, cached_key_value, new_doc, cache_doc, cache_len):
    tok = queries.shape[0]
    width = queries.shape[-1]
    heads = width // head
    shard_rows = cached_key_value.shape[0]
    blk_count = lax.axis_size("blk")
    cp_count = lax.axis_size("cp")
    head_count = lax.axis_size("head")
    assert tok * blk_count >= longest
    place = jnp.stack([lax.axis_index("cp"), lax.axis_index("blk")]).astype(jnp.int32)
    period = blk_count * shard_rows
    turns = [2, 3, cp_count]
    new_raw = new_kv.reshape(2 * tok, head)
    raw_behind = lax.ppermute(new_raw, "cp", [(i, (i + 1) % cp_count) for i in range(cp_count)])
    operands = (
        new_raw,
        cached_key_value.reshape(2 * shard_rows, head),
        new_doc.reshape(-1, tok),
        cache_doc.reshape(-1, 128),
    )
    own, spread, starts, pick = pl.pallas_call(
        functools.partial(prepare_kernel, turns=turns, period=period),
        grid=(1,),
        out_shape=[
            jax.ShapeDtypeStruct((tok, 2 * head), jnp.bfloat16),
            jax.ShapeDtypeStruct((cp_count, shard_rows, 2 * head), jnp.bfloat16),
            jax.ShapeDtypeStruct((2 * documents + 2,), jnp.int32),
            jax.ShapeDtypeStruct((1,), jnp.int32),
        ],
        in_specs=[pl.BlockSpec(operand.shape, lambda i: (0, 0)) for operand in operands],
        out_specs=[vmem, vmem, smem, smem],
        scratch_shapes=[pltpu.VMEM((2 * tok, head), jnp.float32)],
        compiler_params=pltpu.CompilerParams(vmem_limit_bytes=56 * 1024 * 1024),
    )(*operands)
    shards = lax.all_to_all(spread, "cp", split_axis=0, concat_axis=0)
    fresh, behind = pl.pallas_call(
        pack_new_kernel,
        out_shape=[
            jax.ShapeDtypeStruct((blk_count, tok, 2 * head), jnp.bfloat16),
            jax.ShapeDtypeStruct((tok, 2 * head), jnp.bfloat16),
        ],
        in_specs=[smem, vmem, vmem],
        out_specs=[vmem, vmem],
        scratch_shapes=[pltpu.VMEM((2 * tok, head), jnp.float32)],
        compiler_params=limits,
    )(place, own, raw_behind)
    fresh = lax.all_to_all(fresh, "blk", split_axis=0, concat_axis=0)

    def exchange(rounds):
        def run(shards, fresh, behind, starts, cache_len, queries):
            packed = pl.pallas_call(
                functools.partial(pack_cache_kernel, rounds=rounds, tok=tok),
                out_shape=jax.ShapeDtypeStruct(
                    (blk_count, rounds * shard_rows, 2 * head), jnp.bfloat16
                ),
                in_specs=[smem, smem, vmem],
                out_specs=vmem,
                compiler_params=limits,
            )(place, starts, shards)
            arrived = lax.all_to_all(packed, "blk", split_axis=0, concat_axis=0)
            span = pieces * shard_rows
            tiles = rounds * blk_count // pieces
            return pl.pallas_call(
                functools.partial(attention_kernel, shard_rows=shard_rows, rounds=rounds),
                out_shape=jax.ShapeDtypeStruct((tok, width), jnp.bfloat16),
                in_specs=[smem, smem, smem, vmem, vmem, vmem, vmem],
                out_specs=vmem,
                scratch_shapes=[
                    pltpu.VMEM((blk_count + 1, heads, tok, tok), jnp.float32),
                    pltpu.VMEM((tiles, heads, tok, span), jnp.float32),
                    pltpu.VMEM((heads, tok, head), jnp.float32),
                    pltpu.VMEM((heads, tok, head), jnp.float32),
                    pltpu.VMEM((heads, tok, head), jnp.float32),
                ],
                compiler_params=limits,
            )(place, starts, cache_len, queries, fresh, behind, arrived)

        return run

    attended = lax.switch(
        pick[0],
        [exchange(turn) for turn in turns],
        shards,
        fresh,
        behind,
        starts,
        cache_len,
        queries[:, 0],
    )
    share = tok // head_count
    moved = lax.all_to_all(
        attended.reshape(head_count, share, width), "head", split_axis=0, concat_axis=0
    )
    return jnp.transpose(moved, (1, 0, 2))


def solution(mesh):
    placed = (
        P(("cp", "blk"), "head", None),
        P(("cp", "blk"), "head", None, None),
        P(("cp", "blk"), "head", None, None),
        P(),
        P(),
        P(),
    )
    return jax.shard_map(
        local,
        mesh=mesh,
        in_specs=placed,
        out_specs=P(("cp", "blk", "head"), None, None),
        check_vma=False,
    )
```

```python
import functools
import math

import jax
import jax.numpy as jnp
from jax import lax
from jax.experimental import pallas as pl
from jax.experimental.pallas import tpu as pltpu
from jax.sharding import PartitionSpec as P

negative = -1e30
documents = 16
longest = 1024
head = 128
pieces = 4
smem = pl.BlockSpec(memory_space=pltpu.SMEM)
vmem = pl.BlockSpec(memory_space=pltpu.VMEM)
limits = pltpu.CompilerParams(vmem_limit_bytes=44 * 1024 * 1024)


def split_pairs(raw, wide, rows):
    wide[: 2 * rows, :] = raw.astype(jnp.float32)
    keys = wide[pl.ds(0, rows, 2), :]
    values = wide[pl.ds(1, rows, 2), :]
    return jnp.concatenate([keys, values], axis=1).astype(jnp.bfloat16)


def prepare_kernel(
    new_ref,
    cache_ref,
    new_doc_ref,
    cache_doc_ref,
    own_ref,
    spread_ref,
    starts_ref,
    pick_ref,
    wide,
    *,
    turns,
    period,
):
    own_ref[...] = split_pairs(new_ref[...], wide, own_ref.shape[0])
    shard = split_pairs(cache_ref[...], wide, spread_ref.shape[1])
    for target in range(spread_ref.shape[0]):
        spread_ref[target] = shard
    new_doc = new_doc_ref[...]
    cache_doc = cache_doc_ref[...]
    first_doc = new_doc[:, :1]
    last_doc = new_doc[:, -1:]
    low = jnp.zeros(first_doc.shape, jnp.float32)
    high = jnp.full(first_doc.shape, float(cache_doc.size), jnp.float32)
    starts_ref[0] = 0
    starts_ref[documents + 1] = 0
    for doc in range(1, documents):
        before = jnp.sum((new_doc < doc).astype(jnp.float32))
        starts_ref[doc] = before.astype(jnp.int32)
        before = jnp.sum((cache_doc < doc).astype(jnp.float32))
        starts_ref[documents + 1 + doc] = before.astype(jnp.int32)
        low = jnp.where(first_doc == doc, before, low)
        high = jnp.where(last_doc == doc - 1, before, high)
    starts_ref[documents] = new_doc.size
    starts_ref[2 * documents + 1] = cache_doc.size
    widest = jnp.max(high - low).astype(jnp.int32)
    pick = jnp.int32(0)
    for turn in turns[:-1]:
        pick += (widest > turn * period).astype(jnp.int32)
    pick_ref[0] = pick


def pack_new_kernel(place_ref, own_ref, raw_ref, out_ref, behind_ref, wide):
    tok = own_ref.shape[0]
    own = own_ref[...]
    behind = split_pairs(raw_ref[...], wide, tok)
    behind_ref[...] = behind
    for target in range(out_ref.shape[0]):

        @pl.when(place_ref[1] <= target)
        def _():
            out_ref[target] = own

        @pl.when(place_ref[1] > target)
        def _():
            out_ref[target] = behind


def pack_cache_kernel(place_ref, starts_ref, shards_ref, out_ref, *, turns, tok):
    groups, shard_rows, _ = shards_ref.shape
    count = out_ref.shape[0]
    period = count * shard_rows
    cp_index = place_ref[0]
    blk_index = place_ref[1]
    row = lax.broadcasted_iota(jnp.int32, (shard_rows, 1), 0)
    for target in range(count):
        first = (cp_index * count + target) * tok
        low = jnp.int32(0)
        for doc in range(1, documents):
            low = jnp.where(first >= starts_ref[doc], starts_ref[documents + 1 + doc], low)
        reached = low - blk_index * shard_rows
        group = (reached - (shard_rows - 1) + period - 1) // period
        cut = reached - group * period
        for at, turn in enumerate(turns):
            here = jnp.minimum(group + turn, groups - 1)
            after = jnp.minimum(group + turn + 1, groups - 1)
            chosen = jnp.where(
                row >= cut,
                shards_ref[here].astype(jnp.float32),
                shards_ref[after].astype(jnp.float32),
            )
            out_ref[target, at * shard_rows : (at + 1) * shard_rows] = chosen.astype(
                jnp.bfloat16
            )


def attention_kernel(
    place_ref,
    starts_ref,
    cache_len_ref,
    queries_ref,
    fresh_ref,
    behind_ref,
    arrived_ref,
    out_ref,
    new_scores,
    cache_scores,
    lane_max,
    lane_sum,
    total,
    *,
    shard_rows,
    rounds,
):
    tok, width = queries_ref.shape
    heads = width // head
    count = arrived_ref.shape[0]
    shards = cache_len_ref.shape[0]
    period = count * shard_rows
    span = pieces * shard_rows
    exponent_scale = math.log2(math.e) * head**-0.5
    block = place_ref[0] * count + place_ref[1]
    first = block * tok

    row_place = first + lax.broadcasted_iota(jnp.int32, (tok, 1), 0)
    row_start = jnp.zeros((tok, 1), jnp.int32)
    row_low = jnp.zeros((tok, 1), jnp.int32)
    row_high = jnp.full((tok, 1), starts_ref[documents + 2], jnp.int32)
    new_low = jnp.int32(0)
    cache_low = jnp.int32(0)
    cache_high = starts_ref[documents + 2]
    for doc in range(1, documents):
        start = starts_ref[doc]
        low = starts_ref[documents + 1 + doc]
        high = starts_ref[documents + 2 + doc]
        reached = row_place >= start
        row_start = jnp.where(reached, start, row_start)
        row_low = jnp.where(reached, low, row_low)
        row_high = jnp.where(reached, high, row_high)
        new_low = jnp.where(first >= start, start, new_low)
        cache_low = jnp.where(first >= start, low, cache_low)
        cache_high = jnp.where(first + tok - 1 >= start, high, cache_high)

    lane_max[...] = jnp.full(lane_max.shape, negative, jnp.float32)
    lane_sum[...] = jnp.zeros(lane_sum.shape, jnp.float32)
    total[...] = jnp.zeros(total.shape, jnp.float32)

    def score(keys, allowed, scores_ref, at):
        for h in range(heads):
            scores = lax.dot_general(
                queries_ref[:, h * head : (h + 1) * head],
                keys,
                (((1,), (1,)), ((), ())),
                preferred_element_type=jnp.float32,
            )
            scores = jnp.where(allowed, scores, negative)
            scores_ref[at, h] = scores
            best = scores[:, :head]
            for part in range(1, scores.shape[1] // head):
                best = jnp.maximum(best, scores[:, part * head : (part + 1) * head])
            lane_max[h] = jnp.maximum(lane_max[h], best)

    def weigh(values, scores_ref, at):
        for h in range(heads):
            scores = scores_ref[at, h]
            best = lane_max[h]
            added = lane_sum[h]
            parts = []
            for part in range(scores.shape[1] // head):
                piece = scores[:, part * head : (part + 1) * head]
                weight = jnp.exp2((piece - best) * exponent_scale)
                added = added + weight
                parts.append(weight.astype(jnp.bfloat16))
            lane_sum[h] = added
            rounded = parts[0] if len(parts) == 1 else jnp.concatenate(parts, axis=1)
            total[h] += jnp.dot(rounded, values, preferred_element_type=jnp.float32)

    first_block = new_low // tok
    farthest = block - count
    nearest = jnp.maximum(first_block, farthest + 1)

    def new_allowed(number):
        key_place = number * tok + lax.broadcasted_iota(jnp.int32, (1, tok), 1)
        return (key_place >= row_start) & (key_place <= row_place)

    @pl.loop(nearest, block + 1)
    def _(number):
        slot = number % count
        keys = fresh_ref[slot, :, :head]
        score(keys, new_allowed(number), new_scores, slot)

    @pl.when(first_block <= farthest)
    def _():
        score(behind_ref[:, :head], new_allowed(farthest), new_scores, count)

    def cache_tile(number):
        turn = number // (count // pieces)
        source = number % (count // pieces) * pieces
        base = cache_low + turn * period
        begin = base + jnp.bitwise_and(source * shard_rows - base, period - 1)
        holds = jnp.bitwise_and(base - source * shard_rows, period - 1) < span
        return turn, source, base, (begin < cache_high) | (holds & (base < cache_high))

    def cache_part(turn, source, first_lane):
        offset = pl.multiple_of(turn * shard_rows, shard_rows)
        return jnp.concatenate(
            [
                arrived_ref[source + part, pl.ds(offset, shard_rows), first_lane : first_lane + head]
                for part in range(pieces)
            ],
            axis=0,
        )

    tiles = rounds * count // pieces

    @pl.loop(0, tiles)
    def _(number):
        turn, source, base, needed = cache_tile(number)

        @pl.when(needed)
        def _():
            lane = lax.broadcasted_iota(jnp.int32, (1, span), 1)
            place = base + jnp.bitwise_and(source * shard_rows + lane - base, period - 1)
            shard = place // shard_rows
            filled = jnp.zeros((1, span), jnp.int32)
            for part in range(pieces):
                edge = (source + part) * shard_rows
                for at in (0, shard_rows - 1):
                    where = base + jnp.bitwise_and(edge + at - base, period - 1)
                    where = where // shard_rows
                    length = cache_len_ref[jnp.minimum(where, shards - 1)]
                    filled = jnp.where(shard == where, length, filled)
            usable = jnp.bitwise_and(place, shard_rows - 1) < filled
            allowed = (place >= row_low) & (place < row_high) & usable
            score(cache_part(turn, source, 0), allowed, cache_scores, number)

    for h in range(heads):
        best = jnp.max(lane_max[h], axis=1, keepdims=True)
        lane_max[h] = jnp.broadcast_to(best, (tok, head))

    @pl.loop(nearest, block + 1)
    def _(number):
        slot = number % count
        weigh(fresh_ref[slot, :, head:], new_scores, slot)

    @pl.when(first_block <= farthest)
    def _():
        weigh(behind_ref[:, head:], new_scores, count)

    @pl.loop(0, tiles)
    def _(number):
        turn, source, base, needed = cache_tile(number)

        @pl.when(needed)
        def _():
            weigh(cache_part(turn, source, head), cache_scores, number)

    for h in range(heads):
        row_total = jnp.sum(lane_sum[h], axis=1, keepdims=True)
        out_ref[:, h * head : (h + 1) * head] = (total[h] / row_total).astype(jnp.bfloat16)


def local(queries, new_kv, cached_key_value, new_doc, cache_doc, cache_len):
    tok = queries.shape[0]
    width = queries.shape[-1]
    heads = width // head
    shard_rows = cached_key_value.shape[0]
    blk_count = lax.axis_size("blk")
    cp_count = lax.axis_size("cp")
    head_count = lax.axis_size("head")
    assert tok * blk_count >= longest
    place = jnp.stack([lax.axis_index("cp"), lax.axis_index("blk")]).astype(jnp.int32)
    period = blk_count * shard_rows
    turns = [2, 3, cp_count]
    new_raw = new_kv.reshape(2 * tok, head)
    raw_behind = lax.ppermute(new_raw, "cp", [(i, (i + 1) % cp_count) for i in range(cp_count)])
    operands = (
        new_raw,
        cached_key_value.reshape(2 * shard_rows, head),
        new_doc.reshape(-1, tok),
        cache_doc.reshape(-1, 128),
    )
    own, spread, starts, pick = pl.pallas_call(
        functools.partial(prepare_kernel, turns=turns, period=period),
        grid=(1,),
        out_shape=[
            jax.ShapeDtypeStruct((tok, 2 * head), jnp.bfloat16),
            jax.ShapeDtypeStruct((cp_count, shard_rows, 2 * head), jnp.bfloat16),
            jax.ShapeDtypeStruct((2 * documents + 2,), jnp.int32),
            jax.ShapeDtypeStruct((1,), jnp.int32),
        ],
        in_specs=[pl.BlockSpec(operand.shape, lambda i: (0, 0)) for operand in operands],
        out_specs=[vmem, vmem, smem, smem],
        scratch_shapes=[pltpu.VMEM((2 * tok, head), jnp.float32)],
        compiler_params=pltpu.CompilerParams(vmem_limit_bytes=56 * 1024 * 1024),
    )(*operands)
    spread, raw_behind = lax.optimization_barrier((spread, raw_behind))
    shards = lax.all_to_all(spread, "cp", split_axis=0, concat_axis=0)
    fresh, behind = pl.pallas_call(
        pack_new_kernel,
        out_shape=[
            jax.ShapeDtypeStruct((blk_count, tok, 2 * head), jnp.bfloat16),
            jax.ShapeDtypeStruct((tok, 2 * head), jnp.bfloat16),
        ],
        in_specs=[smem, vmem, vmem],
        out_specs=[vmem, vmem],
        scratch_shapes=[pltpu.VMEM((2 * tok, head), jnp.float32)],
        compiler_params=limits,
    )(place, own, raw_behind)
    fresh = lax.all_to_all(fresh, "blk", split_axis=0, concat_axis=0)

    def cached_rows(turns, shards, starts):
        rows = len(turns) * shard_rows
        packed = pl.pallas_call(
            functools.partial(pack_cache_kernel, turns=turns, tok=tok),
            out_shape=jax.ShapeDtypeStruct((blk_count, rows, 2 * head), jnp.bfloat16),
            in_specs=[smem, smem, vmem],
            out_specs=vmem,
            compiler_params=limits,
        )(place, starts, shards)
        return lax.all_to_all(packed, "blk", split_axis=0, concat_axis=0)

    arrived = cached_rows(range(turns[0]), shards, starts)

    def attend(rounds):
        def run(shards, fresh, behind, arrived, starts, cache_len, queries):
            if rounds > turns[0]:
                more = cached_rows(range(turns[0], rounds), shards, starts)
                arrived = jnp.concatenate([arrived, more], axis=1)
            span = pieces * shard_rows
            tiles = rounds * blk_count // pieces
            return pl.pallas_call(
                functools.partial(attention_kernel, shard_rows=shard_rows, rounds=rounds),
                out_shape=jax.ShapeDtypeStruct((tok, width), jnp.bfloat16),
                in_specs=[smem, smem, smem, vmem, vmem, vmem, vmem],
                out_specs=vmem,
                scratch_shapes=[
                    pltpu.VMEM((blk_count + 1, heads, tok, tok), jnp.float32),
                    pltpu.VMEM((tiles, heads, tok, span), jnp.float32),
                    pltpu.VMEM((heads, tok, head), jnp.float32),
                    pltpu.VMEM((heads, tok, head), jnp.float32),
                    pltpu.VMEM((heads, tok, head), jnp.float32),
                ],
                compiler_params=limits,
            )(place, starts, cache_len, queries, fresh, behind, arrived)

        return run

    attended = lax.switch(
        pick[0],
        [attend(turn) for turn in turns],
        shards,
        fresh,
        behind,
        arrived,
        starts,
        cache_len,
        queries[:, 0],
    )
    share = tok // head_count
    moved = lax.all_to_all(
        attended.reshape(head_count, share, width), "head", split_axis=0, concat_axis=0
    )
    return jnp.transpose(moved, (1, 0, 2))


def solution(mesh):
    placed = (
        P(("cp", "blk"), "head", None),
        P(("cp", "blk"), "head", None, None),
        P(("cp", "blk"), "head", None, None),
        P(),
        P(),
        P(),
    )
    return jax.shard_map(
        local,
        mesh=mesh,
        in_specs=placed,
        out_specs=P(("cp", "blk", "head"), None, None),
        check_vma=False,
    )
```

```python
import functools
import math

import jax
import jax.numpy as jnp
from jax import lax
from jax.experimental import pallas as pl
from jax.experimental.pallas import tpu as pltpu
from jax.sharding import PartitionSpec as P

negative = -1e30
documents = 16
longest = 1024
head = 128
pieces = 4
smem = pl.BlockSpec(memory_space=pltpu.SMEM)
vmem = pl.BlockSpec(memory_space=pltpu.VMEM)
limits = pltpu.CompilerParams(vmem_limit_bytes=44 * 1024 * 1024)


def split_pairs(raw, wide, rows):
    wide[: 2 * rows, :] = raw.astype(jnp.float32)
    keys = wide[pl.ds(0, rows, 2), :]
    values = wide[pl.ds(1, rows, 2), :]
    return jnp.concatenate([keys, values], axis=1).astype(jnp.bfloat16)


def prepare_kernel(
    new_ref,
    before_ref,
    new_doc_ref,
    cache_doc_ref,
    pair_ref,
    starts_ref,
    pick_ref,
    wide,
    *,
    turns,
    period,
):
    tok = pair_ref.shape[0] // 2
    pair_ref[:tok] = split_pairs(before_ref[...], wide, tok)
    pair_ref[tok:] = split_pairs(new_ref[...], wide, tok)
    new_doc = new_doc_ref[...]
    cache_doc = cache_doc_ref[...]
    first_doc = new_doc[:, :1]
    last_doc = new_doc[:, -1:]
    low = jnp.zeros(first_doc.shape, jnp.float32)
    high = jnp.full(first_doc.shape, float(cache_doc.size), jnp.float32)
    starts_ref[0] = 0
    starts_ref[documents + 1] = 0
    for doc in range(1, documents):
        before = jnp.sum((new_doc < doc).astype(jnp.float32))
        starts_ref[doc] = before.astype(jnp.int32)
        before = jnp.sum((cache_doc < doc).astype(jnp.float32))
        starts_ref[documents + 1 + doc] = before.astype(jnp.int32)
        low = jnp.where(first_doc == doc, before, low)
        high = jnp.where(last_doc == doc - 1, before, high)
    starts_ref[documents] = new_doc.size
    starts_ref[2 * documents + 1] = cache_doc.size
    widest = jnp.max(high - low).astype(jnp.int32)
    pick = jnp.int32(0)
    for turn in turns[:-1]:
        pick += (widest > turn * period).astype(jnp.int32)
    pick_ref[0] = pick


def pack_cache_kernel(
    place_ref, starts_ref, raw_ref, out_ref, shards_ref, wide, *, turns, tok
):
    groups, shard_rows, _ = shards_ref.shape
    for group in range(groups):
        wide[group] = raw_ref[group].astype(jnp.float32)
        shards_ref[group, :, :head] = wide[group, pl.ds(0, shard_rows, 2), :]
        shards_ref[group, :, head:] = wide[group, pl.ds(1, shard_rows, 2), :]
    count = out_ref.shape[0]
    period = count * shard_rows
    cp_index = place_ref[0]
    blk_index = place_ref[1]
    row = lax.broadcasted_iota(jnp.int32, (shard_rows, 1), 0)
    for target in range(count):
        first = (cp_index * count + target) * tok
        low = jnp.int32(0)
        for doc in range(1, documents):
            low = jnp.where(first >= starts_ref[doc], starts_ref[documents + 1 + doc], low)
        reached = low - blk_index * shard_rows
        group = (reached - (shard_rows - 1) + period - 1) // period
        cut = reached - group * period
        for at, turn in enumerate(turns):
            here = jnp.minimum(group + turn, groups - 1)
            after = jnp.minimum(group + turn + 1, groups - 1)
            chosen = jnp.where(row >= cut, shards_ref[here], shards_ref[after])
            out_ref[target, at * shard_rows : (at + 1) * shard_rows] = chosen.astype(
                jnp.bfloat16
            )


def attention_kernel(
    place_ref,
    starts_ref,
    cache_len_ref,
    queries_ref,
    pair_ref,
    second_ref,
    fourth_ref,
    sixth_ref,
    arrived_ref,
    out_ref,
    window,
    new_scores,
    cache_scores,
    lane_max,
    lane_sum,
    total,
    *,
    shard_rows,
    rounds,
):
    tok, width = queries_ref.shape
    heads = width // head
    count = arrived_ref.shape[0]
    shards = cache_len_ref.shape[0]
    period = count * shard_rows
    span = pieces * shard_rows
    exponent_scale = math.log2(math.e) * head**-0.5
    block = place_ref[0] * count + place_ref[1]
    first = block * tok

    row_place = first + lax.broadcasted_iota(jnp.int32, (tok, 1), 0)
    row_start = jnp.zeros((tok, 1), jnp.int32)
    row_low = jnp.zeros((tok, 1), jnp.int32)
    row_high = jnp.full((tok, 1), starts_ref[documents + 2], jnp.int32)
    new_low = jnp.int32(0)
    cache_low = jnp.int32(0)
    cache_high = starts_ref[documents + 2]
    for doc in range(1, documents):
        start = starts_ref[doc]
        low = starts_ref[documents + 1 + doc]
        high = starts_ref[documents + 2 + doc]
        reached = row_place >= start
        row_start = jnp.where(reached, start, row_start)
        row_low = jnp.where(reached, low, row_low)
        row_high = jnp.where(reached, high, row_high)
        new_low = jnp.where(first >= start, start, new_low)
        cache_low = jnp.where(first >= start, low, cache_low)
        cache_high = jnp.where(first + tok - 1 >= start, high, cache_high)

    lane_max[...] = jnp.full(lane_max.shape, negative, jnp.float32)
    lane_sum[...] = jnp.zeros(lane_sum.shape, jnp.float32)
    total[...] = jnp.zeros(total.shape, jnp.float32)

    def score(keys, allowed, scores_ref, at):
        for h in range(heads):
            scores = lax.dot_general(
                queries_ref[:, h * head : (h + 1) * head],
                keys,
                (((1,), (1,)), ((), ())),
                preferred_element_type=jnp.float32,
            )
            scores = jnp.where(allowed, scores, negative)
            scores_ref[at, h] = scores
            best = scores[:, :head]
            for part in range(1, scores.shape[1] // head):
                best = jnp.maximum(best, scores[:, part * head : (part + 1) * head])
            lane_max[h] = jnp.maximum(lane_max[h], best)

    def weigh(values, scores_ref, at):
        for h in range(heads):
            scores = scores_ref[at, h]
            best = lane_max[h]
            added = lane_sum[h]
            parts = []
            for part in range(scores.shape[1] // head):
                piece = scores[:, part * head : (part + 1) * head]
                weight = jnp.exp2((piece - best) * exponent_scale)
                added = added + weight
                parts.append(weight.astype(jnp.bfloat16))
            lane_sum[h] = added
            rounded = parts[0] if len(parts) == 1 else jnp.concatenate(parts, axis=1)
            total[h] += jnp.dot(rounded, values, preferred_element_type=jnp.float32)

    first_block = new_low // tok
    farthest = block - count
    filled_rows = 0
    for part in (sixth_ref, fourth_ref, second_ref, pair_ref):
        window[filled_rows : filled_rows + part.shape[0]] = part[...]
        filled_rows += part.shape[0]

    @pl.loop(first_block, block + 1)
    def _(number):
        slot = number - farthest
        offset = pl.multiple_of(slot * tok, tok)
        keys = window[pl.ds(offset, tok), :head]
        key_place = number * tok + lax.broadcasted_iota(jnp.int32, (1, tok), 1)
        allowed = (key_place >= row_start) & (key_place <= row_place)
        score(keys, allowed, new_scores, slot)

    def cache_tile(number):
        turn = number // (count // pieces)
        source = number % (count // pieces) * pieces
        base = cache_low + turn * period
        begin = base + jnp.bitwise_and(source * shard_rows - base, period - 1)
        holds = jnp.bitwise_and(base - source * shard_rows, period - 1) < span
        return turn, source, base, (begin < cache_high) | (holds & (base < cache_high))

    def cache_part(turn, source, first_lane):
        offset = pl.multiple_of(turn * shard_rows, shard_rows)
        return jnp.concatenate(
            [
                arrived_ref[source + part, pl.ds(offset, shard_rows), first_lane : first_lane + head]
                for part in range(pieces)
            ],
            axis=0,
        )

    tiles = rounds * count // pieces

    @pl.loop(0, tiles)
    def _(number):
        turn, source, base, needed = cache_tile(number)

        @pl.when(needed)
        def _():
            lane = lax.broadcasted_iota(jnp.int32, (1, span), 1)
            place = base + jnp.bitwise_and(source * shard_rows + lane - base, period - 1)
            shard = place // shard_rows
            filled = jnp.zeros((1, span), jnp.int32)
            for part in range(pieces):
                edge = (source + part) * shard_rows
                for at in (0, shard_rows - 1):
                    where = base + jnp.bitwise_and(edge + at - base, period - 1)
                    where = where // shard_rows
                    length = cache_len_ref[jnp.minimum(where, shards - 1)]
                    filled = jnp.where(shard == where, length, filled)
            usable = jnp.bitwise_and(place, shard_rows - 1) < filled
            allowed = (place >= row_low) & (place < row_high) & usable
            score(cache_part(turn, source, 0), allowed, cache_scores, number)

    for h in range(heads):
        best = jnp.max(lane_max[h], axis=1, keepdims=True)
        lane_max[h] = jnp.broadcast_to(best, (tok, head))

    @pl.loop(first_block, block + 1)
    def _(number):
        slot = number - farthest
        offset = pl.multiple_of(slot * tok, tok)
        weigh(window[pl.ds(offset, tok), head:], new_scores, slot)

    @pl.loop(0, tiles)
    def _(number):
        turn, source, base, needed = cache_tile(number)

        @pl.when(needed)
        def _():
            weigh(cache_part(turn, source, head), cache_scores, number)

    for h in range(heads):
        row_total = jnp.sum(lane_sum[h], axis=1, keepdims=True)
        out_ref[:, h * head : (h + 1) * head] = (total[h] / row_total).astype(jnp.bfloat16)


def local(queries, new_kv, cached_key_value, new_doc, cache_doc, cache_len):
    tok = queries.shape[0]
    width = queries.shape[-1]
    heads = width // head
    shard_rows = cached_key_value.shape[0]
    blk_count = lax.axis_size("blk")
    cp_count = lax.axis_size("cp")
    head_count = lax.axis_size("head")
    assert tok * blk_count >= longest
    place = jnp.stack([lax.axis_index("cp"), lax.axis_index("blk")]).astype(jnp.int32)
    period = blk_count * shard_rows
    turns = [2, 3, cp_count]
    block_count = cp_count * blk_count

    def ahead(value, steps):
        pairs = [(block, (block + steps) % block_count) for block in range(block_count)]
        return lax.ppermute(value, ("cp", "blk"), pairs)

    new_raw = new_kv.reshape(2 * tok, head)
    cache_raw = cached_key_value.reshape(2 * shard_rows, head)
    raw_before = ahead(new_raw, 1)
    spread = jnp.broadcast_to(cache_raw[None], (cp_count,) + cache_raw.shape)
    spread, raw_before = lax.optimization_barrier((spread, raw_before))
    shards = lax.all_to_all(spread, "cp", split_axis=0, concat_axis=0)
    operands = (new_raw, raw_before, new_doc.reshape(-1, tok), cache_doc.reshape(-1, 128))
    pair, starts, pick = pl.pallas_call(
        functools.partial(prepare_kernel, turns=turns, period=period),
        grid=(1,),
        out_shape=[
            jax.ShapeDtypeStruct((2 * tok, 2 * head), jnp.bfloat16),
            jax.ShapeDtypeStruct((2 * documents + 2,), jnp.int32),
            jax.ShapeDtypeStruct((1,), jnp.int32),
        ],
        in_specs=[pl.BlockSpec(operand.shape, lambda i: (0, 0)) for operand in operands],
        out_specs=[vmem, smem, smem],
        scratch_shapes=[pltpu.VMEM((2 * tok, head), jnp.float32)],
        compiler_params=pltpu.CompilerParams(vmem_limit_bytes=56 * 1024 * 1024),
    )(*operands)
    second = ahead(pair, 2)
    fourth = ahead(pair, 4)
    sixth = ahead(jnp.concatenate([second[tok:], pair], axis=0), 6)

    def cached_rows(turns, shards, starts):
        rows = len(turns) * shard_rows
        packed = pl.pallas_call(
            functools.partial(pack_cache_kernel, turns=turns, tok=tok),
            out_shape=jax.ShapeDtypeStruct((blk_count, rows, 2 * head), jnp.bfloat16),
            in_specs=[smem, smem, vmem],
            out_specs=vmem,
            scratch_shapes=[
                pltpu.VMEM((cp_count, shard_rows, 2 * head), jnp.float32),
                pltpu.VMEM((cp_count, 2 * shard_rows, head), jnp.float32),
            ],
            compiler_params=limits,
        )(place, starts, shards)
        return lax.all_to_all(packed, "blk", split_axis=0, concat_axis=0)

    arrived = cached_rows(range(turns[0]), shards, starts)

    def attend(rounds):
        def run(shards, pair, second, fourth, sixth, arrived, starts, cache_len, queries):
            if rounds > turns[0]:
                more = cached_rows(range(turns[0], rounds), shards, starts)
                arrived = jnp.concatenate([arrived, more], axis=1)
            span = pieces * shard_rows
            tiles = rounds * blk_count // pieces
            return pl.pallas_call(
                functools.partial(attention_kernel, shard_rows=shard_rows, rounds=rounds),
                out_shape=jax.ShapeDtypeStruct((tok, width), jnp.bfloat16),
                in_specs=[smem] * 3 + [vmem] * 6,
                out_specs=vmem,
                scratch_shapes=[
                    pltpu.VMEM(((blk_count + 1) * tok, 2 * head), jnp.bfloat16),
                    pltpu.VMEM((blk_count + 1, heads, tok, tok), jnp.float32),
                    pltpu.VMEM((tiles, heads, tok, span), jnp.float32),
                    pltpu.VMEM((heads, tok, head), jnp.float32),
                    pltpu.VMEM((heads, tok, head), jnp.float32),
                    pltpu.VMEM((heads, tok, head), jnp.float32),
                ],
                compiler_params=limits,
            )(place, starts, cache_len, queries, pair, second, fourth, sixth, arrived)

        return run

    attended = lax.switch(
        pick[0],
        [attend(turn) for turn in turns],
        shards,
        pair,
        second,
        fourth,
        sixth,
        arrived,
        starts,
        cache_len,
        queries[:, 0],
    )
    share = tok // head_count
    moved = lax.all_to_all(
        attended.reshape(head_count, share, width), "head", split_axis=0, concat_axis=0
    )
    return jnp.transpose(moved, (1, 0, 2))


def solution(mesh):
    placed = (
        P(("cp", "blk"), "head", None),
        P(("cp", "blk"), "head", None, None),
        P(("cp", "blk"), "head", None, None),
        P(),
        P(),
        P(),
    )
    return jax.shard_map(
        local,
        mesh=mesh,
        in_specs=placed,
        out_specs=P(("cp", "blk", "head"), None, None),
        check_vma=False,
    )
```

```python
import functools
import math

import jax
import jax.numpy as jnp
from jax import lax
from jax.experimental import pallas as pl
from jax.experimental.pallas import tpu as pltpu
from jax.sharding import PartitionSpec as P

negative = -1e30
documents = 16
longest = 1024
head = 128
pieces = 4
exponent_scale = math.log2(math.e) * head**-0.5
smem = pl.BlockSpec(memory_space=pltpu.SMEM)
vmem = pl.BlockSpec(memory_space=pltpu.VMEM)
limits = pltpu.CompilerParams(vmem_limit_bytes=44 * 1024 * 1024)
large = pltpu.CompilerParams(vmem_limit_bytes=56 * 1024 * 1024)


def split_pairs(raw, wide, rows):
    wide[: 2 * rows, :] = raw.astype(jnp.float32)
    keys = wide[pl.ds(0, rows, 2), :]
    values = wide[pl.ds(1, rows, 2), :]
    return jnp.concatenate([keys, values], axis=1).astype(jnp.bfloat16)


def spread_kernel(cache_ref, spread_ref, wide):
    shard = split_pairs(cache_ref[...], wide, spread_ref.shape[1])
    for target in range(spread_ref.shape[0]):
        spread_ref[target] = shard


def prepare_kernel(
    new_ref,
    before_ref,
    new_doc_ref,
    cache_doc_ref,
    pair_ref,
    own_ref,
    starts_ref,
    pick_ref,
    wide,
    *,
    turns,
    period,
):
    tok = pair_ref.shape[0] // 2
    pair_ref[:tok] = split_pairs(before_ref[...], wide, tok)
    own = split_pairs(new_ref[...], wide, tok)
    pair_ref[tok:] = own
    own_ref[...] = own
    new_doc = new_doc_ref[...]
    cache_doc = cache_doc_ref[...]
    first_doc = new_doc[:, :1]
    last_doc = new_doc[:, -1:]
    low = jnp.zeros(first_doc.shape, jnp.float32)
    high = jnp.full(first_doc.shape, float(cache_doc.size), jnp.float32)
    starts_ref[0] = 0
    starts_ref[documents + 1] = 0
    for doc in range(1, documents):
        before = jnp.sum((new_doc < doc).astype(jnp.float32))
        starts_ref[doc] = before.astype(jnp.int32)
        before = jnp.sum((cache_doc < doc).astype(jnp.float32))
        starts_ref[documents + 1 + doc] = before.astype(jnp.int32)
        low = jnp.where(first_doc == doc, before, low)
        high = jnp.where(last_doc == doc - 1, before, high)
    starts_ref[documents] = new_doc.size
    starts_ref[2 * documents + 1] = cache_doc.size
    widest = jnp.max(high - low).astype(jnp.int32)
    pick = jnp.int32(0)
    for turn in turns[:-1]:
        pick += (widest > turn * period).astype(jnp.int32)
    pick_ref[0] = pick


def pack_cache_kernel(place_ref, starts_ref, shards_ref, out_ref, *, turns, tok):
    groups, shard_rows, _ = shards_ref.shape
    count = out_ref.shape[0]
    period = count * shard_rows
    cp_index = place_ref[0] // count
    blk_index = place_ref[0] % count
    row = lax.broadcasted_iota(jnp.int32, (shard_rows, 1), 0)
    for target in range(count):
        first = (cp_index * count + target) * tok
        low = jnp.int32(0)
        for doc in range(1, documents):
            low = jnp.where(first >= starts_ref[doc], starts_ref[documents + 1 + doc], low)
        reached = low - blk_index * shard_rows
        group = (reached - (shard_rows - 1) + period - 1) // period
        cut = reached - group * period
        for at, turn in enumerate(turns):
            here = jnp.minimum(group + turn, groups - 1)
            after = jnp.minimum(group + turn + 1, groups - 1)
            chosen = jnp.where(
                row >= cut,
                shards_ref[here].astype(jnp.float32),
                shards_ref[after].astype(jnp.float32),
            )
            out_ref[target, at * shard_rows : (at + 1) * shard_rows] = chosen.astype(
                jnp.bfloat16
            )


def row_bounds(starts_ref, first, tok):
    row_place = first + lax.broadcasted_iota(jnp.int32, (tok, 1), 0)
    row_start = jnp.zeros((tok, 1), jnp.int32)
    row_low = jnp.zeros((tok, 1), jnp.int32)
    row_high = jnp.full((tok, 1), starts_ref[documents + 2], jnp.int32)
    for doc in range(1, documents):
        reached = row_place >= starts_ref[doc]
        row_start = jnp.where(reached, starts_ref[doc], row_start)
        row_low = jnp.where(reached, starts_ref[documents + 1 + doc], row_low)
        row_high = jnp.where(reached, starts_ref[documents + 2 + doc], row_high)
    return row_place, row_start, row_low, row_high


def block_bounds(starts_ref, first, tok):
    new_low = jnp.int32(0)
    cache_low = jnp.int32(0)
    cache_high = starts_ref[documents + 2]
    for doc in range(1, documents):
        start = starts_ref[doc]
        new_low = jnp.where(first >= start, start, new_low)
        cache_low = jnp.where(first >= start, starts_ref[documents + 1 + doc], cache_low)
        cache_high = jnp.where(
            first + tok - 1 >= start, starts_ref[documents + 2 + doc], cache_high
        )
    return new_low, cache_low, cache_high


def score(queries_ref, keys, allowed, scores_ref, at, lane_max):
    for h in range(lane_max.shape[0]):
        scores = lax.dot_general(
            queries_ref[:, h * head : (h + 1) * head],
            keys,
            (((1,), (1,)), ((), ())),
            preferred_element_type=jnp.float32,
        )
        scores = jnp.where(allowed, scores, negative)
        scores_ref[at, h] = scores
        best = scores[:, :head]
        for part in range(1, scores.shape[1] // head):
            best = jnp.maximum(best, scores[:, part * head : (part + 1) * head])
        lane_max[h] = jnp.maximum(lane_max[h], best)


def weigh(values, scores_ref, at, lane_max, lane_sum, total):
    for h in range(lane_max.shape[0]):
        scores = scores_ref[at, h]
        best = lane_max[h]
        added = lane_sum[h]
        parts = []
        for part in range(scores.shape[1] // head):
            piece = scores[:, part * head : (part + 1) * head]
            weight = jnp.exp2((piece - best) * exponent_scale)
            added = added + weight
            parts.append(weight.astype(jnp.bfloat16))
        lane_sum[h] = added
        rounded = parts[0] if len(parts) == 1 else jnp.concatenate(parts, axis=1)
        total[h] += jnp.dot(rounded, values, preferred_element_type=jnp.float32)


def settle(lane_max):
    for h in range(lane_max.shape[0]):
        best = jnp.max(lane_max[h], axis=1, keepdims=True)
        lane_max[h] = jnp.broadcast_to(best, lane_max.shape[1:])


def new_kernel(
    place_ref,
    starts_ref,
    queries_ref,
    pair_ref,
    second_ref,
    fourth_ref,
    sixth_ref,
    lane_max,
    lane_sum,
    total,
    window,
    scores_ref,
):
    tok = queries_ref.shape[0]
    count = window.shape[0] // tok
    block = place_ref[0]
    first = block * tok
    row_place, row_start, _, _ = row_bounds(starts_ref, first, tok)
    new_low, _, _ = block_bounds(starts_ref, first, tok)
    lane_max[...] = jnp.full(lane_max.shape, negative, jnp.float32)
    lane_sum[...] = jnp.zeros(lane_sum.shape, jnp.float32)
    total[...] = jnp.zeros(total.shape, jnp.float32)
    filled = 0
    for part in (sixth_ref, fourth_ref, second_ref, pair_ref):
        window[filled : filled + part.shape[0]] = part[...]
        filled += part.shape[0]
    oldest = block - count + 1
    first_block = jnp.maximum(new_low // tok, oldest)

    @pl.loop(first_block, block + 1)
    def _(number):
        slot = number - oldest
        keys = window[pl.ds(pl.multiple_of(slot * tok, tok), tok), :head]
        key_place = number * tok + lax.broadcasted_iota(jnp.int32, (1, tok), 1)
        allowed = (key_place >= row_start) & (key_place <= row_place)
        score(queries_ref, keys, allowed, scores_ref, slot, lane_max)

    settle(lane_max)

    @pl.loop(first_block, block + 1)
    def _(number):
        slot = number - oldest
        values = window[pl.ds(pl.multiple_of(slot * tok, tok), tok), head:]
        weigh(values, scores_ref, slot, lane_max, lane_sum, total)


def cache_kernel(
    place_ref,
    starts_ref,
    cache_len_ref,
    queries_ref,
    eighth_ref,
    arrived_ref,
    new_max_ref,
    new_sum_ref,
    new_total_ref,
    out_ref,
    cache_scores,
    eighth_scores,
    lane_max,
    lane_sum,
    total,
    *,
    shard_rows,
    rounds,
):
    tok = queries_ref.shape[0]
    heads = lane_max.shape[0]
    count = arrived_ref.shape[0]
    shards = cache_len_ref.shape[0]
    period = count * shard_rows
    span = pieces * shard_rows
    block = place_ref[0]
    first = block * tok
    row_place, row_start, row_low, row_high = row_bounds(starts_ref, first, tok)
    new_low, cache_low, cache_high = block_bounds(starts_ref, first, tok)
    lane_max[...] = new_max_ref[...]
    farthest = block - count
    reaches = new_low // tok <= farthest

    @pl.when(reaches)
    def _():
        key_place = farthest * tok + lax.broadcasted_iota(jnp.int32, (1, tok), 1)
        allowed = (key_place >= row_start) & (key_place <= row_place)
        score(queries_ref, eighth_ref[:, :head], allowed, eighth_scores, 0, lane_max)

    def cache_tile(number):
        turn = number // (count // pieces)
        source = number % (count // pieces) * pieces
        base = cache_low + turn * period
        begin = base + jnp.bitwise_and(source * shard_rows - base, period - 1)
        holds = jnp.bitwise_and(base - source * shard_rows, period - 1) < span
        return turn, source, base, (begin < cache_high) | (holds & (base < cache_high))

    def cache_part(turn, source, first_lane):
        offset = pl.multiple_of(turn * shard_rows, shard_rows)
        return jnp.concatenate(
            [
                arrived_ref[source + part, pl.ds(offset, shard_rows), first_lane : first_lane + head]
                for part in range(pieces)
            ],
            axis=0,
        )

    tiles = rounds * count // pieces

    @pl.loop(0, tiles)
    def _(number):
        turn, source, base, needed = cache_tile(number)

        @pl.when(needed)
        def _():
            lane = lax.broadcasted_iota(jnp.int32, (1, span), 1)
            place = base + jnp.bitwise_and(source * shard_rows + lane - base, period - 1)
            shard = place // shard_rows
            filled = jnp.zeros((1, span), jnp.int32)
            for part in range(pieces):
                edge = (source + part) * shard_rows
                for at in (0, shard_rows - 1):
                    where = base + jnp.bitwise_and(edge + at - base, period - 1)
                    where = where // shard_rows
                    length = cache_len_ref[jnp.minimum(where, shards - 1)]
                    filled = jnp.where(shard == where, length, filled)
            usable = jnp.bitwise_and(place, shard_rows - 1) < filled
            allowed = (place >= row_low) & (place < row_high) & usable
            keys = cache_part(turn, source, 0)
            score(queries_ref, keys, allowed, cache_scores, number, lane_max)

    settle(lane_max)
    for h in range(heads):
        scale = jnp.exp2((new_max_ref[h] - lane_max[h]) * exponent_scale)
        lane_sum[h] = new_sum_ref[h] * scale
        total[h] = new_total_ref[h] * scale

    @pl.when(reaches)
    def _():
        weigh(eighth_ref[:, head:], eighth_scores, 0, lane_max, lane_sum, total)

    @pl.loop(0, tiles)
    def _(number):
        turn, source, base, needed = cache_tile(number)

        @pl.when(needed)
        def _():
            values = cache_part(turn, source, head)
            weigh(values, cache_scores, number, lane_max, lane_sum, total)

    for h in range(heads):
        row_total = jnp.sum(lane_sum[h], axis=1, keepdims=True)
        out_ref[:, h * head : (h + 1) * head] = (total[h] / row_total).astype(jnp.bfloat16)


def local(queries, new_kv, cached_key_value, new_doc, cache_doc, cache_len):
    tok = queries.shape[0]
    width = queries.shape[-1]
    heads = width // head
    shard_rows = cached_key_value.shape[0]
    blk_count = lax.axis_size("blk")
    cp_count = lax.axis_size("cp")
    head_count = lax.axis_size("head")
    assert tok * blk_count >= longest
    block_count = cp_count * blk_count
    period = blk_count * shard_rows
    turns = [2, 3, cp_count]
    place = lax.axis_index(("cp", "blk")).astype(jnp.int32)[None]

    def ahead(value, steps):
        pairs = [(block, (block + steps) % block_count) for block in range(block_count)]
        return lax.ppermute(value, ("cp", "blk"), pairs)

    new_raw = new_kv.reshape(2 * tok, head)
    cache_raw = cached_key_value.reshape(2 * shard_rows, head)
    raw_before = ahead(new_raw, 1)
    spread = pl.pallas_call(
        spread_kernel,
        out_shape=jax.ShapeDtypeStruct((cp_count, shard_rows, 2 * head), jnp.bfloat16),
        in_specs=[vmem],
        out_specs=vmem,
        scratch_shapes=[pltpu.VMEM((2 * shard_rows, head), jnp.float32)],
        compiler_params=large,
    )(cache_raw)
    spread, raw_before = lax.optimization_barrier((spread, raw_before))
    shards = lax.all_to_all(spread, "cp", split_axis=0, concat_axis=0)
    operands = (new_raw, raw_before, new_doc.reshape(-1, tok), cache_doc.reshape(-1, 128))
    pair, own, starts, pick = pl.pallas_call(
        functools.partial(prepare_kernel, turns=turns, period=period),
        grid=(1,),
        out_shape=[
            jax.ShapeDtypeStruct((2 * tok, 2 * head), jnp.bfloat16),
            jax.ShapeDtypeStruct((tok, 2 * head), jnp.bfloat16),
            jax.ShapeDtypeStruct((2 * documents + 2,), jnp.int32),
            jax.ShapeDtypeStruct((1,), jnp.int32),
        ],
        in_specs=[pl.BlockSpec(operand.shape, lambda i: (0, 0)) for operand in operands],
        out_specs=[vmem, vmem, smem, smem],
        scratch_shapes=[pltpu.VMEM((2 * tok, head), jnp.float32)],
        compiler_params=limits,
    )(*operands)
    second = ahead(pair, 2)
    fourth = ahead(pair, 4)
    sixth = ahead(pair, 6)
    shards, own, second, fourth, sixth = lax.optimization_barrier(
        (shards, own, second, fourth, sixth)
    )
    eighth = ahead(own, 8)

    def cached_rows(turns, shards, starts):
        rows = len(turns) * shard_rows
        packed = pl.pallas_call(
            functools.partial(pack_cache_kernel, turns=turns, tok=tok),
            out_shape=jax.ShapeDtypeStruct((blk_count, rows, 2 * head), jnp.bfloat16),
            in_specs=[smem, smem, vmem],
            out_specs=vmem,
            compiler_params=limits,
        )(place, starts, shards)
        return lax.all_to_all(packed, "blk", split_axis=0, concat_axis=0)

    arrived = cached_rows(range(turns[0]), shards, starts)
    state = jax.ShapeDtypeStruct((heads, tok, head), jnp.float32)
    states = pl.pallas_call(
        new_kernel,
        out_shape=[state] * 3,
        in_specs=[smem] * 2 + [vmem] * 5,
        out_specs=[vmem] * 3,
        scratch_shapes=[
            pltpu.VMEM((blk_count * tok, 2 * head), jnp.bfloat16),
            pltpu.VMEM((blk_count, heads, tok, tok), jnp.float32),
        ],
        compiler_params=limits,
        cost_estimate=pl.CostEstimate(
            flops=4 * heads * tok * tok * head * blk_count,
            bytes_accessed=8 * tok * width,
            transcendentals=heads * tok * tok * blk_count,
        ),
    )(place, starts, queries[:, 0], pair, second, fourth, sixth)

    def attend(rounds):
        def run(shards, eighth, arrived, starts, cache_len, queries, states):
            if rounds > turns[0]:
                more = cached_rows(range(turns[0], rounds), shards, starts)
                arrived = jnp.concatenate([arrived, more], axis=1)
            span = pieces * shard_rows
            tiles = rounds * blk_count // pieces
            return pl.pallas_call(
                functools.partial(cache_kernel, shard_rows=shard_rows, rounds=rounds),
                out_shape=jax.ShapeDtypeStruct((tok, width), jnp.bfloat16),
                in_specs=[smem] * 3 + [vmem] * 6,
                out_specs=vmem,
                scratch_shapes=[
                    pltpu.VMEM((tiles, heads, tok, span), jnp.float32),
                    pltpu.VMEM((1, heads, tok, tok), jnp.float32),
                    pltpu.VMEM((heads, tok, head), jnp.float32),
                    pltpu.VMEM((heads, tok, head), jnp.float32),
                    pltpu.VMEM((heads, tok, head), jnp.float32),
                ],
                compiler_params=limits,
            )(place, starts, cache_len, queries, eighth, arrived, *states)

        return run

    attended = lax.switch(
        pick[0],
        [attend(turn) for turn in turns],
        shards,
        eighth,
        arrived,
        starts,
        cache_len,
        queries[:, 0],
        states,
    )
    share = tok // head_count
    moved = lax.all_to_all(
        attended.reshape(head_count, share, width), "head", split_axis=0, concat_axis=0
    )
    return jnp.transpose(moved, (1, 0, 2))


def solution(mesh):
    placed = (
        P(("cp", "blk"), "head", None),
        P(("cp", "blk"), "head", None, None),
        P(("cp", "blk"), "head", None, None),
        P(),
        P(),
        P(),
    )
    return jax.shard_map(
        local,
        mesh=mesh,
        in_specs=placed,
        out_specs=P(("cp", "blk", "head"), None, None),
        check_vma=False,
    )
```

```python
import functools
import math

import jax
import jax.numpy as jnp
from jax import lax
from jax.experimental import pallas as pl
from jax.experimental.pallas import tpu as pltpu
from jax.sharding import PartitionSpec as P

negative = -1e30
documents = 16
longest = 1024
head = 128
pieces = 4
smem = pl.BlockSpec(memory_space=pltpu.SMEM)
vmem = pl.BlockSpec(memory_space=pltpu.VMEM)
exponent_scale = math.log2(math.e) * head**-0.5
limits = pltpu.CompilerParams(vmem_limit_bytes=44 * 1024 * 1024)
large = pltpu.CompilerParams(vmem_limit_bytes=56 * 1024 * 1024)


def split_pairs(raw, wide, rows):
    wide[: 2 * rows, :] = raw.astype(jnp.float32)
    keys = wide[pl.ds(0, rows, 2), :]
    values = wide[pl.ds(1, rows, 2), :]
    return jnp.concatenate([keys, values], axis=1).astype(jnp.bfloat16)


def spread_kernel(cache_ref, spread_ref, wide):
    shard = split_pairs(cache_ref[...], wide, spread_ref.shape[1])
    for target in range(spread_ref.shape[0]):
        spread_ref[target] = shard


def prepare_kernel(
    new_ref, new_doc_ref, cache_doc_ref, own_ref, starts_ref, pick_ref, wide, *, turns, period
):
    own_ref[...] = split_pairs(new_ref[...], wide, own_ref.shape[0])
    new_doc = new_doc_ref[...]
    cache_doc = cache_doc_ref[...]
    first_doc = new_doc[:, :1]
    last_doc = new_doc[:, -1:]
    low = jnp.zeros(first_doc.shape, jnp.float32)
    high = jnp.full(first_doc.shape, float(cache_doc.size), jnp.float32)
    starts_ref[0] = 0
    starts_ref[documents + 1] = 0
    for doc in range(1, documents):
        before = jnp.sum((new_doc < doc).astype(jnp.float32))
        starts_ref[doc] = before.astype(jnp.int32)
        before = jnp.sum((cache_doc < doc).astype(jnp.float32))
        starts_ref[documents + 1 + doc] = before.astype(jnp.int32)
        low = jnp.where(first_doc == doc, before, low)
        high = jnp.where(last_doc == doc - 1, before, high)
    starts_ref[documents] = new_doc.size
    starts_ref[2 * documents + 1] = cache_doc.size
    widest = jnp.max(high - low).astype(jnp.int32)
    pick = jnp.int32(0)
    for turn in turns[:-1]:
        pick += (widest > turn * period).astype(jnp.int32)
    pick_ref[0] = pick


def pack_kernel(
    place_ref, starts_ref, shards_ref, own_ref, raw_ref, out_ref, behind_ref, wide, *, rounds
):
    groups, shard_rows, _ = shards_ref.shape
    count = out_ref.shape[0]
    tok = own_ref.shape[0]
    period = count * shard_rows
    cp_index = place_ref[0]
    blk_index = place_ref[1]
    behind_ref[...] = split_pairs(raw_ref[...], wide, tok)
    row = lax.broadcasted_iota(jnp.int32, (shard_rows, 1), 0)
    for target in range(count):
        first = (cp_index * count + target) * tok
        low = jnp.int32(0)
        for doc in range(1, documents):
            low = jnp.where(first >= starts_ref[doc], starts_ref[documents + 1 + doc], low)
        reached = low - blk_index * shard_rows
        group = (reached - (shard_rows - 1) + period - 1) // period
        cut = reached - group * period
        for turn in range(rounds):
            here = jnp.minimum(group + turn, groups - 1)
            after = jnp.minimum(group + turn + 1, groups - 1)
            chosen = jnp.where(
                row >= cut,
                shards_ref[here].astype(jnp.float32),
                shards_ref[after].astype(jnp.float32),
            )
            out_ref[target, turn * shard_rows : (turn + 1) * shard_rows] = chosen.astype(
                jnp.bfloat16
            )

        @pl.when(blk_index <= target)
        def _():
            out_ref[target, rounds * shard_rows :] = own_ref[...]

        @pl.when(blk_index > target)
        def _():
            out_ref[target, rounds * shard_rows :] = behind_ref[...]


def row_bounds(starts_ref, first, tok):
    row_place = first + lax.broadcasted_iota(jnp.int32, (tok, 1), 0)
    row_start = jnp.zeros((tok, 1), jnp.int32)
    row_low = jnp.zeros((tok, 1), jnp.int32)
    row_high = jnp.full((tok, 1), starts_ref[documents + 2], jnp.int32)
    for doc in range(1, documents):
        reached = row_place >= starts_ref[doc]
        row_start = jnp.where(reached, starts_ref[doc], row_start)
        row_low = jnp.where(reached, starts_ref[documents + 1 + doc], row_low)
        row_high = jnp.where(reached, starts_ref[documents + 2 + doc], row_high)
    return row_place, row_start, row_low, row_high


def block_bounds(starts_ref, first, tok):
    new_low = jnp.int32(0)
    cache_low = jnp.int32(0)
    cache_high = starts_ref[documents + 2]
    for doc in range(1, documents):
        start = starts_ref[doc]
        new_low = jnp.where(first >= start, start, new_low)
        cache_low = jnp.where(first >= start, starts_ref[documents + 1 + doc], cache_low)
        cache_high = jnp.where(
            first + tok - 1 >= start, starts_ref[documents + 2 + doc], cache_high
        )
    return new_low, cache_low, cache_high


def score(queries_ref, keys, allowed, scores_ref, at, lane_max):
    for h in range(lane_max.shape[0]):
        scores = lax.dot_general(
            queries_ref[:, h * head : (h + 1) * head],
            keys,
            (((1,), (1,)), ((), ())),
            preferred_element_type=jnp.float32,
        )
        scores = jnp.where(allowed, scores, negative)
        scores_ref[at, h] = scores
        best = scores[:, :head]
        for part in range(1, scores.shape[1] // head):
            best = jnp.maximum(best, scores[:, part * head : (part + 1) * head])
        lane_max[h] = jnp.maximum(lane_max[h], best)


def weigh(values, scores_ref, at, lane_max, lane_sum, total):
    for h in range(lane_max.shape[0]):
        scores = scores_ref[at, h]
        best = lane_max[h]
        added = lane_sum[h]
        parts = []
        for part in range(scores.shape[1] // head):
            piece = scores[:, part * head : (part + 1) * head]
            weight = jnp.exp2((piece - best) * exponent_scale)
            added = added + weight
            parts.append(weight.astype(jnp.bfloat16))
        lane_sum[h] = added
        rounded = parts[0] if len(parts) == 1 else jnp.concatenate(parts, axis=1)
        total[h] += jnp.dot(rounded, values, preferred_element_type=jnp.float32)


def settle(lane_max):
    for h in range(lane_max.shape[0]):
        best = jnp.max(lane_max[h], axis=1, keepdims=True)
        lane_max[h] = jnp.broadcast_to(best, lane_max.shape[1:])


def attention_kernel(
    place_ref,
    starts_ref,
    cache_len_ref,
    queries_ref,
    arrived_ref,
    behind_ref,
    out_ref,
    new_scores,
    far_scores,
    cache_scores,
    lane_max,
    lane_sum,
    total,
    *,
    shard_rows,
    rounds,
):
    tok = queries_ref.shape[0]
    heads = lane_max.shape[0]
    count = arrived_ref.shape[0]
    shards = cache_len_ref.shape[0]
    period = count * shard_rows
    span = pieces * shard_rows
    new_offset = rounds * shard_rows
    block = place_ref[0] * count + place_ref[1]
    first = block * tok
    row_place, row_start, row_low, row_high = row_bounds(starts_ref, first, tok)
    new_low, cache_low, cache_high = block_bounds(starts_ref, first, tok)
    lane_max[...] = jnp.full(lane_max.shape, negative, jnp.float32)
    lane_sum[...] = jnp.zeros(lane_sum.shape, jnp.float32)
    total[...] = jnp.zeros(total.shape, jnp.float32)
    farthest = block - count
    first_block = new_low // tok
    new_tiles = jnp.minimum((block - first_block) // 2 + 1, count // 2)
    reaches = first_block <= farthest

    def new_part(number, first_lane):
        lanes = slice(first_lane, first_lane + head)
        return jnp.concatenate(
            [
                arrived_ref[lax.rem(block - 2 * number - back + count, count), new_offset:, lanes]
                for back in (1, 0)
            ],
            axis=0,
        )

    def new_allowed(place, lanes):
        key_place = place + lax.broadcasted_iota(jnp.int32, (1, lanes), 1)
        return (key_place >= row_start) & (key_place <= row_place)

    @pl.loop(0, new_tiles)
    def _(number):
        allowed = new_allowed((block - 2 * number - 1) * tok, 2 * tok)
        score(queries_ref, new_part(number, 0), allowed, new_scores, number, lane_max)

    @pl.when(reaches)
    def _():
        allowed = new_allowed(farthest * tok, tok)
        score(queries_ref, behind_ref[:, :head], allowed, far_scores, 0, lane_max)

    def cache_tile(number):
        turn = number // (count // pieces)
        source = number % (count // pieces) * pieces
        base = cache_low + turn * period
        begin = base + jnp.bitwise_and(source * shard_rows - base, period - 1)
        holds = jnp.bitwise_and(base - source * shard_rows, period - 1) < span
        return turn, source, base, (begin < cache_high) | (holds & (base < cache_high))

    def cache_part(turn, source, first_lane):
        offset = pl.multiple_of(turn * shard_rows, shard_rows)
        return jnp.concatenate(
            [
                arrived_ref[source + part, pl.ds(offset, shard_rows), first_lane : first_lane + head]
                for part in range(pieces)
            ],
            axis=0,
        )

    tiles = rounds * count // pieces

    @pl.loop(0, tiles)
    def _(number):
        turn, source, base, needed = cache_tile(number)

        @pl.when(needed)
        def _():
            lane = lax.broadcasted_iota(jnp.int32, (1, span), 1)
            place = base + jnp.bitwise_and(source * shard_rows + lane - base, period - 1)
            shard = place // shard_rows
            filled = jnp.zeros((1, span), jnp.int32)
            for part in range(pieces):
                edge = (source + part) * shard_rows
                for at in (0, shard_rows - 1):
                    where = base + jnp.bitwise_and(edge + at - base, period - 1)
                    where = where // shard_rows
                    length = cache_len_ref[jnp.minimum(where, shards - 1)]
                    filled = jnp.where(shard == where, length, filled)
            usable = jnp.bitwise_and(place, shard_rows - 1) < filled
            allowed = (place >= row_low) & (place < row_high) & usable
            keys = cache_part(turn, source, 0)
            score(queries_ref, keys, allowed, cache_scores, number, lane_max)

    settle(lane_max)

    @pl.loop(0, new_tiles)
    def _(number):
        weigh(new_part(number, head), new_scores, number, lane_max, lane_sum, total)

    @pl.when(reaches)
    def _():
        weigh(behind_ref[:, head:], far_scores, 0, lane_max, lane_sum, total)

    @pl.loop(0, tiles)
    def _(number):
        turn, source, base, needed = cache_tile(number)

        @pl.when(needed)
        def _():
            values = cache_part(turn, source, head)
            weigh(values, cache_scores, number, lane_max, lane_sum, total)

    for h in range(heads):
        row_total = jnp.sum(lane_sum[h], axis=1, keepdims=True)
        out_ref[:, h * head : (h + 1) * head] = (total[h] / row_total).astype(jnp.bfloat16)


def local(queries, new_kv, cached_key_value, new_doc, cache_doc, cache_len):
    tok = queries.shape[0]
    width = queries.shape[-1]
    heads = width // head
    shard_rows = cached_key_value.shape[0]
    blk_count = lax.axis_size("blk")
    cp_count = lax.axis_size("cp")
    head_count = lax.axis_size("head")
    assert tok * blk_count >= longest
    place = jnp.stack([lax.axis_index("cp"), lax.axis_index("blk")]).astype(jnp.int32)
    period = blk_count * shard_rows
    turns = [2, 3, cp_count]
    new_raw = new_kv.reshape(2 * tok, head)
    cache_raw = cached_key_value.reshape(2 * shard_rows, head)
    spread = pl.pallas_call(
        spread_kernel,
        out_shape=jax.ShapeDtypeStruct((cp_count, shard_rows, 2 * head), jnp.bfloat16),
        in_specs=[vmem],
        out_specs=vmem,
        scratch_shapes=[pltpu.VMEM((2 * shard_rows, head), jnp.float32)],
        compiler_params=large,
    )(cache_raw)
    shards = lax.all_to_all(spread, "cp", split_axis=0, concat_axis=0)
    raw_behind = lax.ppermute(new_raw, "cp", [(i, (i + 1) % cp_count) for i in range(cp_count)])
    own, starts, pick = pl.pallas_call(
        functools.partial(prepare_kernel, turns=turns, period=period),
        out_shape=[
            jax.ShapeDtypeStruct((tok, 2 * head), jnp.bfloat16),
            jax.ShapeDtypeStruct((2 * documents + 2,), jnp.int32),
            jax.ShapeDtypeStruct((1,), jnp.int32),
        ],
        in_specs=[vmem] * 3,
        out_specs=[vmem, smem, smem],
        scratch_shapes=[pltpu.VMEM((2 * tok, head), jnp.float32)],
        compiler_params=limits,
    )(new_raw, new_doc.reshape(-1, tok), cache_doc.reshape(-1, 128))

    def exchange(rounds):
        def run(shards, own, raw_behind, starts, cache_len, queries):
            rows = rounds * shard_rows + tok
            packed, behind = pl.pallas_call(
                functools.partial(pack_kernel, rounds=rounds),
                out_shape=[
                    jax.ShapeDtypeStruct((blk_count, rows, 2 * head), jnp.bfloat16),
                    jax.ShapeDtypeStruct((tok, 2 * head), jnp.bfloat16),
                ],
                in_specs=[smem, smem, vmem, vmem, vmem],
                out_specs=[vmem, vmem],
                scratch_shapes=[pltpu.VMEM((2 * tok, head), jnp.float32)],
                compiler_params=limits,
            )(place, starts, shards, own, raw_behind)
            arrived = lax.all_to_all(packed, "blk", split_axis=0, concat_axis=0)
            span = pieces * shard_rows
            tiles = rounds * blk_count // pieces
            return pl.pallas_call(
                functools.partial(attention_kernel, shard_rows=shard_rows, rounds=rounds),
                out_shape=jax.ShapeDtypeStruct((tok, width), jnp.bfloat16),
                in_specs=[smem, smem, smem, vmem, vmem, vmem],
                out_specs=vmem,
                scratch_shapes=[
                    pltpu.VMEM((blk_count // 2, heads, tok, 2 * tok), jnp.float32),
                    pltpu.VMEM((1, heads, tok, tok), jnp.float32),
                    pltpu.VMEM((tiles, heads, tok, span), jnp.float32),
                    pltpu.VMEM((heads, tok, head), jnp.float32),
                    pltpu.VMEM((heads, tok, head), jnp.float32),
                    pltpu.VMEM((heads, tok, head), jnp.float32),
                ],
                compiler_params=limits,
            )(place, starts, cache_len, queries, arrived, behind)

        return run

    attended = lax.switch(
        pick[0],
        [exchange(turn) for turn in turns],
        shards,
        own,
        raw_behind,
        starts,
        cache_len,
        queries[:, 0],
    )
    share = tok // head_count
    moved = lax.all_to_all(
        attended.reshape(head_count, share, width), "head", split_axis=0, concat_axis=0
    )
    return jnp.transpose(moved, (1, 0, 2))


def solution(mesh):
    placed = (
        P(("cp", "blk"), "head", None),
        P(("cp", "blk"), "head", None, None),
        P(("cp", "blk"), "head", None, None),
        P(),
        P(),
        P(),
    )
    return jax.shard_map(
        local,
        mesh=mesh,
        in_specs=placed,
        out_specs=P(("cp", "blk", "head"), None, None),
        check_vma=False,
    )
```

```python
import functools
import math

import jax
import jax.numpy as jnp
from jax import lax
from jax.experimental import pallas as pl
from jax.experimental.pallas import tpu as pltpu
from jax.sharding import PartitionSpec as P

negative = -1e30
documents = 16
block_at, new_low_at, cache_low_at, cache_high_at, target_low_at = 0, 1, 2, 3, 4
longest = 1024
head = 128
pieces = 4
smem = pl.BlockSpec(memory_space=pltpu.SMEM)
vmem = pl.BlockSpec(memory_space=pltpu.VMEM)
exponent_scale = math.log2(math.e) * head**-0.5
limits = pltpu.CompilerParams(vmem_limit_bytes=44 * 1024 * 1024)


def split_pairs(raw, wide, rows):
    wide[: 2 * rows, :] = raw.astype(jnp.float32)
    keys = wide[pl.ds(0, rows, 2), :]
    values = wide[pl.ds(1, rows, 2), :]
    return jnp.concatenate([keys, values], axis=1).astype(jnp.bfloat16)


def spread_kernel(cache_ref, spread_ref, wide):
    shard = split_pairs(cache_ref[...], wide, spread_ref.shape[1])
    for target in range(spread_ref.shape[0]):
        spread_ref[target] = shard


def table_places(count):
    new_starts = target_low_at + count
    cache_starts = new_starts + documents + 1
    return new_starts, cache_starts, cache_starts + documents + 1


def prepare_kernel(
    place_ref,
    cache_len_ref,
    new_ref,
    new_doc_ref,
    cache_doc_ref,
    own_ref,
    table_ref,
    pick_ref,
    wide,
    *,
    turns,
    period,
    count,
):
    tok = own_ref.shape[0]
    new_starts, cache_starts, lengths = table_places(count)
    own_ref[...] = split_pairs(new_ref[...], wide, tok)
    new_doc = new_doc_ref[...]
    cache_doc = cache_doc_ref[...]
    first_doc = new_doc[:, :1]
    last_doc = new_doc[:, -1:]
    low = jnp.zeros(first_doc.shape, jnp.float32)
    high = jnp.full(first_doc.shape, float(cache_doc.size), jnp.float32)
    new_at = [jnp.int32(0)]
    cache_at = [jnp.int32(0)]
    for doc in range(1, documents):
        before = jnp.sum((new_doc < doc).astype(jnp.float32))
        new_at.append(before.astype(jnp.int32))
        before = jnp.sum((cache_doc < doc).astype(jnp.float32))
        cache_at.append(before.astype(jnp.int32))
        low = jnp.where(first_doc == doc, before, low)
        high = jnp.where(last_doc == doc - 1, before, high)
    new_at.append(jnp.int32(new_doc.size))
    cache_at.append(jnp.int32(cache_doc.size))
    for doc in range(documents + 1):
        table_ref[new_starts + doc] = new_at[doc]
        table_ref[cache_starts + doc] = cache_at[doc]
    for shard in range(cache_len_ref.shape[0]):
        table_ref[lengths + shard] = cache_len_ref[shard]

    def cache_start(place):
        found = jnp.int32(0)
        for doc in range(1, documents):
            found = jnp.where(place >= new_at[doc], cache_at[doc], found)
        return found

    block = place_ref[0]
    first = block * tok
    group_first = block // count * count * tok
    new_low = jnp.int32(0)
    cache_high = cache_at[1]
    for doc in range(1, documents):
        new_low = jnp.where(first >= new_at[doc], new_at[doc], new_low)
        cache_high = jnp.where(first + tok - 1 >= new_at[doc], cache_at[doc + 1], cache_high)
    table_ref[block_at] = block
    table_ref[new_low_at] = new_low
    table_ref[cache_low_at] = cache_start(first)
    table_ref[cache_high_at] = cache_high
    for target in range(count):
        table_ref[target_low_at + target] = cache_start(group_first + target * tok)
    widest = jnp.max(high - low).astype(jnp.int32)
    pick = jnp.int32(0)
    for turn in turns[:-1]:
        pick += (widest > turn * period).astype(jnp.int32)
    pick_ref[0] = pick


def pack_kernel(
    table_ref, shards_ref, own_ref, raw_ref, out_ref, behind_ref, wide, *, rounds
):
    groups, shard_rows, _ = shards_ref.shape
    count = out_ref.shape[0]
    tok = own_ref.shape[0]
    period = count * shard_rows
    blk_index = table_ref[block_at] % count
    behind_ref[...] = split_pairs(raw_ref[...], wide, tok)
    row = lax.broadcasted_iota(jnp.int32, (shard_rows, 1), 0)
    for target in range(count):
        low = table_ref[target_low_at + target]
        reached = low - blk_index * shard_rows
        group = (reached - (shard_rows - 1) + period - 1) // period
        cut = reached - group * period
        for turn in range(rounds):
            here = jnp.minimum(group + turn, groups - 1)
            after = jnp.minimum(group + turn + 1, groups - 1)
            chosen = jnp.where(
                row >= cut,
                shards_ref[here].astype(jnp.float32),
                shards_ref[after].astype(jnp.float32),
            )
            out_ref[target, turn * shard_rows : (turn + 1) * shard_rows] = chosen.astype(
                jnp.bfloat16
            )

        @pl.when(blk_index <= target)
        def _():
            out_ref[target, rounds * shard_rows :] = own_ref[...]

        @pl.when(blk_index > target)
        def _():
            out_ref[target, rounds * shard_rows :] = behind_ref[...]


def row_bounds(table_ref, count, first, tok):
    new_starts, cache_starts, _ = table_places(count)
    row_place = first + lax.broadcasted_iota(jnp.int32, (tok, 1), 0)
    row_start = jnp.zeros((tok, 1), jnp.int32)
    row_low = jnp.zeros((tok, 1), jnp.int32)
    row_high = jnp.full((tok, 1), table_ref[cache_starts + 1], jnp.int32)
    for doc in range(1, documents):
        start = table_ref[new_starts + doc]
        reached = row_place >= start
        row_start = jnp.where(reached, start, row_start)
        row_low = jnp.where(reached, table_ref[cache_starts + doc], row_low)
        row_high = jnp.where(reached, table_ref[cache_starts + doc + 1], row_high)
    return row_place, row_start, row_low, row_high


def score(queries_ref, keys, allowed, scores_ref, at, lane_max):
    for h in range(lane_max.shape[0]):
        scores = lax.dot_general(
            queries_ref[:, h * head : (h + 1) * head],
            keys,
            (((1,), (1,)), ((), ())),
            preferred_element_type=jnp.float32,
        )
        scores = jnp.where(allowed, scores, negative)
        scores_ref[at, h] = scores
        best = scores[:, :head]
        for part in range(1, scores.shape[1] // head):
            best = jnp.maximum(best, scores[:, part * head : (part + 1) * head])
        lane_max[h] = jnp.maximum(lane_max[h], best)


def weigh(values, scores_ref, at, lane_max, lane_sum, total):
    for h in range(lane_max.shape[0]):
        scores = scores_ref[at, h]
        best = lane_max[h]
        added = lane_sum[h]
        parts = []
        for part in range(scores.shape[1] // head):
            piece = scores[:, part * head : (part + 1) * head]
            weight = jnp.exp2((piece - best) * exponent_scale)
            added = added + weight
            parts.append(weight.astype(jnp.bfloat16))
        lane_sum[h] = added
        rounded = parts[0] if len(parts) == 1 else jnp.concatenate(parts, axis=1)
        total[h] += jnp.dot(rounded, values, preferred_element_type=jnp.float32)


def settle(lane_max):
    for h in range(lane_max.shape[0]):
        best = jnp.max(lane_max[h], axis=1, keepdims=True)
        lane_max[h] = jnp.broadcast_to(best, lane_max.shape[1:])


def attention_kernel(
    table_ref,
    queries_ref,
    arrived_ref,
    behind_ref,
    out_ref,
    new_scores,
    far_scores,
    cache_scores,
    lane_max,
    lane_sum,
    total,
    *,
    shard_rows,
    rounds,
    shards,
):
    tok = queries_ref.shape[0]
    heads = lane_max.shape[0]
    count = arrived_ref.shape[0]
    lengths = table_places(count)[2]
    period = count * shard_rows
    span = pieces * shard_rows
    new_offset = rounds * shard_rows
    block = table_ref[block_at]
    cache_low = table_ref[cache_low_at]
    cache_high = table_ref[cache_high_at]
    row_place, row_start, row_low, row_high = row_bounds(table_ref, count, block * tok, tok)
    lane_max[...] = jnp.full(lane_max.shape, negative, jnp.float32)
    lane_sum[...] = jnp.zeros(lane_sum.shape, jnp.float32)
    total[...] = jnp.zeros(total.shape, jnp.float32)
    farthest = block - count
    first_block = table_ref[new_low_at] // tok
    new_tiles = jnp.minimum((block - first_block) // 2 + 1, count // 2)
    reaches = first_block <= farthest

    def new_part(number, first_lane):
        lanes = slice(first_lane, first_lane + head)
        return jnp.concatenate(
            [
                arrived_ref[lax.rem(block - 2 * number - back + count, count), new_offset:, lanes]
                for back in (1, 0)
            ],
            axis=0,
        )

    def new_allowed(place, lanes):
        key_place = place + lax.broadcasted_iota(jnp.int32, (1, lanes), 1)
        return (key_place >= row_start) & (key_place <= row_place)

    @pl.loop(0, new_tiles)
    def _(number):
        allowed = new_allowed((block - 2 * number - 1) * tok, 2 * tok)
        score(queries_ref, new_part(number, 0), allowed, new_scores, number, lane_max)

    @pl.when(reaches)
    def _():
        allowed = new_allowed(farthest * tok, tok)
        score(queries_ref, behind_ref[:, :head], allowed, far_scores, 0, lane_max)

    def cache_tile(number):
        turn = number // (count // pieces)
        source = number % (count // pieces) * pieces
        base = cache_low + turn * period
        begin = base + jnp.bitwise_and(source * shard_rows - base, period - 1)
        holds = jnp.bitwise_and(base - source * shard_rows, period - 1) < span
        return turn, source, base, (begin < cache_high) | (holds & (base < cache_high))

    def cache_part(turn, source, first_lane):
        offset = pl.multiple_of(turn * shard_rows, shard_rows)
        return jnp.concatenate(
            [
                arrived_ref[source + part, pl.ds(offset, shard_rows), first_lane : first_lane + head]
                for part in range(pieces)
            ],
            axis=0,
        )

    tiles = rounds * count // pieces

    @pl.loop(0, tiles)
    def _(number):
        turn, source, base, needed = cache_tile(number)

        @pl.when(needed)
        def _():
            lane = lax.broadcasted_iota(jnp.int32, (1, span), 1)
            place = base + jnp.bitwise_and(source * shard_rows + lane - base, period - 1)
            shard = place // shard_rows
            filled = jnp.zeros((1, span), jnp.int32)
            for part in range(pieces):
                edge = (source + part) * shard_rows
                for at in (0, shard_rows - 1):
                    where = base + jnp.bitwise_and(edge + at - base, period - 1)
                    where = where // shard_rows
                    length = table_ref[lengths + jnp.minimum(where, shards - 1)]
                    filled = jnp.where(shard == where, length, filled)
            usable = jnp.bitwise_and(place, shard_rows - 1) < filled
            allowed = (place >= row_low) & (place < row_high) & usable
            keys = cache_part(turn, source, 0)
            score(queries_ref, keys, allowed, cache_scores, number, lane_max)

    settle(lane_max)

    @pl.loop(0, new_tiles)
    def _(number):
        weigh(new_part(number, head), new_scores, number, lane_max, lane_sum, total)

    @pl.when(reaches)
    def _():
        weigh(behind_ref[:, head:], far_scores, 0, lane_max, lane_sum, total)

    @pl.loop(0, tiles)
    def _(number):
        turn, source, base, needed = cache_tile(number)

        @pl.when(needed)
        def _():
            values = cache_part(turn, source, head)
            weigh(values, cache_scores, number, lane_max, lane_sum, total)

    for h in range(heads):
        row_total = jnp.sum(lane_sum[h], axis=1, keepdims=True)
        out_ref[:, h * head : (h + 1) * head] = (total[h] / row_total).astype(jnp.bfloat16)


def local(queries, new_kv, cached_key_value, new_doc, cache_doc, cache_len):
    tok = queries.shape[0]
    width = queries.shape[-1]
    heads = width // head
    shard_rows = cached_key_value.shape[0]
    blk_count = lax.axis_size("blk")
    cp_count = lax.axis_size("cp")
    head_count = lax.axis_size("head")
    assert tok * blk_count >= longest
    shard_count = cache_len.shape[0]
    place = lax.axis_index(("cp", "blk")).astype(jnp.int32)[None]
    period = blk_count * shard_rows
    turns = [2, 3, cp_count]
    new_raw = new_kv.reshape(2 * tok, head)
    cache_raw = cached_key_value.reshape(2 * shard_rows, head)
    spread = pl.pallas_call(
        spread_kernel,
        out_shape=jax.ShapeDtypeStruct((cp_count, shard_rows, 2 * head), jnp.bfloat16),
        in_specs=[vmem],
        out_specs=vmem,
        scratch_shapes=[pltpu.VMEM((2 * shard_rows, head), jnp.float32)],
        compiler_params=limits,
    )(cache_raw)
    shards = lax.all_to_all(spread, "cp", split_axis=0, concat_axis=0)
    raw_behind = lax.ppermute(new_raw, "cp", [(i, (i + 1) % cp_count) for i in range(cp_count)])
    own, table, pick = pl.pallas_call(
        functools.partial(prepare_kernel, turns=turns, period=period, count=blk_count),
        out_shape=[
            jax.ShapeDtypeStruct((tok, 2 * head), jnp.bfloat16),
            jax.ShapeDtypeStruct((table_places(blk_count)[2] + shard_count,), jnp.int32),
            jax.ShapeDtypeStruct((1,), jnp.int32),
        ],
        in_specs=[smem] * 2 + [vmem] * 3,
        out_specs=[vmem, smem, smem],
        scratch_shapes=[pltpu.VMEM((2 * tok, head), jnp.float32)],
        compiler_params=limits,
    )(place, cache_len, new_raw, new_doc.reshape(-1, tok), cache_doc.reshape(-1, 128))

    def exchange(rounds):
        def run(shards, own, raw_behind, table, queries):
            rows = rounds * shard_rows + tok
            packed, behind = pl.pallas_call(
                functools.partial(pack_kernel, rounds=rounds),
                out_shape=[
                    jax.ShapeDtypeStruct((blk_count, rows, 2 * head), jnp.bfloat16),
                    jax.ShapeDtypeStruct((tok, 2 * head), jnp.bfloat16),
                ],
                in_specs=[smem, vmem, vmem, vmem],
                out_specs=[vmem, vmem],
                scratch_shapes=[pltpu.VMEM((2 * tok, head), jnp.float32)],
                compiler_params=limits,
            )(table, shards, own, raw_behind)
            arrived = lax.all_to_all(packed, "blk", split_axis=0, concat_axis=0)
            span = pieces * shard_rows
            tiles = rounds * blk_count // pieces
            return pl.pallas_call(
                functools.partial(
                    attention_kernel, shard_rows=shard_rows, rounds=rounds, shards=shard_count
                ),
                out_shape=jax.ShapeDtypeStruct((tok, width), jnp.bfloat16),
                in_specs=[smem, vmem, vmem, vmem],
                out_specs=vmem,
                scratch_shapes=[
                    pltpu.VMEM((blk_count // 2, heads, tok, 2 * tok), jnp.float32),
                    pltpu.VMEM((1, heads, tok, tok), jnp.float32),
                    pltpu.VMEM((tiles, heads, tok, span), jnp.float32),
                    pltpu.VMEM((heads, tok, head), jnp.float32),
                    pltpu.VMEM((heads, tok, head), jnp.float32),
                    pltpu.VMEM((heads, tok, head), jnp.float32),
                ],
                compiler_params=limits,
            )(table, queries, arrived, behind)

        return run

    attended = lax.switch(
        pick[0],
        [exchange(turn) for turn in turns],
        shards,
        own,
        raw_behind,
        table,
        queries[:, 0],
    )
    share = tok // head_count
    moved = lax.all_to_all(
        attended.reshape(head_count, share, width), "head", split_axis=0, concat_axis=0
    )
    return jnp.transpose(moved, (1, 0, 2))


def solution(mesh):
    placed = (
        P(("cp", "blk"), "head", None),
        P(("cp", "blk"), "head", None, None),
        P(("cp", "blk"), "head", None, None),
        P(),
        P(),
        P(),
    )
    return jax.shard_map(
        local,
        mesh=mesh,
        in_specs=placed,
        out_specs=P(("cp", "blk", "head"), None, None),
        check_vma=False,
    )
```

```python
import functools
import math

import jax
import jax.numpy as jnp
from jax import lax
from jax.experimental import pallas as pl
from jax.experimental.pallas import tpu as pltpu
from jax.sharding import PartitionSpec as P

negative = -1e30
documents = 16
block_at, new_low_at, cache_low_at, cache_high_at, target_low_at = 0, 1, 2, 3, 4
longest = 1024
head = 128
pieces = 4
smem = pl.BlockSpec(memory_space=pltpu.SMEM)
vmem = pl.BlockSpec(memory_space=pltpu.VMEM)
exponent_scale = math.log2(math.e) * head**-0.5
limits = pltpu.CompilerParams(vmem_limit_bytes=44 * 1024 * 1024)


def split_pairs(raw, wide, rows):
    wide[: 2 * rows, :] = raw.astype(jnp.float32)
    keys = wide[pl.ds(0, rows, 2), :]
    values = wide[pl.ds(1, rows, 2), :]
    return jnp.concatenate([keys, values], axis=1).astype(jnp.bfloat16)


def spread_kernel(cache_ref, spread_ref, wide):
    shard = split_pairs(cache_ref[...], wide, spread_ref.shape[1])
    for target in range(spread_ref.shape[0]):
        spread_ref[target] = shard


def table_places(count):
    new_starts = target_low_at + count
    cache_starts = new_starts + documents + 1
    return new_starts, cache_starts, cache_starts + documents + 1


def prepare_kernel(
    place_ref,
    cache_len_ref,
    new_ref,
    new_doc_ref,
    cache_doc_ref,
    own_ref,
    table_ref,
    pick_ref,
    wide,
    *,
    turns,
    period,
    count,
):
    tok = own_ref.shape[0]
    new_starts, cache_starts, lengths = table_places(count)
    own_ref[...] = split_pairs(new_ref[...], wide, tok)
    new_doc = new_doc_ref[...]
    cache_doc = cache_doc_ref[...]
    first_doc = new_doc[:, :1]
    last_doc = new_doc[:, -1:]
    low = jnp.zeros(first_doc.shape, jnp.float32)
    high = jnp.full(first_doc.shape, float(cache_doc.size), jnp.float32)
    new_at = [jnp.int32(0)]
    cache_at = [jnp.int32(0)]
    for doc in range(1, documents):
        before = jnp.sum((new_doc < doc).astype(jnp.float32))
        new_at.append(before.astype(jnp.int32))
        before = jnp.sum((cache_doc < doc).astype(jnp.float32))
        cache_at.append(before.astype(jnp.int32))
        low = jnp.where(first_doc == doc, before, low)
        high = jnp.where(last_doc == doc - 1, before, high)
    new_at.append(jnp.int32(new_doc.size))
    cache_at.append(jnp.int32(cache_doc.size))
    for doc in range(documents + 1):
        table_ref[new_starts + doc] = new_at[doc]
        table_ref[cache_starts + doc] = cache_at[doc]
    for shard in range(cache_len_ref.shape[0]):
        table_ref[lengths + shard] = cache_len_ref[shard]

    def cache_start(place):
        found = jnp.int32(0)
        for doc in range(1, documents):
            found = jnp.where(place >= new_at[doc], cache_at[doc], found)
        return found

    block = place_ref[0]
    first = block * tok
    group_first = block // count * count * tok
    new_low = jnp.int32(0)
    cache_high = cache_at[1]
    for doc in range(1, documents):
        new_low = jnp.where(first >= new_at[doc], new_at[doc], new_low)
        cache_high = jnp.where(first + tok - 1 >= new_at[doc], cache_at[doc + 1], cache_high)
    table_ref[block_at] = block
    table_ref[new_low_at] = new_low
    table_ref[cache_low_at] = cache_start(first)
    table_ref[cache_high_at] = cache_high
    for target in range(count):
        table_ref[target_low_at + target] = cache_start(group_first + target * tok)
    widest = jnp.max(high - low).astype(jnp.int32)
    pick = jnp.int32(0)
    for turn in turns[:-1]:
        pick += (widest > turn * period).astype(jnp.int32)
    pick_ref[0] = pick


def pack_kernel(
    table_ref, shards_ref, own_ref, raw_ref, out_ref, behind_ref, wide, *, rounds
):
    groups, shard_rows, _ = shards_ref.shape
    count = out_ref.shape[0]
    tok = own_ref.shape[0]
    period = count * shard_rows
    blk_index = table_ref[block_at] % count
    behind_ref[...] = split_pairs(raw_ref[...], wide, tok)
    row = lax.broadcasted_iota(jnp.int32, (shard_rows, 1), 0)
    for target in range(count):
        low = table_ref[target_low_at + target]
        reached = low - blk_index * shard_rows
        group = (reached - (shard_rows - 1) + period - 1) // period
        cut = reached - group * period
        for turn in range(rounds):
            here = jnp.minimum(group + turn, groups - 1)
            after = jnp.minimum(group + turn + 1, groups - 1)
            chosen = jnp.where(
                row >= cut,
                shards_ref[here].astype(jnp.float32),
                shards_ref[after].astype(jnp.float32),
            )
            out_ref[target, turn * shard_rows : (turn + 1) * shard_rows] = chosen.astype(
                jnp.bfloat16
            )

        @pl.when(blk_index <= target)
        def _():
            out_ref[target, rounds * shard_rows :] = own_ref[...]

        @pl.when(blk_index > target)
        def _():
            out_ref[target, rounds * shard_rows :] = behind_ref[...]


def row_bounds(table_ref, count, first, tok):
    new_starts, cache_starts, _ = table_places(count)
    row_place = first + lax.broadcasted_iota(jnp.int32, (tok, 1), 0)
    row_start = jnp.zeros((tok, 1), jnp.int32)
    row_low = jnp.zeros((tok, 1), jnp.int32)
    row_high = jnp.full((tok, 1), table_ref[cache_starts + 1], jnp.int32)
    for doc in range(1, documents):
        start = table_ref[new_starts + doc]
        reached = row_place >= start
        row_start = jnp.where(reached, start, row_start)
        row_low = jnp.where(reached, table_ref[cache_starts + doc], row_low)
        row_high = jnp.where(reached, table_ref[cache_starts + doc + 1], row_high)
    return row_place, row_start, row_low, row_high


def score(rows_ref, keys, allowed, scores_ref, at, lane_max):
    tok = allowed.shape[0]
    products = lax.dot_general(
        rows_ref[...], keys, (((1,), (1,)), ((), ())), preferred_element_type=jnp.float32
    )
    for first in range(0, rows_ref.shape[0], tok):
        rows = slice(first, first + tok)
        scores = jnp.where(allowed, products[rows], negative)
        scores_ref[at, rows] = scores
        best = lane_max[rows]
        for lane in range(0, scores.shape[1], head):
            best = jnp.maximum(best, scores[:, lane : lane + head])
        lane_max[rows] = best


def weigh(values, scores_ref, at, lane_max, lane_sum, total, tok):
    rounded = []
    for first in range(0, total.shape[0], tok):
        rows = slice(first, first + tok)
        scores = scores_ref[at, rows]
        best = lane_max[rows]
        added = lane_sum[rows]
        parts = []
        for lane in range(0, scores.shape[1], head):
            weight = jnp.exp2((scores[:, lane : lane + head] - best) * exponent_scale)
            added = added + weight
            parts.append(weight.astype(jnp.bfloat16))
        lane_sum[rows] = added
        rounded.append(parts[0] if len(parts) == 1 else jnp.concatenate(parts, axis=1))
    total[...] += jnp.dot(
        jnp.concatenate(rounded, axis=0), values, preferred_element_type=jnp.float32
    )


def settle(lane_max):
    best = jnp.max(lane_max[...], axis=1, keepdims=True)
    lane_max[...] = jnp.broadcast_to(best, lane_max.shape)


def attention_kernel(
    table_ref,
    queries_ref,
    arrived_ref,
    behind_ref,
    out_ref,
    query_rows,
    new_scores,
    far_scores,
    cache_scores,
    lane_max,
    lane_sum,
    total,
    *,
    shard_rows,
    rounds,
    shards,
):
    tok = queries_ref.shape[0]
    heads = query_rows.shape[0] // tok
    count = arrived_ref.shape[0]
    lengths = table_places(count)[2]
    period = count * shard_rows
    span = pieces * shard_rows
    new_offset = rounds * shard_rows
    block = table_ref[block_at]
    cache_low = table_ref[cache_low_at]
    cache_high = table_ref[cache_high_at]
    row_place, row_start, row_low, row_high = row_bounds(table_ref, count, block * tok, tok)
    for h in range(heads):
        query_rows[h * tok : (h + 1) * tok] = queries_ref[:, h * head : (h + 1) * head]
    lane_max[...] = jnp.full(lane_max.shape, negative, jnp.float32)
    lane_sum[...] = jnp.zeros(lane_sum.shape, jnp.float32)
    total[...] = jnp.zeros(total.shape, jnp.float32)
    farthest = block - count
    first_block = table_ref[new_low_at] // tok
    new_tiles = jnp.minimum((block - first_block) // 2 + 1, count // 2)
    reaches = first_block <= farthest

    def new_part(number, first_lane):
        lanes = slice(first_lane, first_lane + head)
        return jnp.concatenate(
            [
                arrived_ref[lax.rem(block - 2 * number - back + count, count), new_offset:, lanes]
                for back in (1, 0)
            ],
            axis=0,
        )

    def new_allowed(place, lanes):
        key_place = place + lax.broadcasted_iota(jnp.int32, (1, lanes), 1)
        return (key_place >= row_start) & (key_place <= row_place)

    @pl.loop(0, new_tiles)
    def _(number):
        allowed = new_allowed((block - 2 * number - 1) * tok, 2 * tok)
        score(query_rows, new_part(number, 0), allowed, new_scores, number, lane_max)

    @pl.when(reaches)
    def _():
        allowed = new_allowed(farthest * tok, tok)
        score(query_rows, behind_ref[:, :head], allowed, far_scores, 0, lane_max)

    def cache_tile(number):
        turn = number // (count // pieces)
        source = number % (count // pieces) * pieces
        base = cache_low + turn * period
        begin = base + jnp.bitwise_and(source * shard_rows - base, period - 1)
        holds = jnp.bitwise_and(base - source * shard_rows, period - 1) < span
        return turn, source, base, (begin < cache_high) | (holds & (base < cache_high))

    def cache_part(turn, source, first_lane):
        offset = pl.multiple_of(turn * shard_rows, shard_rows)
        return jnp.concatenate(
            [
                arrived_ref[source + part, pl.ds(offset, shard_rows), first_lane : first_lane + head]
                for part in range(pieces)
            ],
            axis=0,
        )

    tiles = rounds * count // pieces

    @pl.loop(0, tiles)
    def _(number):
        turn, source, base, needed = cache_tile(number)

        @pl.when(needed)
        def _():
            lane = lax.broadcasted_iota(jnp.int32, (1, span), 1)
            place = base + jnp.bitwise_and(source * shard_rows + lane - base, period - 1)
            shard = place // shard_rows
            filled = jnp.zeros((1, span), jnp.int32)
            for part in range(pieces):
                edge = (source + part) * shard_rows
                for at in (0, shard_rows - 1):
                    where = base + jnp.bitwise_and(edge + at - base, period - 1)
                    where = where // shard_rows
                    length = table_ref[lengths + jnp.minimum(where, shards - 1)]
                    filled = jnp.where(shard == where, length, filled)
            usable = jnp.bitwise_and(place, shard_rows - 1) < filled
            allowed = (place >= row_low) & (place < row_high) & usable
            keys = cache_part(turn, source, 0)
            score(query_rows, keys, allowed, cache_scores, number, lane_max)

    settle(lane_max)

    @pl.loop(0, new_tiles)
    def _(number):
        weigh(new_part(number, head), new_scores, number, lane_max, lane_sum, total, tok)

    @pl.when(reaches)
    def _():
        weigh(behind_ref[:, head:], far_scores, 0, lane_max, lane_sum, total, tok)

    @pl.loop(0, tiles)
    def _(number):
        turn, source, base, needed = cache_tile(number)

        @pl.when(needed)
        def _():
            values = cache_part(turn, source, head)
            weigh(values, cache_scores, number, lane_max, lane_sum, total, tok)

    for h in range(heads):
        rows = slice(h * tok, (h + 1) * tok)
        row_total = jnp.sum(lane_sum[rows], axis=1, keepdims=True)
        out_ref[:, h * head : (h + 1) * head] = (total[rows] / row_total).astype(jnp.bfloat16)


def local(queries, new_kv, cached_key_value, new_doc, cache_doc, cache_len):
    tok = queries.shape[0]
    width = queries.shape[-1]
    heads = width // head
    shard_rows = cached_key_value.shape[0]
    blk_count = lax.axis_size("blk")
    cp_count = lax.axis_size("cp")
    head_count = lax.axis_size("head")
    assert tok * blk_count >= longest
    shard_count = cache_len.shape[0]
    place = lax.axis_index(("cp", "blk")).astype(jnp.int32)[None]
    period = blk_count * shard_rows
    turns = [2, 3, cp_count]
    new_raw = new_kv.reshape(2 * tok, head)
    cache_raw = cached_key_value.reshape(2 * shard_rows, head)
    spread = pl.pallas_call(
        spread_kernel,
        out_shape=jax.ShapeDtypeStruct((cp_count, shard_rows, 2 * head), jnp.bfloat16),
        in_specs=[vmem],
        out_specs=vmem,
        scratch_shapes=[pltpu.VMEM((2 * shard_rows, head), jnp.float32)],
        compiler_params=limits,
    )(cache_raw)
    shards = lax.all_to_all(spread, "cp", split_axis=0, concat_axis=0)
    raw_behind = lax.ppermute(new_raw, "cp", [(i, (i + 1) % cp_count) for i in range(cp_count)])
    own, table, pick = pl.pallas_call(
        functools.partial(prepare_kernel, turns=turns, period=period, count=blk_count),
        out_shape=[
            jax.ShapeDtypeStruct((tok, 2 * head), jnp.bfloat16),
            jax.ShapeDtypeStruct((table_places(blk_count)[2] + shard_count,), jnp.int32),
            jax.ShapeDtypeStruct((1,), jnp.int32),
        ],
        in_specs=[smem] * 2 + [vmem] * 3,
        out_specs=[vmem, smem, smem],
        scratch_shapes=[pltpu.VMEM((2 * tok, head), jnp.float32)],
        compiler_params=limits,
    )(place, cache_len, new_raw, new_doc.reshape(-1, tok), cache_doc.reshape(-1, 128))

    def exchange(rounds):
        def run(shards, own, raw_behind, table, queries):
            rows = rounds * shard_rows + tok
            packed, behind = pl.pallas_call(
                functools.partial(pack_kernel, rounds=rounds),
                out_shape=[
                    jax.ShapeDtypeStruct((blk_count, rows, 2 * head), jnp.bfloat16),
                    jax.ShapeDtypeStruct((tok, 2 * head), jnp.bfloat16),
                ],
                in_specs=[smem, vmem, vmem, vmem],
                out_specs=[vmem, vmem],
                scratch_shapes=[pltpu.VMEM((2 * tok, head), jnp.float32)],
                compiler_params=limits,
            )(table, shards, own, raw_behind)
            arrived = lax.all_to_all(packed, "blk", split_axis=0, concat_axis=0)
            span = pieces * shard_rows
            tiles = rounds * blk_count // pieces
            return pl.pallas_call(
                functools.partial(
                    attention_kernel, shard_rows=shard_rows, rounds=rounds, shards=shard_count
                ),
                out_shape=jax.ShapeDtypeStruct((tok, width), jnp.bfloat16),
                in_specs=[smem, vmem, vmem, vmem],
                out_specs=vmem,
                scratch_shapes=[
                    pltpu.VMEM((heads * tok, head), jnp.bfloat16),
                    pltpu.VMEM((blk_count // 2, heads * tok, 2 * tok), jnp.float32),
                    pltpu.VMEM((1, heads * tok, tok), jnp.float32),
                    pltpu.VMEM((tiles, heads * tok, span), jnp.float32),
                    pltpu.VMEM((heads * tok, head), jnp.float32),
                    pltpu.VMEM((heads * tok, head), jnp.float32),
                    pltpu.VMEM((heads * tok, head), jnp.float32),
                ],
                compiler_params=limits,
            )(table, queries, arrived, behind)

        return run

    attended = lax.switch(
        pick[0],
        [exchange(turn) for turn in turns],
        shards,
        own,
        raw_behind,
        table,
        queries[:, 0],
    )
    share = tok // head_count
    moved = lax.all_to_all(
        attended.reshape(head_count, share, width), "head", split_axis=0, concat_axis=0
    )
    return jnp.transpose(moved, (1, 0, 2))


def solution(mesh):
    placed = (
        P(("cp", "blk"), "head", None),
        P(("cp", "blk"), "head", None, None),
        P(("cp", "blk"), "head", None, None),
        P(),
        P(),
        P(),
    )
    return jax.shard_map(
        local,
        mesh=mesh,
        in_specs=placed,
        out_specs=P(("cp", "blk", "head"), None, None),
        check_vma=False,
    )
```

```python
import functools
import math

import jax
import jax.numpy as jnp
from jax import lax
from jax.experimental import pallas as pl
from jax.experimental.pallas import tpu as pltpu
from jax.sharding import PartitionSpec as P

negative = -1e30
documents = 16
block_at, new_low_at, cache_low_at, cache_high_at, target_low_at = 0, 1, 2, 3, 4
longest = 1024
head = 128
pieces = 4
smem = pl.BlockSpec(memory_space=pltpu.SMEM)
vmem = pl.BlockSpec(memory_space=pltpu.VMEM)
exponent_scale = math.log2(math.e) * head**-0.5
limits = pltpu.CompilerParams(vmem_limit_bytes=44 * 1024 * 1024)


def split_pairs(raw, wide, rows):
    wide[: 2 * rows, :] = raw.astype(jnp.float32)
    keys = wide[pl.ds(0, rows, 2), :]
    values = wide[pl.ds(1, rows, 2), :]
    return jnp.concatenate([keys, values], axis=1).astype(jnp.bfloat16)


def spread_kernel(cache_ref, spread_ref, wide):
    shard = split_pairs(cache_ref[...], wide, spread_ref.shape[1])
    for target in range(spread_ref.shape[0]):
        spread_ref[target] = shard


def table_places(count):
    new_starts = target_low_at + count
    cache_starts = new_starts + documents + 1
    return new_starts, cache_starts, cache_starts + documents + 1


def prepare_kernel(
    place_ref,
    cache_len_ref,
    new_ref,
    new_doc_ref,
    cache_doc_ref,
    own_ref,
    table_ref,
    pick_ref,
    wide,
    *,
    turns,
    period,
    count,
):
    tok = own_ref.shape[0]
    new_starts, cache_starts, lengths = table_places(count)
    own_ref[...] = split_pairs(new_ref[...], wide, tok)
    new_doc = new_doc_ref[...]
    cache_doc = cache_doc_ref[...]
    first_doc = new_doc[:, :1]
    last_doc = new_doc[:, -1:]
    low = jnp.zeros(first_doc.shape, jnp.float32)
    high = jnp.full(first_doc.shape, float(cache_doc.size), jnp.float32)
    new_at = [jnp.int32(0)]
    cache_at = [jnp.int32(0)]
    for doc in range(1, documents):
        before = jnp.sum((new_doc < doc).astype(jnp.float32))
        new_at.append(before.astype(jnp.int32))
        before = jnp.sum((cache_doc < doc).astype(jnp.float32))
        cache_at.append(before.astype(jnp.int32))
        low = jnp.where(first_doc == doc, before, low)
        high = jnp.where(last_doc == doc - 1, before, high)
    new_at.append(jnp.int32(new_doc.size))
    cache_at.append(jnp.int32(cache_doc.size))
    for doc in range(documents + 1):
        table_ref[new_starts + doc] = new_at[doc]
        table_ref[cache_starts + doc] = cache_at[doc]
    for shard in range(cache_len_ref.shape[0]):
        table_ref[lengths + shard] = cache_len_ref[shard]

    def cache_start(place):
        found = jnp.int32(0)
        for doc in range(1, documents):
            found = jnp.where(place >= new_at[doc], cache_at[doc], found)
        return found

    block = place_ref[0]
    first = block * tok
    group_first = block // count * count * tok
    new_low = jnp.int32(0)
    cache_high = cache_at[1]
    for doc in range(1, documents):
        new_low = jnp.where(first >= new_at[doc], new_at[doc], new_low)
        cache_high = jnp.where(first + tok - 1 >= new_at[doc], cache_at[doc + 1], cache_high)
    table_ref[block_at] = block
    table_ref[new_low_at] = new_low
    table_ref[cache_low_at] = cache_start(first)
    table_ref[cache_high_at] = cache_high
    for target in range(count):
        table_ref[target_low_at + target] = cache_start(group_first + target * tok)
    widest = jnp.max(high - low).astype(jnp.int32)
    pick = jnp.int32(0)
    for turn in turns[:-1]:
        pick += (widest > turn * period).astype(jnp.int32)
    pick_ref[0] = pick


def pack_kernel(
    table_ref, shards_ref, own_ref, raw_ref, out_ref, behind_ref, wide, *, rounds
):
    groups, shard_rows, _ = shards_ref.shape
    count = out_ref.shape[0]
    tok = own_ref.shape[0]
    period = count * shard_rows
    blk_index = table_ref[block_at] % count
    behind_ref[...] = split_pairs(raw_ref[...], wide, tok)
    row = lax.broadcasted_iota(jnp.int32, (shard_rows, 1), 0)
    for target in range(count):
        low = table_ref[target_low_at + target]
        reached = low - blk_index * shard_rows
        group = (reached - (shard_rows - 1) + period - 1) // period
        cut = reached - group * period
        for turn in range(rounds):
            here = jnp.minimum(group + turn, groups - 1)
            after = jnp.minimum(group + turn + 1, groups - 1)
            chosen = jnp.where(
                row >= cut,
                shards_ref[here].astype(jnp.float32),
                shards_ref[after].astype(jnp.float32),
            )
            out_ref[target, turn * shard_rows : (turn + 1) * shard_rows] = chosen.astype(
                jnp.bfloat16
            )

        @pl.when(blk_index <= target)
        def _():
            out_ref[target, rounds * shard_rows :] = own_ref[...]

        @pl.when(blk_index > target)
        def _():
            out_ref[target, rounds * shard_rows :] = behind_ref[...]


def row_bounds(table_ref, count, first, tok):
    new_starts, cache_starts, _ = table_places(count)
    row_place = first + lax.broadcasted_iota(jnp.int32, (tok, 1), 0)
    row_start = jnp.zeros((tok, 1), jnp.int32)
    row_low = jnp.zeros((tok, 1), jnp.int32)
    row_high = jnp.full((tok, 1), table_ref[cache_starts + 1], jnp.int32)
    for doc in range(1, documents):
        start = table_ref[new_starts + doc]
        reached = row_place >= start
        row_start = jnp.where(reached, start, row_start)
        row_low = jnp.where(reached, table_ref[cache_starts + doc], row_low)
        row_high = jnp.where(reached, table_ref[cache_starts + doc + 1], row_high)
    return row_place, row_start, row_low, row_high


def score(queries_ref, keys, allowed, scores_ref, at, lane_max):
    turned = keys.T
    shift = jnp.where(allowed, 0.0, negative)
    for h in range(lane_max.shape[0]):
        scores = jnp.dot(
            queries_ref[:, h * head : (h + 1) * head], turned, preferred_element_type=jnp.float32
        )
        scores = scores + shift
        scores_ref[at, h] = scores
        best = scores[:, :head]
        for part in range(1, scores.shape[1] // head):
            best = jnp.maximum(best, scores[:, part * head : (part + 1) * head])
        lane_max[h] = jnp.maximum(lane_max[h], best)


def weigh(values, scores_ref, at, lane_max, lane_sum, total):
    for h in range(lane_max.shape[0]):
        scores = scores_ref[at, h]
        best = lane_max[h]
        added = lane_sum[h]
        parts = []
        for part in range(scores.shape[1] // head):
            piece = scores[:, part * head : (part + 1) * head]
            weight = jnp.exp2((piece - best) * exponent_scale)
            added = added + weight
            parts.append(weight.astype(jnp.bfloat16))
        lane_sum[h] = added
        rounded = parts[0] if len(parts) == 1 else jnp.concatenate(parts, axis=1)
        total[h] += jnp.dot(rounded, values, preferred_element_type=jnp.float32)


def settle(lane_max):
    for h in range(lane_max.shape[0]):
        best = jnp.max(lane_max[h], axis=1, keepdims=True)
        lane_max[h] = jnp.broadcast_to(best, lane_max.shape[1:])


def attention_kernel(
    table_ref,
    queries_ref,
    arrived_ref,
    behind_ref,
    out_ref,
    new_scores,
    far_scores,
    cache_scores,
    lane_max,
    lane_sum,
    total,
    *,
    shard_rows,
    rounds,
    shards,
):
    tok = queries_ref.shape[0]
    heads = lane_max.shape[0]
    count = arrived_ref.shape[0]
    lengths = table_places(count)[2]
    period = count * shard_rows
    span = pieces * shard_rows
    new_offset = rounds * shard_rows
    block = table_ref[block_at]
    cache_low = table_ref[cache_low_at]
    cache_high = table_ref[cache_high_at]
    row_place, row_start, row_low, row_high = row_bounds(table_ref, count, block * tok, tok)
    lane_max[...] = jnp.full(lane_max.shape, negative, jnp.float32)
    lane_sum[...] = jnp.zeros(lane_sum.shape, jnp.float32)
    total[...] = jnp.zeros(total.shape, jnp.float32)
    farthest = block - count
    first_block = table_ref[new_low_at] // tok
    new_tiles = jnp.minimum((block - first_block) // 2 + 1, count // 2)
    reaches = first_block <= farthest

    def new_part(number, first_lane):
        lanes = slice(first_lane, first_lane + head)
        return jnp.concatenate(
            [
                arrived_ref[lax.rem(block - 2 * number - back + count, count), new_offset:, lanes]
                for back in (1, 0)
            ],
            axis=0,
        )

    def new_allowed(place, lanes):
        key_place = place + lax.broadcasted_iota(jnp.int32, (1, lanes), 1)
        return (key_place >= row_start) & (key_place <= row_place)

    @pl.loop(0, new_tiles)
    def _(number):
        allowed = new_allowed((block - 2 * number - 1) * tok, 2 * tok)
        score(queries_ref, new_part(number, 0), allowed, new_scores, number, lane_max)

    @pl.when(reaches)
    def _():
        allowed = new_allowed(farthest * tok, tok)
        score(queries_ref, behind_ref[:, :head], allowed, far_scores, 0, lane_max)

    def cache_tile(number):
        turn = number // (count // pieces)
        source = number % (count // pieces) * pieces
        base = cache_low + turn * period
        begin = base + jnp.bitwise_and(source * shard_rows - base, period - 1)
        holds = jnp.bitwise_and(base - source * shard_rows, period - 1) < span
        return turn, source, base, (begin < cache_high) | (holds & (base < cache_high))

    def cache_part(turn, source, first_lane):
        offset = pl.multiple_of(turn * shard_rows, shard_rows)
        return jnp.concatenate(
            [
                arrived_ref[source + part, pl.ds(offset, shard_rows), first_lane : first_lane + head]
                for part in range(pieces)
            ],
            axis=0,
        )

    tiles = rounds * count // pieces

    @pl.loop(0, tiles)
    def _(number):
        turn, source, base, needed = cache_tile(number)

        @pl.when(needed)
        def _():
            lane = lax.broadcasted_iota(jnp.int32, (1, span), 1)
            place = base + jnp.bitwise_and(source * shard_rows + lane - base, period - 1)
            shard = place // shard_rows
            filled = jnp.zeros((1, span), jnp.int32)
            for part in range(pieces):
                edge = (source + part) * shard_rows
                for at in (0, shard_rows - 1):
                    where = base + jnp.bitwise_and(edge + at - base, period - 1)
                    where = where // shard_rows
                    length = table_ref[lengths + jnp.minimum(where, shards - 1)]
                    filled = jnp.where(shard == where, length, filled)
            usable = jnp.bitwise_and(place, shard_rows - 1) < filled
            allowed = (place >= row_low) & (place < row_high) & usable
            keys = cache_part(turn, source, 0)
            score(queries_ref, keys, allowed, cache_scores, number, lane_max)

    settle(lane_max)

    @pl.loop(0, new_tiles)
    def _(number):
        weigh(new_part(number, head), new_scores, number, lane_max, lane_sum, total)

    @pl.when(reaches)
    def _():
        weigh(behind_ref[:, head:], far_scores, 0, lane_max, lane_sum, total)

    @pl.loop(0, tiles)
    def _(number):
        turn, source, base, needed = cache_tile(number)

        @pl.when(needed)
        def _():
            values = cache_part(turn, source, head)
            weigh(values, cache_scores, number, lane_max, lane_sum, total)

    for h in range(heads):
        row_total = jnp.sum(lane_sum[h], axis=1, keepdims=True)
        out_ref[:, h * head : (h + 1) * head] = (total[h] / row_total).astype(jnp.bfloat16)


def local(queries, new_kv, cached_key_value, new_doc, cache_doc, cache_len):
    tok = queries.shape[0]
    width = queries.shape[-1]
    heads = width // head
    shard_rows = cached_key_value.shape[0]
    blk_count = lax.axis_size("blk")
    cp_count = lax.axis_size("cp")
    head_count = lax.axis_size("head")
    assert tok * blk_count >= longest
    shard_count = cache_len.shape[0]
    place = lax.axis_index(("cp", "blk")).astype(jnp.int32)[None]
    period = blk_count * shard_rows
    turns = [2, 3, cp_count]
    new_raw = new_kv.reshape(2 * tok, head)
    cache_raw = cached_key_value.reshape(2 * shard_rows, head)
    spread = pl.pallas_call(
        spread_kernel,
        out_shape=jax.ShapeDtypeStruct((cp_count, shard_rows, 2 * head), jnp.bfloat16),
        in_specs=[vmem],
        out_specs=vmem,
        scratch_shapes=[pltpu.VMEM((2 * shard_rows, head), jnp.float32)],
        compiler_params=limits,
    )(cache_raw)
    shards = lax.all_to_all(spread, "cp", split_axis=0, concat_axis=0)
    raw_behind = lax.ppermute(new_raw, "cp", [(i, (i + 1) % cp_count) for i in range(cp_count)])
    own, table, pick = pl.pallas_call(
        functools.partial(prepare_kernel, turns=turns, period=period, count=blk_count),
        out_shape=[
            jax.ShapeDtypeStruct((tok, 2 * head), jnp.bfloat16),
            jax.ShapeDtypeStruct((table_places(blk_count)[2] + shard_count,), jnp.int32),
            jax.ShapeDtypeStruct((1,), jnp.int32),
        ],
        in_specs=[smem] * 2 + [vmem] * 3,
        out_specs=[vmem, smem, smem],
        scratch_shapes=[pltpu.VMEM((2 * tok, head), jnp.float32)],
        compiler_params=limits,
    )(place, cache_len, new_raw, new_doc.reshape(-1, tok), cache_doc.reshape(-1, 128))

    def exchange(rounds):
        def run(shards, own, raw_behind, table, queries):
            rows = rounds * shard_rows + tok
            packed, behind = pl.pallas_call(
                functools.partial(pack_kernel, rounds=rounds),
                out_shape=[
                    jax.ShapeDtypeStruct((blk_count, rows, 2 * head), jnp.bfloat16),
                    jax.ShapeDtypeStruct((tok, 2 * head), jnp.bfloat16),
                ],
                in_specs=[smem, vmem, vmem, vmem],
                out_specs=[vmem, vmem],
                scratch_shapes=[pltpu.VMEM((2 * tok, head), jnp.float32)],
                compiler_params=limits,
            )(table, shards, own, raw_behind)
            arrived = lax.all_to_all(packed, "blk", split_axis=0, concat_axis=0)
            span = pieces * shard_rows
            tiles = rounds * blk_count // pieces
            return pl.pallas_call(
                functools.partial(
                    attention_kernel, shard_rows=shard_rows, rounds=rounds, shards=shard_count
                ),
                out_shape=jax.ShapeDtypeStruct((tok, width), jnp.bfloat16),
                in_specs=[smem, vmem, vmem, vmem],
                out_specs=vmem,
                scratch_shapes=[
                    pltpu.VMEM((blk_count // 2, heads, tok, 2 * tok), jnp.float32),
                    pltpu.VMEM((1, heads, tok, tok), jnp.float32),
                    pltpu.VMEM((tiles, heads, tok, span), jnp.float32),
                    pltpu.VMEM((heads, tok, head), jnp.float32),
                    pltpu.VMEM((heads, tok, head), jnp.float32),
                    pltpu.VMEM((heads, tok, head), jnp.float32),
                ],
                compiler_params=limits,
            )(table, queries, arrived, behind)

        return run

    attended = lax.switch(
        pick[0],
        [exchange(turn) for turn in turns],
        shards,
        own,
        raw_behind,
        table,
        queries[:, 0],
    )
    share = tok // head_count
    moved = lax.all_to_all(
        attended.reshape(head_count, share, width), "head", split_axis=0, concat_axis=0
    )
    return jnp.transpose(moved, (1, 0, 2))


def solution(mesh):
    placed = (
        P(("cp", "blk"), "head", None),
        P(("cp", "blk"), "head", None, None),
        P(("cp", "blk"), "head", None, None),
        P(),
        P(),
        P(),
    )
    return jax.shard_map(
        local,
        mesh=mesh,
        in_specs=placed,
        out_specs=P(("cp", "blk", "head"), None, None),
        check_vma=False,
    )
```

```python
import functools
import math

import jax
import jax.numpy as jnp
from jax import lax
from jax.experimental import pallas as pl
from jax.experimental.pallas import tpu as pltpu
from jax.sharding import PartitionSpec as P

negative = -1e30
documents = 16
block_at, new_low_at, cache_low_at, cache_high_at, target_low_at = 0, 1, 2, 3, 4
longest = 1024
head = 128
pieces = 4
smem = pl.BlockSpec(memory_space=pltpu.SMEM)
vmem = pl.BlockSpec(memory_space=pltpu.VMEM)
exponent_scale = math.log2(math.e) * head**-0.5
limits = pltpu.CompilerParams(vmem_limit_bytes=44 * 1024 * 1024)


def split_pairs(raw, wide, rows):
    wide[: 2 * rows, :] = raw.astype(jnp.float32)
    keys = wide[pl.ds(0, rows, 2), :]
    values = wide[pl.ds(1, rows, 2), :]
    return jnp.concatenate([keys, values], axis=1).astype(jnp.bfloat16)


def spread_kernel(cache_ref, spread_ref, wide):
    shard = split_pairs(cache_ref[...], wide, spread_ref.shape[1])
    for target in range(spread_ref.shape[0]):
        spread_ref[target] = shard


def table_places(count):
    new_starts = target_low_at + count
    cache_starts = new_starts + documents + 1
    return new_starts, cache_starts, cache_starts + documents + 1


def prepare_kernel(
    place_ref,
    cache_len_ref,
    new_ref,
    new_doc_ref,
    cache_doc_ref,
    queries_ref,
    own_ref,
    turned_ref,
    table_ref,
    pick_ref,
    wide,
    *,
    turns,
    period,
    count,
):
    tok = own_ref.shape[0]
    new_starts, cache_starts, lengths = table_places(count)
    own_ref[...] = split_pairs(new_ref[...], wide, tok)
    for first in range(0, turned_ref.shape[1], head):
        turned_ref[:, first : first + head] = queries_ref[:, first : first + head].T
    new_doc = new_doc_ref[...]
    cache_doc = cache_doc_ref[...]
    first_doc = new_doc[:, :1]
    last_doc = new_doc[:, -1:]
    low = jnp.zeros(first_doc.shape, jnp.float32)
    high = jnp.full(first_doc.shape, float(cache_doc.size), jnp.float32)
    new_at = [jnp.int32(0)]
    cache_at = [jnp.int32(0)]
    for doc in range(1, documents):
        before = jnp.sum((new_doc < doc).astype(jnp.float32))
        new_at.append(before.astype(jnp.int32))
        before = jnp.sum((cache_doc < doc).astype(jnp.float32))
        cache_at.append(before.astype(jnp.int32))
        low = jnp.where(first_doc == doc, before, low)
        high = jnp.where(last_doc == doc - 1, before, high)
    new_at.append(jnp.int32(new_doc.size))
    cache_at.append(jnp.int32(cache_doc.size))
    for doc in range(documents + 1):
        table_ref[new_starts + doc] = new_at[doc]
        table_ref[cache_starts + doc] = cache_at[doc]
    for shard in range(cache_len_ref.shape[0]):
        table_ref[lengths + shard] = cache_len_ref[shard]

    def cache_start(place):
        found = jnp.int32(0)
        for doc in range(1, documents):
            found = jnp.where(place >= new_at[doc], cache_at[doc], found)
        return found

    block = place_ref[0]
    first = block * tok
    group_first = block // count * count * tok
    new_low = jnp.int32(0)
    cache_high = cache_at[1]
    for doc in range(1, documents):
        new_low = jnp.where(first >= new_at[doc], new_at[doc], new_low)
        cache_high = jnp.where(first + tok - 1 >= new_at[doc], cache_at[doc + 1], cache_high)
    table_ref[block_at] = block
    table_ref[new_low_at] = new_low
    table_ref[cache_low_at] = cache_start(first)
    table_ref[cache_high_at] = cache_high
    for target in range(count):
        table_ref[target_low_at + target] = cache_start(group_first + target * tok)
    widest = jnp.max(high - low).astype(jnp.int32)
    pick = jnp.int32(0)
    for turn in turns[:-1]:
        pick += (widest > turn * period).astype(jnp.int32)
    pick_ref[0] = pick


def pack_kernel(
    table_ref, shards_ref, own_ref, raw_ref, out_ref, behind_ref, wide, *, rounds
):
    groups, shard_rows, _ = shards_ref.shape
    count = out_ref.shape[0]
    tok = own_ref.shape[0]
    period = count * shard_rows
    blk_index = table_ref[block_at] % count
    behind_ref[...] = split_pairs(raw_ref[...], wide, tok)
    row = lax.broadcasted_iota(jnp.int32, (shard_rows, 1), 0)
    for target in range(count):
        low = table_ref[target_low_at + target]
        reached = low - blk_index * shard_rows
        group = (reached - (shard_rows - 1) + period - 1) // period
        cut = reached - group * period
        for turn in range(rounds):
            here = jnp.minimum(group + turn, groups - 1)
            after = jnp.minimum(group + turn + 1, groups - 1)
            chosen = jnp.where(
                row >= cut,
                shards_ref[here].astype(jnp.float32),
                shards_ref[after].astype(jnp.float32),
            )
            out_ref[target, turn * shard_rows : (turn + 1) * shard_rows] = chosen.astype(
                jnp.bfloat16
            )

        @pl.when(blk_index <= target)
        def _():
            out_ref[target, rounds * shard_rows :] = own_ref[...]

        @pl.when(blk_index > target)
        def _():
            out_ref[target, rounds * shard_rows :] = behind_ref[...]


def row_bounds(table_ref, count, first, tok):
    new_starts, cache_starts, _ = table_places(count)
    row_place = first + lax.broadcasted_iota(jnp.int32, (1, tok), 1)
    row_start = jnp.zeros((1, tok), jnp.int32)
    row_low = jnp.zeros((1, tok), jnp.int32)
    row_high = jnp.full((1, tok), table_ref[cache_starts + 1], jnp.int32)
    for doc in range(1, documents):
        start = table_ref[new_starts + doc]
        reached = row_place >= start
        row_start = jnp.where(reached, start, row_start)
        row_low = jnp.where(reached, table_ref[cache_starts + doc], row_low)
        row_high = jnp.where(reached, table_ref[cache_starts + doc + 1], row_high)
    return row_place, row_start, row_low, row_high


def attend_tile(turned_ref, keys, values, allowed, best_ref, sum_ref, total):
    turned_values = values.T
    shift = jnp.where(allowed, 0.0, negative)
    wide = 2 * allowed.shape[1]
    shift = jnp.concatenate([shift, shift], axis=1)
    for first in range(0, turned_ref.shape[1], wide):
        rows = slice(first, first + wide)
        scores = jnp.dot(keys, turned_ref[:, rows], preferred_element_type=jnp.float32) + shift
        before = best_ref[:, rows]
        best = jnp.maximum(before, jnp.max(scores, axis=0, keepdims=True))
        weights = jnp.exp2((scores - best) * exponent_scale)
        scale = jnp.exp2((before - best) * exponent_scale)
        best_ref[:, rows] = best
        sum_ref[:, rows] = sum_ref[:, rows] * scale + jnp.sum(weights, axis=0, keepdims=True)
        total[:, rows] = total[:, rows] * scale + jnp.dot(
            turned_values, weights.astype(jnp.bfloat16), preferred_element_type=jnp.float32
        )


def attention_kernel(
    table_ref,
    turned_ref,
    arrived_ref,
    behind_ref,
    out_ref,
    best_ref,
    sum_ref,
    total,
    *,
    shard_rows,
    rounds,
    shards,
):
    tok, width = out_ref.shape
    count = arrived_ref.shape[0]
    lengths = table_places(count)[2]
    period = count * shard_rows
    span = pieces * shard_rows
    new_offset = rounds * shard_rows
    block = table_ref[block_at]
    cache_low = table_ref[cache_low_at]
    cache_high = table_ref[cache_high_at]
    row_place, row_start, row_low, row_high = row_bounds(table_ref, count, block * tok, tok)
    best_ref[...] = jnp.full(best_ref.shape, negative, jnp.float32)
    sum_ref[...] = jnp.zeros(sum_ref.shape, jnp.float32)
    total[...] = jnp.zeros(total.shape, jnp.float32)
    farthest = block - count
    first_block = table_ref[new_low_at] // tok
    new_tiles = jnp.minimum((block - first_block) // 2 + 1, count // 2)

    def attend(keys, values, allowed):
        attend_tile(turned_ref, keys, values, allowed, best_ref, sum_ref, total)

    def new_allowed(place, keys):
        key_place = place + lax.broadcasted_iota(jnp.int32, (keys, tok), 0)
        return (key_place >= row_start) & (key_place <= row_place)

    @pl.loop(0, new_tiles)
    def _(number):
        rows = jnp.concatenate(
            [
                arrived_ref[lax.rem(block - 2 * number - back + count, count), new_offset:]
                for back in (1, 0)
            ],
            axis=0,
        )
        allowed = new_allowed((block - 2 * number - 1) * tok, 2 * tok)
        attend(rows[:, :head], rows[:, head:], allowed)

    @pl.when(first_block <= farthest)
    def _():
        attend(behind_ref[:, :head], behind_ref[:, head:], new_allowed(farthest * tok, tok))

    @pl.loop(0, rounds * count // pieces)
    def _(number):
        turn = number // (count // pieces)
        source = number % (count // pieces) * pieces
        base = cache_low + turn * period
        begin = base + jnp.bitwise_and(source * shard_rows - base, period - 1)
        holds = jnp.bitwise_and(base - source * shard_rows, period - 1) < span

        @pl.when((begin < cache_high) | (holds & (base < cache_high)))
        def _():
            offset = pl.multiple_of(turn * shard_rows, shard_rows)
            rows = jnp.concatenate(
                [arrived_ref[source + part, pl.ds(offset, shard_rows)] for part in range(pieces)],
                axis=0,
            )
            key = lax.broadcasted_iota(jnp.int32, (shard_rows, tok), 0)
            allowed = []
            for part in range(pieces):
                edge = (source + part) * shard_rows - base
                place = base + jnp.bitwise_and(edge + key, period - 1)
                head_shard = (base + jnp.bitwise_and(edge, period - 1)) // shard_rows
                tail_shard = (
                    base + jnp.bitwise_and(edge + shard_rows - 1, period - 1)
                ) // shard_rows
                head_length = table_ref[lengths + jnp.minimum(head_shard, shards - 1)]
                tail_length = table_ref[lengths + jnp.minimum(tail_shard, shards - 1)]
                in_head = place < (head_shard + 1) * shard_rows
                in_head = in_head & (place >= head_shard * shard_rows)
                filled = jnp.where(in_head, head_length, tail_length)
                allowed.append((place >= row_low) & (place < row_high) & (key < filled))
            attend(rows[:, :head], rows[:, head:], jnp.concatenate(allowed, axis=0))

    for first in range(0, width, head):
        rows = slice(first, first + head)
        out_ref[:, rows] = (total[:, rows] / sum_ref[:, rows]).T.astype(jnp.bfloat16)


def local(queries, new_kv, cached_key_value, new_doc, cache_doc, cache_len):
    tok = queries.shape[0]
    width = queries.shape[-1]
    heads = width // head
    shard_rows = cached_key_value.shape[0]
    blk_count = lax.axis_size("blk")
    cp_count = lax.axis_size("cp")
    head_count = lax.axis_size("head")
    assert tok * blk_count >= longest
    shard_count = cache_len.shape[0]
    place = lax.axis_index(("cp", "blk")).astype(jnp.int32)[None]
    period = blk_count * shard_rows
    turns = [2, 3, cp_count]
    new_raw = new_kv.reshape(2 * tok, head)
    cache_raw = cached_key_value.reshape(2 * shard_rows, head)
    spread = pl.pallas_call(
        spread_kernel,
        out_shape=jax.ShapeDtypeStruct((cp_count, shard_rows, 2 * head), jnp.bfloat16),
        in_specs=[vmem],
        out_specs=vmem,
        scratch_shapes=[pltpu.VMEM((2 * shard_rows, head), jnp.float32)],
        compiler_params=limits,
    )(cache_raw)
    shards = lax.all_to_all(spread, "cp", split_axis=0, concat_axis=0)
    raw_behind = lax.ppermute(new_raw, "cp", [(i, (i + 1) % cp_count) for i in range(cp_count)])
    own, turned, table, pick = pl.pallas_call(
        functools.partial(prepare_kernel, turns=turns, period=period, count=blk_count),
        out_shape=[
            jax.ShapeDtypeStruct((tok, 2 * head), jnp.bfloat16),
            jax.ShapeDtypeStruct((head, heads * tok), jnp.bfloat16),
            jax.ShapeDtypeStruct((table_places(blk_count)[2] + shard_count,), jnp.int32),
            jax.ShapeDtypeStruct((1,), jnp.int32),
        ],
        in_specs=[smem] * 2 + [vmem] * 4,
        out_specs=[vmem, vmem, smem, smem],
        scratch_shapes=[pltpu.VMEM((2 * tok, head), jnp.float32)],
        compiler_params=limits,
    )(
        place,
        cache_len,
        new_raw,
        new_doc.reshape(-1, tok),
        cache_doc.reshape(-1, 128),
        queries[:, 0],
    )

    def exchange(rounds):
        def run(shards, own, raw_behind, table, turned):
            rows = rounds * shard_rows + tok
            packed, behind = pl.pallas_call(
                functools.partial(pack_kernel, rounds=rounds),
                out_shape=[
                    jax.ShapeDtypeStruct((blk_count, rows, 2 * head), jnp.bfloat16),
                    jax.ShapeDtypeStruct((tok, 2 * head), jnp.bfloat16),
                ],
                in_specs=[smem, vmem, vmem, vmem],
                out_specs=[vmem, vmem],
                scratch_shapes=[pltpu.VMEM((2 * tok, head), jnp.float32)],
                compiler_params=limits,
            )(table, shards, own, raw_behind)
            arrived = lax.all_to_all(packed, "blk", split_axis=0, concat_axis=0)
            return pl.pallas_call(
                functools.partial(
                    attention_kernel, shard_rows=shard_rows, rounds=rounds, shards=shard_count
                ),
                out_shape=jax.ShapeDtypeStruct((tok, width), jnp.bfloat16),
                in_specs=[smem, vmem, vmem, vmem],
                out_specs=vmem,
                scratch_shapes=[
                    pltpu.VMEM((1, heads * tok), jnp.float32),
                    pltpu.VMEM((1, heads * tok), jnp.float32),
                    pltpu.VMEM((head, heads * tok), jnp.float32),
                ],
                compiler_params=limits,
            )(table, turned, arrived, behind)

        return run

    attended = lax.switch(
        pick[0],
        [exchange(turn) for turn in turns],
        shards,
        own,
        raw_behind,
        table,
        turned,
    )
    share = tok // head_count
    moved = lax.all_to_all(
        attended.reshape(head_count, share, width), "head", split_axis=0, concat_axis=0
    )
    return jnp.transpose(moved, (1, 0, 2))


def solution(mesh):
    placed = (
        P(("cp", "blk"), "head", None),
        P(("cp", "blk"), "head", None, None),
        P(("cp", "blk"), "head", None, None),
        P(),
        P(),
        P(),
    )
    return jax.shard_map(
        local,
        mesh=mesh,
        in_specs=placed,
        out_specs=P(("cp", "blk", "head"), None, None),
        check_vma=False,
    )
```

```python
import functools
import math

import jax
import jax.numpy as jnp
from jax import lax
from jax.experimental import pallas as pl
from jax.experimental.pallas import tpu as pltpu
from jax.sharding import PartitionSpec as P

negative = -1e30
documents = 16
block_at, new_low_at, cache_low_at, cache_high_at, target_low_at = 0, 1, 2, 3, 4
longest = 1024
head = 128
pieces = 8
blocks = 4
smem = pl.BlockSpec(memory_space=pltpu.SMEM)
vmem = pl.BlockSpec(memory_space=pltpu.VMEM)
exponent_scale = math.log2(math.e) * head**-0.5
limits = pltpu.CompilerParams(vmem_limit_bytes=44 * 1024 * 1024)


def split_pairs(raw, wide, rows):
    wide[: 2 * rows, :] = raw.astype(jnp.float32)
    keys = wide[pl.ds(0, rows, 2), :]
    values = wide[pl.ds(1, rows, 2), :]
    return jnp.concatenate([keys, values], axis=1).astype(jnp.bfloat16)


def spread_kernel(cache_ref, spread_ref, wide):
    shard = split_pairs(cache_ref[...], wide, spread_ref.shape[1])
    for target in range(spread_ref.shape[0]):
        spread_ref[target] = shard


def table_places(count):
    new_starts = target_low_at + count
    cache_starts = new_starts + documents + 1
    return new_starts, cache_starts, cache_starts + documents + 1


def prepare_kernel(
    place_ref,
    cache_len_ref,
    new_ref,
    new_doc_ref,
    cache_doc_ref,
    own_ref,
    table_ref,
    pick_ref,
    wide,
    *,
    turns,
    period,
    count,
):
    tok = own_ref.shape[0]
    new_starts, cache_starts, lengths = table_places(count)
    own_ref[...] = split_pairs(new_ref[...], wide, tok)
    new_doc = new_doc_ref[...]
    cache_doc = cache_doc_ref[...]
    first_doc = new_doc[:, :1]
    last_doc = new_doc[:, -1:]
    low = jnp.zeros(first_doc.shape, jnp.float32)
    high = jnp.full(first_doc.shape, float(cache_doc.size), jnp.float32)
    new_at = [jnp.int32(0)]
    cache_at = [jnp.int32(0)]
    for doc in range(1, documents):
        before = jnp.sum((new_doc < doc).astype(jnp.float32))
        new_at.append(before.astype(jnp.int32))
        before = jnp.sum((cache_doc < doc).astype(jnp.float32))
        cache_at.append(before.astype(jnp.int32))
        low = jnp.where(first_doc == doc, before, low)
        high = jnp.where(last_doc == doc - 1, before, high)
    new_at.append(jnp.int32(new_doc.size))
    cache_at.append(jnp.int32(cache_doc.size))
    for doc in range(documents + 1):
        table_ref[new_starts + doc] = new_at[doc]
        table_ref[cache_starts + doc] = cache_at[doc]
    for shard in range(cache_len_ref.shape[0]):
        table_ref[lengths + shard] = cache_len_ref[shard]

    def cache_start(place):
        found = jnp.int32(0)
        for doc in range(1, documents):
            found = jnp.where(place >= new_at[doc], cache_at[doc], found)
        return found

    block = place_ref[0]
    first = block * tok
    group_first = block // count * count * tok
    new_low = jnp.int32(0)
    cache_high = cache_at[1]
    for doc in range(1, documents):
        new_low = jnp.where(first >= new_at[doc], new_at[doc], new_low)
        cache_high = jnp.where(first + tok - 1 >= new_at[doc], cache_at[doc + 1], cache_high)
    table_ref[block_at] = block
    table_ref[new_low_at] = new_low
    table_ref[cache_low_at] = cache_start(first)
    table_ref[cache_high_at] = cache_high
    for target in range(count):
        table_ref[target_low_at + target] = cache_start(group_first + target * tok)
    widest = jnp.max(high - low).astype(jnp.int32)
    pick = jnp.int32(0)
    for turn in turns[:-1]:
        pick += (widest > turn * period).astype(jnp.int32)
    pick_ref[0] = pick


def pack_kernel(
    table_ref, shards_ref, own_ref, raw_ref, out_ref, behind_ref, wide, *, rounds
):
    groups, shard_rows, _ = shards_ref.shape
    count = out_ref.shape[0]
    tok = own_ref.shape[0]
    period = count * shard_rows
    blk_index = table_ref[block_at] % count
    behind_ref[...] = split_pairs(raw_ref[...], wide, tok)
    row = lax.broadcasted_iota(jnp.int32, (shard_rows, 1), 0)
    for target in range(count):
        low = table_ref[target_low_at + target]
        reached = low - blk_index * shard_rows
        group = (reached - (shard_rows - 1) + period - 1) // period
        cut = reached - group * period
        for turn in range(rounds):
            here = jnp.minimum(group + turn, groups - 1)
            after = jnp.minimum(group + turn + 1, groups - 1)
            chosen = jnp.where(
                row >= cut,
                shards_ref[here].astype(jnp.float32),
                shards_ref[after].astype(jnp.float32),
            )
            out_ref[target, turn * shard_rows : (turn + 1) * shard_rows] = chosen.astype(
                jnp.bfloat16
            )

        @pl.when(blk_index <= target)
        def _():
            out_ref[target, rounds * shard_rows :] = own_ref[...]

        @pl.when(blk_index > target)
        def _():
            out_ref[target, rounds * shard_rows :] = behind_ref[...]


def row_bounds(table_ref, count, first, tok):
    new_starts, cache_starts, _ = table_places(count)
    row_place = first + lax.broadcasted_iota(jnp.int32, (tok, 1), 0)
    row_start = jnp.zeros((tok, 1), jnp.int32)
    row_low = jnp.zeros((tok, 1), jnp.int32)
    row_high = jnp.full((tok, 1), table_ref[cache_starts + 1], jnp.int32)
    for doc in range(1, documents):
        start = table_ref[new_starts + doc]
        reached = row_place >= start
        row_start = jnp.where(reached, start, row_start)
        row_low = jnp.where(reached, table_ref[cache_starts + doc], row_low)
        row_high = jnp.where(reached, table_ref[cache_starts + doc + 1], row_high)
    return row_place, row_start, row_low, row_high


def score(queries_ref, keys, allowed, scores_ref, at, lane_max):
    turned = keys.T
    shift = jnp.where(allowed, 0.0, negative)
    for h in range(lane_max.shape[0]):
        scores = jnp.dot(
            queries_ref[:, h * head : (h + 1) * head], turned, preferred_element_type=jnp.float32
        )
        scores = scores + shift
        scores_ref[at, h] = scores
        best = scores[:, :head]
        for part in range(1, scores.shape[1] // head):
            best = jnp.maximum(best, scores[:, part * head : (part + 1) * head])
        lane_max[h] = jnp.maximum(lane_max[h], best)


def weigh(values, scores_ref, at, lane_max, lane_sum, total):
    for h in range(lane_max.shape[0]):
        scores = scores_ref[at, h]
        best = lane_max[h]
        added = lane_sum[h]
        parts = []
        for part in range(scores.shape[1] // head):
            piece = scores[:, part * head : (part + 1) * head]
            weight = jnp.exp2((piece - best) * exponent_scale)
            added = added + weight
            parts.append(weight.astype(jnp.bfloat16))
        lane_sum[h] = added
        rounded = parts[0] if len(parts) == 1 else jnp.concatenate(parts, axis=1)
        total[h] += jnp.dot(rounded, values, preferred_element_type=jnp.float32)


def settle(lane_max):
    for h in range(lane_max.shape[0]):
        best = jnp.max(lane_max[h], axis=1, keepdims=True)
        lane_max[h] = jnp.broadcast_to(best, lane_max.shape[1:])


def attention_kernel(
    table_ref,
    queries_ref,
    arrived_ref,
    behind_ref,
    out_ref,
    new_scores,
    far_scores,
    cache_scores,
    lane_max,
    lane_sum,
    total,
    *,
    shard_rows,
    rounds,
    shards,
):
    tok = queries_ref.shape[0]
    heads = lane_max.shape[0]
    count = arrived_ref.shape[0]
    lengths = table_places(count)[2]
    period = count * shard_rows
    span = pieces * shard_rows
    new_offset = rounds * shard_rows
    block = table_ref[block_at]
    cache_low = table_ref[cache_low_at]
    cache_high = table_ref[cache_high_at]
    row_place, row_start, row_low, row_high = row_bounds(table_ref, count, block * tok, tok)
    lane_max[...] = jnp.full(lane_max.shape, negative, jnp.float32)
    lane_sum[...] = jnp.zeros(lane_sum.shape, jnp.float32)
    total[...] = jnp.zeros(total.shape, jnp.float32)
    farthest = block - count
    first_block = table_ref[new_low_at] // tok
    new_tiles = jnp.minimum((block - first_block) // blocks + 1, count // blocks)
    reaches = first_block <= farthest

    def new_part(number, first_lane):
        lanes = slice(first_lane, first_lane + head)
        return jnp.concatenate(
            [
                arrived_ref[
                    lax.rem(block - blocks * number - back + count, count), new_offset:, lanes
                ]
                for back in range(blocks - 1, -1, -1)
            ],
            axis=0,
        )

    def new_allowed(place, lanes):
        key_place = place + lax.broadcasted_iota(jnp.int32, (1, lanes), 1)
        return (key_place >= row_start) & (key_place <= row_place)

    @pl.loop(0, new_tiles)
    def _(number):
        allowed = new_allowed((block - blocks * number - blocks + 1) * tok, blocks * tok)
        score(queries_ref, new_part(number, 0), allowed, new_scores, number, lane_max)

    @pl.when(reaches)
    def _():
        allowed = new_allowed(farthest * tok, tok)
        score(queries_ref, behind_ref[:, :head], allowed, far_scores, 0, lane_max)

    def cache_tile(number):
        turn = number // (count // pieces)
        source = number % (count // pieces) * pieces
        base = cache_low + turn * period
        begin = base + jnp.bitwise_and(source * shard_rows - base, period - 1)
        holds = jnp.bitwise_and(base - source * shard_rows, period - 1) < span
        return turn, source, base, (begin < cache_high) | (holds & (base < cache_high))

    def cache_part(turn, source, first_lane):
        offset = pl.multiple_of(turn * shard_rows, shard_rows)
        return jnp.concatenate(
            [
                arrived_ref[source + part, pl.ds(offset, shard_rows), first_lane : first_lane + head]
                for part in range(pieces)
            ],
            axis=0,
        )

    tiles = rounds * count // pieces

    @pl.loop(0, tiles)
    def _(number):
        turn, source, base, needed = cache_tile(number)

        @pl.when(needed)
        def _():
            lane = lax.broadcasted_iota(jnp.int32, (1, span), 1)
            place = base + jnp.bitwise_and(source * shard_rows + lane - base, period - 1)
            shard = place // shard_rows
            filled = jnp.zeros((1, span), jnp.int32)
            for part in range(pieces):
                edge = (source + part) * shard_rows
                for at in (0, shard_rows - 1):
                    where = base + jnp.bitwise_and(edge + at - base, period - 1)
                    where = where // shard_rows
                    length = table_ref[lengths + jnp.minimum(where, shards - 1)]
                    filled = jnp.where(shard == where, length, filled)
            usable = jnp.bitwise_and(place, shard_rows - 1) < filled
            allowed = (place >= row_low) & (place < row_high) & usable
            keys = cache_part(turn, source, 0)
            score(queries_ref, keys, allowed, cache_scores, number, lane_max)

    settle(lane_max)

    @pl.loop(0, new_tiles)
    def _(number):
        weigh(new_part(number, head), new_scores, number, lane_max, lane_sum, total)

    @pl.when(reaches)
    def _():
        weigh(behind_ref[:, head:], far_scores, 0, lane_max, lane_sum, total)

    @pl.loop(0, tiles)
    def _(number):
        turn, source, base, needed = cache_tile(number)

        @pl.when(needed)
        def _():
            values = cache_part(turn, source, head)
            weigh(values, cache_scores, number, lane_max, lane_sum, total)

    for h in range(heads):
        row_total = jnp.sum(lane_sum[h], axis=1, keepdims=True)
        out_ref[:, h * head : (h + 1) * head] = (total[h] / row_total).astype(jnp.bfloat16)


def local(queries, new_kv, cached_key_value, new_doc, cache_doc, cache_len):
    tok = queries.shape[0]
    width = queries.shape[-1]
    heads = width // head
    shard_rows = cached_key_value.shape[0]
    blk_count = lax.axis_size("blk")
    cp_count = lax.axis_size("cp")
    head_count = lax.axis_size("head")
    assert tok * blk_count >= longest
    shard_count = cache_len.shape[0]
    place = lax.axis_index(("cp", "blk")).astype(jnp.int32)[None]
    period = blk_count * shard_rows
    turns = [2, 3, cp_count]
    new_raw = new_kv.reshape(2 * tok, head)
    cache_raw = cached_key_value.reshape(2 * shard_rows, head)
    spread = pl.pallas_call(
        spread_kernel,
        out_shape=jax.ShapeDtypeStruct((cp_count, shard_rows, 2 * head), jnp.bfloat16),
        in_specs=[vmem],
        out_specs=vmem,
        scratch_shapes=[pltpu.VMEM((2 * shard_rows, head), jnp.float32)],
        compiler_params=limits,
    )(cache_raw)
    shards = lax.all_to_all(spread, "cp", split_axis=0, concat_axis=0)
    raw_behind = lax.ppermute(new_raw, "cp", [(i, (i + 1) % cp_count) for i in range(cp_count)])
    own, table, pick = pl.pallas_call(
        functools.partial(prepare_kernel, turns=turns, period=period, count=blk_count),
        out_shape=[
            jax.ShapeDtypeStruct((tok, 2 * head), jnp.bfloat16),
            jax.ShapeDtypeStruct((table_places(blk_count)[2] + shard_count,), jnp.int32),
            jax.ShapeDtypeStruct((1,), jnp.int32),
        ],
        in_specs=[smem] * 2 + [vmem] * 3,
        out_specs=[vmem, smem, smem],
        scratch_shapes=[pltpu.VMEM((2 * tok, head), jnp.float32)],
        compiler_params=limits,
    )(place, cache_len, new_raw, new_doc.reshape(-1, tok), cache_doc.reshape(-1, 128))

    def exchange(rounds):
        def run(shards, own, raw_behind, table, queries):
            rows = rounds * shard_rows + tok
            packed, behind = pl.pallas_call(
                functools.partial(pack_kernel, rounds=rounds),
                out_shape=[
                    jax.ShapeDtypeStruct((blk_count, rows, 2 * head), jnp.bfloat16),
                    jax.ShapeDtypeStruct((tok, 2 * head), jnp.bfloat16),
                ],
                in_specs=[smem, vmem, vmem, vmem],
                out_specs=[vmem, vmem],
                scratch_shapes=[pltpu.VMEM((2 * tok, head), jnp.float32)],
                compiler_params=limits,
            )(table, shards, own, raw_behind)
            arrived = lax.all_to_all(packed, "blk", split_axis=0, concat_axis=0)
            span = pieces * shard_rows
            tiles = rounds * blk_count // pieces
            return pl.pallas_call(
                functools.partial(
                    attention_kernel, shard_rows=shard_rows, rounds=rounds, shards=shard_count
                ),
                out_shape=jax.ShapeDtypeStruct((tok, width), jnp.bfloat16),
                in_specs=[smem, vmem, vmem, vmem],
                out_specs=vmem,
                scratch_shapes=[
                    pltpu.VMEM((blk_count // blocks, heads, tok, blocks * tok), jnp.float32),
                    pltpu.VMEM((1, heads, tok, tok), jnp.float32),
                    pltpu.VMEM((tiles, heads, tok, span), jnp.float32),
                    pltpu.VMEM((heads, tok, head), jnp.float32),
                    pltpu.VMEM((heads, tok, head), jnp.float32),
                    pltpu.VMEM((heads, tok, head), jnp.float32),
                ],
                compiler_params=limits,
            )(table, queries, arrived, behind)

        return run

    attended = lax.switch(
        pick[0],
        [exchange(turn) for turn in turns],
        shards,
        own,
        raw_behind,
        table,
        queries[:, 0],
    )
    share = tok // head_count
    moved = lax.all_to_all(
        attended.reshape(head_count, share, width), "head", split_axis=0, concat_axis=0
    )
    return jnp.transpose(moved, (1, 0, 2))


def solution(mesh):
    placed = (
        P(("cp", "blk"), "head", None),
        P(("cp", "blk"), "head", None, None),
        P(("cp", "blk"), "head", None, None),
        P(),
        P(),
        P(),
    )
    return jax.shard_map(
        local,
        mesh=mesh,
        in_specs=placed,
        out_specs=P(("cp", "blk", "head"), None, None),
        check_vma=False,
    )
```

```python
import functools
import math

import jax
import jax.numpy as jnp
from jax import lax
from jax.experimental import pallas as pl
from jax.experimental.pallas import tpu as pltpu
from jax.sharding import PartitionSpec as P

negative = -1e30
documents = 16
block_at, new_low_at, cache_low_at, cache_high_at, target_low_at = 0, 1, 2, 3, 4
longest = 1024
head = 128
pieces = 8
blocks = 4
smem = pl.BlockSpec(memory_space=pltpu.SMEM)
vmem = pl.BlockSpec(memory_space=pltpu.VMEM)
exponent_scale = math.log2(math.e) * head**-0.5
limits = pltpu.CompilerParams(vmem_limit_bytes=44 * 1024 * 1024)


def split_pairs(raw, wide, rows):
    wide[: 2 * rows, :] = raw.astype(jnp.float32)
    keys = wide[pl.ds(0, rows, 2), :]
    values = wide[pl.ds(1, rows, 2), :]
    return jnp.concatenate([keys, values], axis=1).astype(jnp.bfloat16)


def spread_kernel(cache_ref, spread_ref, wide):
    shard = split_pairs(cache_ref[...], wide, spread_ref.shape[1])
    for target in range(spread_ref.shape[0]):
        spread_ref[target] = shard


def table_places(count):
    new_starts = target_low_at + count
    cache_starts = new_starts + documents + 1
    return new_starts, cache_starts, cache_starts + documents + 1


def prepare_kernel(
    place_ref,
    cache_len_ref,
    new_ref,
    new_doc_ref,
    cache_doc_ref,
    own_ref,
    table_ref,
    pick_ref,
    wide,
    *,
    turns,
    period,
    count,
):
    tok = own_ref.shape[0]
    new_starts, cache_starts, lengths = table_places(count)
    own_ref[...] = split_pairs(new_ref[...], wide, tok)
    new_doc = new_doc_ref[...]
    cache_doc = cache_doc_ref[...]
    first_doc = new_doc[:, :1]
    last_doc = new_doc[:, -1:]
    low = jnp.zeros(first_doc.shape, jnp.float32)
    high = jnp.full(first_doc.shape, float(cache_doc.size), jnp.float32)
    new_at = [jnp.int32(0)]
    cache_at = [jnp.int32(0)]
    for doc in range(1, documents):
        before = jnp.sum((new_doc < doc).astype(jnp.float32))
        new_at.append(before.astype(jnp.int32))
        before = jnp.sum((cache_doc < doc).astype(jnp.float32))
        cache_at.append(before.astype(jnp.int32))
        low = jnp.where(first_doc == doc, before, low)
        high = jnp.where(last_doc == doc - 1, before, high)
    new_at.append(jnp.int32(new_doc.size))
    cache_at.append(jnp.int32(cache_doc.size))
    for doc in range(documents + 1):
        table_ref[new_starts + doc] = new_at[doc]
        table_ref[cache_starts + doc] = cache_at[doc]
    for shard in range(cache_len_ref.shape[0]):
        table_ref[lengths + shard] = cache_len_ref[shard]

    def cache_start(place):
        found = jnp.int32(0)
        for doc in range(1, documents):
            found = jnp.where(place >= new_at[doc], cache_at[doc], found)
        return found

    block = place_ref[0]
    first = block * tok
    group_first = block // count * count * tok
    new_low = jnp.int32(0)
    cache_high = cache_at[1]
    for doc in range(1, documents):
        new_low = jnp.where(first >= new_at[doc], new_at[doc], new_low)
        cache_high = jnp.where(first + tok - 1 >= new_at[doc], cache_at[doc + 1], cache_high)
    table_ref[block_at] = block
    table_ref[new_low_at] = new_low
    table_ref[cache_low_at] = cache_start(first)
    table_ref[cache_high_at] = cache_high
    for target in range(count):
        table_ref[target_low_at + target] = cache_start(group_first + target * tok)
    widest = jnp.max(high - low).astype(jnp.int32)
    pick = jnp.int32(0)
    for turn in turns[:-1]:
        pick += (widest > turn * period).astype(jnp.int32)
    pick_ref[0] = pick


def pack_kernel(
    table_ref, shards_ref, own_ref, raw_ref, out_ref, behind_ref, wide, *, rounds
):
    groups, shard_rows, _ = shards_ref.shape
    count = out_ref.shape[0]
    tok = own_ref.shape[0]
    period = count * shard_rows
    blk_index = table_ref[block_at] % count
    behind_ref[...] = split_pairs(raw_ref[...], wide, tok)
    row = lax.broadcasted_iota(jnp.int32, (shard_rows, 1), 0)
    for target in range(count):
        low = table_ref[target_low_at + target]
        reached = low - blk_index * shard_rows
        group = (reached - (shard_rows - 1) + period - 1) // period
        cut = reached - group * period
        for turn in range(rounds):
            here = jnp.minimum(group + turn, groups - 1)
            after = jnp.minimum(group + turn + 1, groups - 1)
            chosen = jnp.where(
                row >= cut,
                shards_ref[here].astype(jnp.float32),
                shards_ref[after].astype(jnp.float32),
            )
            out_ref[target, turn * shard_rows : (turn + 1) * shard_rows] = chosen.astype(
                jnp.bfloat16
            )

        @pl.when(blk_index <= target)
        def _():
            out_ref[target, rounds * shard_rows :] = own_ref[...]

        @pl.when(blk_index > target)
        def _():
            out_ref[target, rounds * shard_rows :] = behind_ref[...]


def row_bounds(table_ref, count, first, tok):
    new_starts, cache_starts, _ = table_places(count)
    row_place = first + lax.broadcasted_iota(jnp.int32, (tok, 1), 0)
    row_start = jnp.zeros((tok, 1), jnp.int32)
    row_low = jnp.zeros((tok, 1), jnp.int32)
    row_high = jnp.full((tok, 1), table_ref[cache_starts + 1], jnp.int32)
    for doc in range(1, documents):
        start = table_ref[new_starts + doc]
        reached = row_place >= start
        row_start = jnp.where(reached, start, row_start)
        row_low = jnp.where(reached, table_ref[cache_starts + doc], row_low)
        row_high = jnp.where(reached, table_ref[cache_starts + doc + 1], row_high)
    return row_place, row_start, row_low, row_high


def score(rows_ref, keys, allowed, scores_ref, at, lane_max):
    tok = allowed.shape[0]
    products = lax.dot_general(
        rows_ref[...], keys, (((1,), (1,)), ((), ())), preferred_element_type=jnp.float32
    )
    for first in range(0, rows_ref.shape[0], tok):
        rows = slice(first, first + tok)
        scores = jnp.where(allowed, products[rows], negative)
        scores_ref[at, rows] = scores
        best = lane_max[rows]
        for lane in range(0, scores.shape[1], head):
            best = jnp.maximum(best, scores[:, lane : lane + head])
        lane_max[rows] = best


def weigh(values, scores_ref, at, lane_max, lane_sum, total, tok):
    rounded = []
    for first in range(0, total.shape[0], tok):
        rows = slice(first, first + tok)
        scores = scores_ref[at, rows]
        best = lane_max[rows]
        added = lane_sum[rows]
        parts = []
        for lane in range(0, scores.shape[1], head):
            weight = jnp.exp2((scores[:, lane : lane + head] - best) * exponent_scale)
            added = added + weight
            parts.append(weight.astype(jnp.bfloat16))
        lane_sum[rows] = added
        rounded.append(parts[0] if len(parts) == 1 else jnp.concatenate(parts, axis=1))
    total[...] += jnp.dot(
        jnp.concatenate(rounded, axis=0), values, preferred_element_type=jnp.float32
    )


def settle(lane_max):
    best = jnp.max(lane_max[...], axis=1, keepdims=True)
    lane_max[...] = jnp.broadcast_to(best, lane_max.shape)


def attention_kernel(
    table_ref,
    queries_ref,
    arrived_ref,
    behind_ref,
    out_ref,
    query_rows,
    new_scores,
    far_scores,
    cache_scores,
    lane_max,
    lane_sum,
    total,
    *,
    shard_rows,
    rounds,
    shards,
):
    tok = queries_ref.shape[0]
    heads = query_rows.shape[0] // tok
    count = arrived_ref.shape[0]
    lengths = table_places(count)[2]
    period = count * shard_rows
    span = pieces * shard_rows
    new_offset = rounds * shard_rows
    block = table_ref[block_at]
    cache_low = table_ref[cache_low_at]
    cache_high = table_ref[cache_high_at]
    row_place, row_start, row_low, row_high = row_bounds(table_ref, count, block * tok, tok)
    for h in range(heads):
        query_rows[h * tok : (h + 1) * tok] = queries_ref[:, h * head : (h + 1) * head]
    lane_max[...] = jnp.full(lane_max.shape, negative, jnp.float32)
    lane_sum[...] = jnp.zeros(lane_sum.shape, jnp.float32)
    total[...] = jnp.zeros(total.shape, jnp.float32)
    farthest = block - count
    first_block = table_ref[new_low_at] // tok
    new_tiles = jnp.minimum((block - first_block) // blocks + 1, count // blocks)
    reaches = first_block <= farthest

    def new_part(number, first_lane):
        lanes = slice(first_lane, first_lane + head)
        return jnp.concatenate(
            [
                arrived_ref[
                    lax.rem(block - blocks * number - back + count, count), new_offset:, lanes
                ]
                for back in range(blocks - 1, -1, -1)
            ],
            axis=0,
        )

    def new_allowed(place, lanes):
        key_place = place + lax.broadcasted_iota(jnp.int32, (1, lanes), 1)
        return (key_place >= row_start) & (key_place <= row_place)

    @pl.loop(0, new_tiles)
    def _(number):
        allowed = new_allowed((block - blocks * number - blocks + 1) * tok, blocks * tok)
        score(query_rows, new_part(number, 0), allowed, new_scores, number, lane_max)

    @pl.when(reaches)
    def _():
        allowed = new_allowed(farthest * tok, tok)
        score(query_rows, behind_ref[:, :head], allowed, far_scores, 0, lane_max)

    def cache_tile(number):
        turn = number // (count // pieces)
        source = number % (count // pieces) * pieces
        base = cache_low + turn * period
        begin = base + jnp.bitwise_and(source * shard_rows - base, period - 1)
        holds = jnp.bitwise_and(base - source * shard_rows, period - 1) < span
        return turn, source, base, (begin < cache_high) | (holds & (base < cache_high))

    def cache_part(turn, source, first_lane):
        offset = pl.multiple_of(turn * shard_rows, shard_rows)
        return jnp.concatenate(
            [
                arrived_ref[source + part, pl.ds(offset, shard_rows), first_lane : first_lane + head]
                for part in range(pieces)
            ],
            axis=0,
        )

    tiles = rounds * count // pieces

    @pl.loop(0, tiles)
    def _(number):
        turn, source, base, needed = cache_tile(number)

        @pl.when(needed)
        def _():
            lane = lax.broadcasted_iota(jnp.int32, (1, span), 1)
            place = base + jnp.bitwise_and(source * shard_rows + lane - base, period - 1)
            shard = place // shard_rows
            filled = jnp.zeros((1, span), jnp.int32)
            for part in range(pieces):
                edge = (source + part) * shard_rows
                for at in (0, shard_rows - 1):
                    where = base + jnp.bitwise_and(edge + at - base, period - 1)
                    where = where // shard_rows
                    length = table_ref[lengths + jnp.minimum(where, shards - 1)]
                    filled = jnp.where(shard == where, length, filled)
            usable = jnp.bitwise_and(place, shard_rows - 1) < filled
            allowed = (place >= row_low) & (place < row_high) & usable
            keys = cache_part(turn, source, 0)
            score(query_rows, keys, allowed, cache_scores, number, lane_max)

    settle(lane_max)

    @pl.loop(0, new_tiles)
    def _(number):
        weigh(new_part(number, head), new_scores, number, lane_max, lane_sum, total, tok)

    @pl.when(reaches)
    def _():
        weigh(behind_ref[:, head:], far_scores, 0, lane_max, lane_sum, total, tok)

    @pl.loop(0, tiles)
    def _(number):
        turn, source, base, needed = cache_tile(number)

        @pl.when(needed)
        def _():
            values = cache_part(turn, source, head)
            weigh(values, cache_scores, number, lane_max, lane_sum, total, tok)

    for h in range(heads):
        rows = slice(h * tok, (h + 1) * tok)
        row_total = jnp.sum(lane_sum[rows], axis=1, keepdims=True)
        out_ref[:, h * head : (h + 1) * head] = (total[rows] / row_total).astype(jnp.bfloat16)


def local(queries, new_kv, cached_key_value, new_doc, cache_doc, cache_len):
    tok = queries.shape[0]
    width = queries.shape[-1]
    heads = width // head
    shard_rows = cached_key_value.shape[0]
    blk_count = lax.axis_size("blk")
    cp_count = lax.axis_size("cp")
    head_count = lax.axis_size("head")
    assert tok * blk_count >= longest
    shard_count = cache_len.shape[0]
    place = lax.axis_index(("cp", "blk")).astype(jnp.int32)[None]
    period = blk_count * shard_rows
    turns = [2, 3, cp_count]
    new_raw = new_kv.reshape(2 * tok, head)
    cache_raw = cached_key_value.reshape(2 * shard_rows, head)
    spread = pl.pallas_call(
        spread_kernel,
        out_shape=jax.ShapeDtypeStruct((cp_count, shard_rows, 2 * head), jnp.bfloat16),
        in_specs=[vmem],
        out_specs=vmem,
        scratch_shapes=[pltpu.VMEM((2 * shard_rows, head), jnp.float32)],
        compiler_params=limits,
    )(cache_raw)
    shards = lax.all_to_all(spread, "cp", split_axis=0, concat_axis=0)
    raw_behind = lax.ppermute(new_raw, "cp", [(i, (i + 1) % cp_count) for i in range(cp_count)])
    own, table, pick = pl.pallas_call(
        functools.partial(prepare_kernel, turns=turns, period=period, count=blk_count),
        out_shape=[
            jax.ShapeDtypeStruct((tok, 2 * head), jnp.bfloat16),
            jax.ShapeDtypeStruct((table_places(blk_count)[2] + shard_count,), jnp.int32),
            jax.ShapeDtypeStruct((1,), jnp.int32),
        ],
        in_specs=[smem] * 2 + [vmem] * 3,
        out_specs=[vmem, smem, smem],
        scratch_shapes=[pltpu.VMEM((2 * tok, head), jnp.float32)],
        compiler_params=limits,
    )(place, cache_len, new_raw, new_doc.reshape(-1, tok), cache_doc.reshape(-1, 128))

    def exchange(rounds):
        def run(shards, own, raw_behind, table, queries):
            rows = rounds * shard_rows + tok
            packed, behind = pl.pallas_call(
                functools.partial(pack_kernel, rounds=rounds),
                out_shape=[
                    jax.ShapeDtypeStruct((blk_count, rows, 2 * head), jnp.bfloat16),
                    jax.ShapeDtypeStruct((tok, 2 * head), jnp.bfloat16),
                ],
                in_specs=[smem, vmem, vmem, vmem],
                out_specs=[vmem, vmem],
                scratch_shapes=[pltpu.VMEM((2 * tok, head), jnp.float32)],
                compiler_params=limits,
            )(table, shards, own, raw_behind)
            arrived = lax.all_to_all(packed, "blk", split_axis=0, concat_axis=0)
            span = pieces * shard_rows
            tiles = rounds * blk_count // pieces
            return pl.pallas_call(
                functools.partial(
                    attention_kernel, shard_rows=shard_rows, rounds=rounds, shards=shard_count
                ),
                out_shape=jax.ShapeDtypeStruct((tok, width), jnp.bfloat16),
                in_specs=[smem, vmem, vmem, vmem],
                out_specs=vmem,
                scratch_shapes=[
                    pltpu.VMEM((heads * tok, head), jnp.bfloat16),
                    pltpu.VMEM((blk_count // blocks, heads * tok, blocks * tok), jnp.float32),
                    pltpu.VMEM((1, heads * tok, tok), jnp.float32),
                    pltpu.VMEM((tiles, heads * tok, span), jnp.float32),
                    pltpu.VMEM((heads * tok, head), jnp.float32),
                    pltpu.VMEM((heads * tok, head), jnp.float32),
                    pltpu.VMEM((heads * tok, head), jnp.float32),
                ],
                compiler_params=limits,
            )(table, queries, arrived, behind)

        return run

    attended = lax.switch(
        pick[0],
        [exchange(turn) for turn in turns],
        shards,
        own,
        raw_behind,
        table,
        queries[:, 0],
    )
    share = tok // head_count
    moved = lax.all_to_all(
        attended.reshape(head_count, share, width), "head", split_axis=0, concat_axis=0
    )
    return jnp.transpose(moved, (1, 0, 2))


def solution(mesh):
    placed = (
        P(("cp", "blk"), "head", None),
        P(("cp", "blk"), "head", None, None),
        P(("cp", "blk"), "head", None, None),
        P(),
        P(),
        P(),
    )
    return jax.shard_map(
        local,
        mesh=mesh,
        in_specs=placed,
        out_specs=P(("cp", "blk", "head"), None, None),
        check_vma=False,
    )
```
